32 devices in a mesh: region: 4 (over z), tile: 8 (over y, x, core).
Axes of the slice: x: 2, y: 2, z: 4, core: 2. Of those that a mesh axis runs over, the one named last changes fastest.
Arguments:
- offsets: float32 [2, 131072], P(None, ('region', 'tile')), may hold values from 0 to 1
- design: float32 [2, 131072], P(None, ('region', 'tile')), may hold values from -4 to 4
- target: float32 [131072], P(('region', 'tile')), may hold values from -6 to 6
- beta_second: float32 [131072], P(('region', 'tile')), may hold values from -3 to 3
- counts: int32 [512], P(('region', 'tile')), may hold values from 1 to 256, as said below
- kernel_width: int32 [2, 512], P(None, ('region', 'tile')), may hold values from 2 to 8
- reach: int32 [2, 512, 9], P(None, ('region', 'tile')), may hold values 0 or 1
- assignment: int32 [4, 128], P('region', 'tile'), may hold values from 0 to 127, each once within a row
Outputs:
- betas: float32 [2, 131072], P(None, ('region', 'tile'))
- hats: float32 [2, 131072], P(None, ('region', 'tile'))
- residual: float32 [131072], P(('region', 'tile'))
The draws below stay inside these ranges and needn't reach their ends.
Inputs may be any that keep to these rules, and one draw needn't show every extreme that they name: `counts`: some tile holds 256 live records in every draw.
All inputs are finite; a program needn't handle non-finite values. No bound on the sum of `reach` on one device may be relied on, other than what follows from the above.
Results may differ from the reference program's by a relative error of at most 0.0003.
Values sent between devices are 32-bit elements; how exact they have to be, the bound alone decides.
No kernel may reach another device: no remote copies, remote signals or barrier semaphores. Data moves between devices by JAX's collectives and lax.ppermute only.
A program may use at most 64 MiB of HBM per device.

```python
import jax
import jax.numpy as jnp
from jax import lax

TILE = 256
TX = 4
NREG = 4
TPR = 128
TY = 32
NTILES = 512
RECORDS = 131072


def draw_counts(key, part):
    subkeys = jax.random.split(key, 3)
    upper_draw = jax.random.randint(subkeys[0], (NTILES,), 0, TILE)
    lower_draw = jax.random.randint(subkeys[1], (NTILES,), 0, TILE)
    filled = 1 + upper_draw * lower_draw // TILE
    chosen = jax.random.randint(subkeys[2], (), 0, NTILES)
    return filled.at[chosen].set(TILE).astype(jnp.int32)


def place_ends(drawn, stream_key, least, largest):
    place = [jax.random.randint(jax.random.fold_in(stream_key, axis), (), 0, length) for axis, length in enumerate(drawn.shape)]
    longest = drawn.shape.index(max(drawn.shape))
    beside = place[:longest] + [(place[longest] + 1) % drawn.shape[longest]] + place[longest + 1:]
    return drawn.at[tuple(place)].set(least).at[tuple(beside)].set(largest)


def level_of(rng, dims, pieces, smallest, top_value):
    gain = 1.0
    for axis_at, shards_of in pieces:
        steps = jax.random.uniform(jax.random.fold_in(jax.random.fold_in(rng, 6), axis_at), (shards_of,), jnp.float32, smallest / len(pieces), top_value / len(pieces))
        gain = gain * jnp.repeat(jnp.exp(steps), dims[axis_at] // shards_of).reshape((-1,) + (1,) * (len(dims) - 1 - axis_at))
    return gain


def gaussian(rng, extent, deviation, bound, pieces=(), held_as=jnp.bfloat16):
    values = deviation * jax.random.normal(rng, extent, jnp.float32)
    if pieces:
        values = values * level_of(rng, extent, pieces, -0.22, 0.18)
    return jnp.clip(values, -bound, bound).astype(held_as)


def setup_inputs(seed: int = 0) -> dict:
    arg_keys = jax.random.split(jax.random.key(seed), 9)
    return {
        "offsets": jnp.clip(1.0 * jax.random.uniform(arg_keys[0], (2, RECORDS), jnp.float32) ** level_of(arg_keys[0], (2, RECORDS), ((1, 32),), -0.2, 0.2), 0.0, 1.0),
        "design": gaussian(arg_keys[1], (2, RECORDS), 1.0, 4.0, ((1, 32),), jnp.float32),
        "target": gaussian(arg_keys[2], (RECORDS,), 1.0, 6.0, ((0, 32),), jnp.float32),
        "beta_second": gaussian(arg_keys[3], (RECORDS,), 0.5, 3.0, ((0, 32),), jnp.float32),
        "counts": draw_counts(jax.random.fold_in(arg_keys[8], 71), 0),
        "kernel_width": place_ends(jax.random.randint(arg_keys[5], (2, NTILES), 2, 9), jax.random.fold_in(arg_keys[5], 1), 2, 8).astype(jnp.int32),
        "reach": place_ends((jax.random.randint(arg_keys[6], (2, NTILES, 9), 0, 4) < 3).astype(jnp.int32), jax.random.fold_in(arg_keys[6], 1), 0, 1),
        "assignment": jax.vmap(lambda own: jax.random.permutation(own, TPR))(jax.random.split(arg_keys[7], NREG)).reshape((NREG, TPR)).astype(jnp.int32),
    }


def pick_rows(values, order):
    return values[order]


def extend(grid):
    blank = jnp.zeros_like(grid[:1, :1])
    lower = jnp.concatenate([blank, grid[:-1, TX - 1:]], axis=0)
    upper = jnp.concatenate([grid[1:, :1], blank], axis=0)
    wider = jnp.concatenate([lower, grid, upper], axis=1)
    return jnp.pad(wider, ((0, 0), (0, 0), (1, 1), (0, 0)))


def reference(offsets, design, target, beta_second, counts, kernel_width, reach, assignment):
    layout_shape = (NREG, TPR, TILE)
    column = assignment // TY
    across = assignment % TY
    region_ids = jnp.arange(NREG, dtype=jnp.int32)[:, None]
    places = offsets.reshape(2, NREG, TPR, TILE)
    east = (region_ids * TX + column).astype(jnp.float32)[:, :, None] + places[0]
    north = across.astype(jnp.float32)[:, :, None] + places[1]
    present = (jnp.arange(TILE, dtype=jnp.int32)[None, None, :] < counts.reshape(NREG, TPR)[:, :, None]).astype(jnp.float32)
    cov_one = design[0].reshape(layout_shape)
    cov_two = design[1].reshape(layout_shape)
    observed = target.reshape(layout_shape)
    prior_beta = beta_second.reshape(layout_shape)
    inverse = jnp.argsort(assignment, axis=1).astype(jnp.int32)
    flat_cells = assignment.reshape(-1)

    def layout(values):
        return extend(jax.vmap(pick_rows)(values, inverse).reshape(NREG, TX, TY, TILE))

    base = [layout(east), layout(north), layout(present)]

    def smooth_all(covariate, partial_value, widths, near_mask):
        table = jnp.stack(base + [layout(covariate), layout(partial_value)])
        anchor = jnp.int32(0)

        def per_tile(item):
            number, own_east, own_north, own_cov, own_live, width, mask_row = item
            region_of = number // TPR
            cell = flat_cells[number]
            block = lax.dynamic_slice(table, (anchor, region_of, cell // TY, cell % TY, anchor), (5, 1, 3, 3, TILE)).reshape(5, 9 * TILE)
            centre = jnp.arange(9) == 4
            valid = ((mask_row > 0) | centre).astype(jnp.float32)
            weight_mask = block[2] * jnp.repeat(valid, TILE)
            squared = (own_east[:, None] - block[0][None, :]) ** 2 + (own_north[:, None] - block[1][None, :]) ** 2
            inverse_width = 32.0 / (width.astype(jnp.float32) ** 2)
            kernel = jnp.exp(-squared * inverse_width) * weight_mask[None, :]
            totals = 1.0 + jnp.dot(kernel, block[3] * block[3], precision=lax.Precision.HIGHEST)
            weighted = jnp.dot(kernel, block[3] * block[4], precision=lax.Precision.HIGHEST)
            return own_live * weighted / totals, own_live * own_cov * own_cov / totals

        items = (jnp.arange(NTILES, dtype=jnp.int32), east.reshape(NTILES, TILE), north.reshape(NTILES, TILE),
                 covariate.reshape(NTILES, TILE), present.reshape(NTILES, TILE), widths, near_mask)
        return lax.map(per_tile, items)

    beta_one, hat_one = smooth_all(cov_one, observed - cov_two * prior_beta, kernel_width[0], reach[0])
    beta_one_grid = beta_one.reshape(layout_shape)
    beta_two, hat_two = smooth_all(cov_two, observed - cov_one * beta_one_grid, kernel_width[1], reach[1])
    residual = present * (observed - cov_one * beta_one_grid - cov_two * beta_two.reshape(layout_shape))
    betas = jnp.stack([beta_one.reshape(-1), beta_two.reshape(-1)])
    hats = jnp.stack([hat_one.reshape(-1), hat_two.reshape(-1)])
    return betas, hats, residual.reshape(-1)
```

```python
import functools

import jax
import jax.numpy as jnp
from jax import lax
from jax.experimental import pallas as pl
from jax.experimental.pallas import tpu as pltpu
from jax.sharding import PartitionSpec as P

TILE = 256
TX = 4
LANES = 128
TWO, EAST, NORTH, ONE, PART, PRICE, INFO = range(7)
SLOTS = 16
LABEL, COUNT, WIDTH, REACH = 0, 1, 2, 3
NEAR = [(a, b) for a in (-1, 0, 1) for b in (-1, 0, 1)]
F32, I32 = jnp.float32, jnp.int32
ANY = pl.BlockSpec(memory_space=pl.ANY)
SMEM = pl.BlockSpec(memory_space=pltpu.SMEM)
VMEM = pl.BlockSpec(memory_space=pltpu.VMEM)


def prepare_kernel(off, des, tgt, sec, counts, widths, reach, cells, out, mine):
    lane = lax.broadcasted_iota(I32, (1, LANES), 1)
    packed = []
    for t in range(counts.shape[0]):
        row = jnp.zeros((1, LANES), F32)
        facts = [cells[0, t], counts[t], widths[0, t]] + [reach[e, 0, t] for e in range(9)]
        for k, fact in enumerate(facts):
            row = jnp.where(lane == k, fact.astype(F32), row)
        out[INFO, 0, t : t + 1, :] = row
        facts[WIDTH:] = [widths[1, t]] + [reach[e, 1, t] for e in range(9)]
        for k, fact in enumerate(facts + [jnp.int32(0)] * 4):
            mine[t * SLOTS + k] = fact
        packed.append(row)
        for h in range(2):
            at = slice(t * TILE + h * LANES, t * TILE + (h + 1) * LANES)
            live = lane + h * LANES < counts[t]
            one = jnp.where(live, des[0:1, at], 0.0)
            two = jnp.where(live, des[1:2, at], 0.0)
            price = tgt[0:1, at]
            out[EAST, h, t : t + 1, :] = off[0:1, at] - 0.5
            out[NORTH, h, t : t + 1, :] = off[1:2, at] - 0.5
            out[ONE, h, t : t + 1, :] = one
            out[PART, h, t : t + 1, :] = one * (price - two * sec[0:1, at])
            out[TWO, h, t : t + 1, :] = two
            out[PRICE, h, t : t + 1, :] = price
    for t in range(8):
        out[INFO, 1, t : t + 1, :] = packed[t] + pltpu.roll(packed[t + 8], LANES // 2, 1)
    out[INFO, 1, 8:16, :] = jnp.zeros((8, LANES), F32)


def fact(facts, number, k):
    slot = number % SLOTS
    return facts[number // SLOTS, slot % 8, (slot // 8) * (LANES // 2) + k]


def fetch(same, other, table, fields, sem):
    half = same.shape[0]
    return [
        pltpu.make_async_copy(
            held.at[:, pl.ds(0, fields)], table.at[pl.ds(side * half, half)], sem
        )
        for side, held in enumerate((same, other))
    ]


def fetch_facts(same, other, facts, sem):
    half = same.shape[0]
    return [
        pltpu.make_async_copy(held.at[:, INFO, 1, pl.ds(0, 8)], facts.at[pl.ds(side * half, half)], sem)
        for side, held in enumerate((same, other))
    ]


def invert(facts, inverse, number, cells):
    def step(s, carry):
        cell = fact(facts, s, LABEL).astype(I32)
        inverse[cell] = s
        number[cell] = fact(facts, s, COUNT).astype(I32)
        return carry

    lax.fori_loop(0, cells, step, 0, unroll=8)


def border_kernel(same, other, out, inverse, number, table, facts, sem, fact_sem):
    copies = fetch(same, other, table, 7, sem)
    fact_copies = fetch_facts(same, other, facts, fact_sem)
    for copy in fact_copies + copies:
        copy.start()
    for copy in fact_copies:
        copy.wait()
    cells = inverse.shape[0]
    rows = cells // TX
    per_pair = 8
    invert(facts, inverse, number, cells)
    for copy in copies:
        copy.wait()
    me = lax.axis_index("tile")
    odd = me % 2
    first = (me // 2) * per_pair
    order = [(0, r) for r in range(1, 9)] + [(1, r) for r in range(1, 9)]
    order += [(0, 0), (0, 9), (1, 0), (1, 9)]
    for i, (away, r) in enumerate(order):
        column = jnp.where(odd == 1, away, TX - 1 - away)
        row = jnp.clip(first + r - 1, 0, rows - 1)
        source = inverse[column * rows + row]
        source = (source // SLOTS, source % SLOTS)
        for f, field in enumerate((EAST, NORTH, ONE, PART, INFO)):
            out[:, f * 24 + i : f * 24 + i + 1, :] = row_of(table, field, source)
        if i < 8:
            for f, field in enumerate((TWO, PRICE)):
                out[:, 120 + 8 * f + i : 121 + 8 * f + i, :] = row_of(table, field, source)
    for f in range(5):
        out[:, f * 24 + 20 : f * 24 + 24, :] = jnp.zeros((2, 4, LANES), F32)


def row_of(table, field, source):
    return table[source[0], field, :, pl.ds(source[1], 1), :]


def records(tiles):
    shape = (2, tiles, LANES)
    number = lax.broadcasted_iota(I32, shape, 2) + LANES * lax.broadcasted_iota(I32, shape, 0)
    return number.astype(F32)


def columns_of(rows):
    pad = jnp.zeros((64 - rows.shape[1], LANES), F32)
    return jnp.concatenate([rows[0], pad, rows[1], pad], axis=0).T


def rows_of(columns, tiles):
    flat = columns.T
    return jnp.stack([flat[:tiles], flat[64 : 64 + tiles]])


def sweep_tile(t, number, pairs, scale, east, north, table, part, cov, lists, sums):
    which, start, step_e, step_n = lists
    den_ref, num_ref = sums
    lane = lax.broadcasted_iota(I32, (64, LANES), 1)

    def block(nb, carry):
        at = pl.ds(pl.multiple_of((nb % 2) * 64, 64), 64)
        mine = lane == (nb // 2) * 64 + t
        x = jnp.sum(jnp.where(mine, east[at, :], 0.0), axis=1, keepdims=True)
        y = jnp.sum(jnp.where(mine, north[at, :], 0.0), axis=1, keepdims=True)
        x = jnp.broadcast_to(x, (64, LANES))
        y = jnp.broadcast_to(y, (64, LANES))

        def pair(p, sums_now):
            den, num = sums_now
            for k in range(2):
                i = 2 * p + k
                n = which[i] // SLOTS
                at_row = pl.ds(which[i] % SLOTS, 1)
                h = start[i]
                u = table[n, EAST, h, at_row, :] + step_e[i]
                v = table[n, NORTH, h, at_row, :] + step_n[i]
                c = table[n, cov, h, at_row, :]
                d = part(i, n, h, at_row)
                q = scale * (u * u + v * v)
                w = jnp.exp(x * u + y * v - q)
                den = den + w * (c * c)
                num = num + w * d
            return den, num

        zero = jnp.zeros((64, LANES), F32)
        den, num = lax.fori_loop(0, pairs, pair, (zero, zero))
        den = jnp.sum(den, axis=1, keepdims=True)
        num = jnp.sum(num, axis=1, keepdims=True)
        den_ref[at, :] = jnp.where(mine, den, den_ref[at, :])
        num_ref[at, :] = jnp.where(mine, num, num_ref[at, :])
        return carry

    lax.fori_loop(0, (number + 63) // 64, block, 0)


def first_kernel(
    inverse, number, same, other, border, out,
    table, own, scales, numbers, east, north, dens, nums,
    facts, border_facts, window, live, which, start, step_e, step_n, sem, fact_sem,
):
    copies = fetch(same, other, table, 6, sem)
    fact_copies = fetch_facts(same, other, facts, fact_sem)
    cells = inverse.shape[0]
    rows = cells // TX
    blocks = cells // SLOTS
    empty = cells + 20
    for f, field in enumerate((EAST, NORTH, ONE, PART, INFO)):
        for k, size in enumerate((16, 8)):
            held = pl.ds(f * 24 + 16 * k, size)
            if field == INFO:
                to = border_facts.at[pl.ds(16 * k, size)]
                fact_copies.append(pltpu.make_async_copy(border.at[0, held], to, fact_sem))
            else:
                to = table.at[blocks + k, field, :, pl.ds(0, size)]
                copies.append(pltpu.make_async_copy(border.at[:, held], to, sem))
    for f, field in enumerate((TWO, PRICE)):
        to = table.at[blocks, field, :, pl.ds(0, 8)]
        copies.append(pltpu.make_async_copy(border.at[:, pl.ds(120 + 8 * f, 8)], to, sem))
    for copy in fact_copies + copies:
        copy.start()
    for copy in fact_copies:
        copy.wait()
    me = lax.axis_index("tile")
    odd = me % 2
    first = (me // 2) * 8
    toward = 1 - 2 * odd
    order = [(0, r) for r in range(1, 9)] + [(1, r) for r in range(1, 9)]
    order += [(0, 0), (0, 9), (1, 0), (1, 9)]
    for u in range(5):
        for r in range(10):
            row = first + r - 1
            if u < 2:
                i = order.index((1 - u, r))
                source = cells + i
                held = border_facts[i, COUNT].astype(I32)
            else:
                column = jnp.where(odd == 1, 5 - u, u - 2)
                cell = column * rows + jnp.clip(row, 0, rows - 1)
                source = inverse[cell]
                held = number[cell]
            if r in (0, 9):
                held = jnp.where((row >= 0) & (row < rows), held, 0)
            window[u * 10 + r] = source
            live[u * 10 + r] = held
    for copy in copies:
        copy.wait()
    tiles = 24

    def target_fact(t, target, k):
        inner = fact(facts, jnp.minimum(target, cells - 1), k)
        return jnp.where(t < 8, border_facts[jnp.minimum(t, 7), k], inner)

    def gather(t, carry):
        place = (t // 8 + 1) * 10 + t % 8 + 1
        target = window[place]
        at = (target // SLOTS, target % SLOTS)
        width = jnp.full((1, LANES), target_fact(t, target, WIDTH), F32)
        scales[pl.ds(t, 1), :] = 32.0 / (width * width)
        numbers[pl.ds(t, 1), :] = jnp.full((1, LANES), live[place].astype(F32), F32)
        for field in range(6):
            own[field, :, pl.ds(t, 1), :] = row_of(table, field, at)
        return carry

    lax.fori_loop(0, tiles, gather, 0, unroll=2)
    present = records(tiles) < numbers[...][None]
    scale_rows = scales[...][None]
    x, y = own[EAST], own[NORTH]
    east[...] = columns_of(2.0 * scale_rows * x)
    north[...] = columns_of(2.0 * scale_rows * y)
    dens[...] = jnp.zeros_like(dens)
    nums[...] = jnp.zeros_like(nums)

    def each(t, carry):
        u = t // 8 + 1
        r = t % 8 + 1
        target = window[u * 10 + r]
        number = live[u * 10 + r]
        used = jnp.int32(0)
        for e, (a, b) in enumerate(NEAR):
            place = (u + toward * a) * 10 + r + b
            source = window[place]
            held = live[place]
            taken = held > 0
            if e != 4:
                taken = taken & (target_fact(t, target, REACH + e) > 0.5)
            for h in range(2):
                which[used] = source
                start[used] = jnp.int32(h)
                step_e[used] = jnp.float32(a)
                step_n[used] = jnp.float32(b)
                more = taken if h == 0 else taken & (held > LANES)
                used = used + more.astype(I32)
        which[used] = jnp.int32(empty)
        start[used] = jnp.int32(0)
        step_e[used] = jnp.float32(0)
        step_n[used] = jnp.float32(0)
        sweep_tile(
            t, number, (used + 1) // 2, scales[pl.ds(t, 1), :], east, north, table,
            lambda i, n, h, at_row: table[n, PART, h, at_row, :],
            ONE, (which, start, step_e, step_n), (dens, nums),
        )
        return carry

    lax.fori_loop(0, tiles, each, 0)
    shrink = jnp.exp(-scale_rows * (x * x + y * y))
    inv = 1.0 / (1.0 + shrink * rows_of(dens[...], tiles))
    beta = jnp.where(present, shrink * rows_of(nums[...], tiles) * inv, 0.0)
    one, two = own[ONE], own[TWO]
    out[:, 0:24, :] = two * (own[PRICE] - one * beta)
    out[:, 24:40, :] = beta[:, 8:24]
    out[:, 40:56, :] = (one * one * inv)[:, 8:24]
    out[:, 56:64, :] = two[:, 0:8]
    out[:, 64:72, :] = x[:, 0:8]
    out[:, 72:80, :] = y[:, 0:8]
    out[:, 80:88, :] = jnp.broadcast_to(numbers[0:8, :][None], (2, 8, LANES))


def second_kernel(
    inverse, number, own_block, same, other, same_b, other_b, mine,
    betas, hats, residual,
    table, results, own, scales, numbers, east, north, dens, nums,
    border_facts, which, start, step_e, step_n, held_by, held_at, sem, fact_sem,
):
    copies = fetch(same, other, table, 3, sem)
    fact_copies = []
    half, _, _, tiles, _ = same.shape
    cells = inverse.shape[0]
    rows = cells // TX
    blocks = cells // SLOTS
    empty = cells + 2 * half * 8
    for side, held in enumerate((same_b, other_b)):
        at = pl.ds(side * half, half)
        copies.append(pltpu.make_async_copy(held, results.at[at, :, pl.ds(0, 88)], sem))
        fact_copies.append(
            pltpu.make_async_copy(held.at[:, 0, pl.ds(80, 8)], border_facts.at[at], fact_sem)
        )
    for copy in fact_copies + copies:
        copy.start()
    for t in range(tiles):
        width = jnp.full((1, LANES), mine[t * SLOTS + WIDTH].astype(F32), F32)
        scales[t : t + 1, :] = 32.0 / (width * width)
        numbers[t : t + 1, :] = jnp.full((1, LANES), mine[t * SLOTS + COUNT].astype(F32), F32)
    present = records(tiles) < numbers[...][None]
    scale_rows = scales[...][None]
    x, y = own_block[EAST], own_block[NORTH]
    east[...] = columns_of(2.0 * scale_rows * x)
    north[...] = columns_of(2.0 * scale_rows * y)
    dens[...] = jnp.zeros_like(dens)
    nums[...] = jnp.zeros_like(nums)
    for copy in fact_copies:
        copy.wait()
    me = lax.axis_index("tile")
    for copy in copies:
        copy.wait()

    def lay(n, carry):
        at = pl.ds(pl.multiple_of((n % 2) * 8, 8), 8)
        for field in range(3):
            held = results[n, :, 56 + 8 * field : 64 + 8 * field, :]
            table[blocks + n // 2, field, :, at, :] = held
        return carry

    lax.fori_loop(0, 2 * half, lay, 0)
    for field in range(3):
        table[blocks + half, field, :, 0:8, :] = jnp.zeros((2, 8, LANES), F32)
    results[0, :, 88:96, :] = jnp.zeros((2, 8, LANES), F32)

    def place(column, row):
        low = (column < TX // 2).astype(I32)
        device = (row // 8) * 2 + 1 - low
        k = device ^ me
        n = (k % 2) * half + k // 2
        depth = jnp.where(low == 1, column + 1, TX - column)
        return n, depth, row % 8

    def each(t, carry):
        cell = mine[t * SLOTS + LABEL]
        column, across = cell // rows, cell % rows
        used = jnp.int32(0)
        for e, (a, b) in enumerate(NEAR):
            col, row = column + a, across + b
            inside = (row >= 0) & (row < rows)
            row = jnp.clip(row, 0, rows - 1)
            n, depth, r = place(col, row)
            in_strip = (col >= 0) & (col < TX)
            near = jnp.clip(col, 0, TX - 1) * rows + row
            source = jnp.where(in_strip, inverse[near], cells + n * 8 + r)
            live = jnp.where(in_strip, number[near], border_facts[n, r, 0].astype(I32))
            taken = inside & (live > 0)
            if e != 4:
                taken = taken & (mine[t * SLOTS + REACH + e] > 0)
            for h in range(2):
                which[used] = source
                held_by[used] = n
                held_at[used] = depth * 8 + r
                start[used] = jnp.int32(h)
                step_e[used] = jnp.float32(a)
                step_n[used] = jnp.float32(b)
                more = taken if h == 0 else taken & (live > LANES)
                used = used + more.astype(I32)
        which[used] = jnp.int32(empty)
        start[used] = jnp.int32(0)
        step_e[used] = jnp.float32(0)
        step_n[used] = jnp.float32(0)
        held_by[used] = jnp.int32(0)
        held_at[used] = jnp.int32(88)
        n, depth, r = place(column, across)
        own[0, :, pl.ds(t, 1), :] = results[n, :, pl.ds(16 + depth * 8 + r, 1), :]
        own[1, :, pl.ds(t, 1), :] = results[n, :, pl.ds(32 + depth * 8 + r, 1), :]
        sweep_tile(
            t, mine[t * SLOTS + COUNT], (used + 1) // 2, scales[pl.ds(t, 1), :], east, north, table,
            lambda i, n, h, at_row: results[held_by[i], h, pl.ds(held_at[i], 1), :],
            TWO, (which, start, step_e, step_n), (dens, nums),
        )
        return carry

    lax.fori_loop(0, tiles, each, 0)
    shrink = jnp.exp(-scale_rows * (x * x + y * y))
    inv = 1.0 / (1.0 + shrink * rows_of(dens[...], tiles))
    beta_two = jnp.where(present, shrink * rows_of(nums[...], tiles) * inv, 0.0)
    beta_one = own[0]
    one, two = own_block[ONE], own_block[TWO]
    left = jnp.where(present, own_block[PRICE] - one * beta_one - two * beta_two, 0.0)
    hat_two = two * two * inv
    for t in range(tiles):
        for h in range(2):
            at = slice(t * TILE + h * LANES, t * TILE + (h + 1) * LANES)
            betas[0:1, at] = beta_one[h, t : t + 1]
            betas[1:2, at] = beta_two[h, t : t + 1]
            hats[0:1, at] = own[1, h, t : t + 1, :]
            hats[1:2, at] = hat_two[h, t : t + 1]
            residual[0:1, at] = left[h, t : t + 1]


def swap(x, k):
    count = lax.axis_size("tile")
    return lax.ppermute(x, "tile", [(i, i ^ k) for i in range(count)])


def spread(block):
    count = lax.axis_size("tile")
    same = jnp.stack([block] + [swap(block, k) for k in range(2, count, 2)])
    return same, swap(same, 1)


def body(offsets, design, target, beta_second, counts, kernel_width, reach, assignment):
    tiles = counts.shape[0]
    count = lax.axis_size("tile")
    regions = lax.axis_size("region")
    cells = tiles * count
    limit = pltpu.CompilerParams(vmem_limit_bytes=48 * 1024 * 1024)
    price = target.reshape(1, -1)
    block, mine = pl.pallas_call(
        prepare_kernel,
        out_shape=(
            jax.ShapeDtypeStruct((7, 2, tiles, LANES), F32),
            jax.ShapeDtypeStruct((tiles * SLOTS,), I32),
        ),
        in_specs=[VMEM] * 4 + [SMEM] * 4,
        out_specs=(VMEM, SMEM),
        compiler_params=limit,
    )(
        offsets, design, price, beta_second.reshape(1, -1),
        counts, kernel_width, reach.transpose(2, 0, 1), assignment,
    )
    same, other = spread(block)
    dma = pltpu.SemaphoreType.DMA
    edge, inverse, number = pl.pallas_call(
        border_kernel,
        out_shape=(
            jax.ShapeDtypeStruct((2, 136, LANES), F32),
            jax.ShapeDtypeStruct((cells,), I32),
            jax.ShapeDtypeStruct((cells,), I32),
        ),
        in_specs=[ANY, ANY],
        out_specs=(VMEM, SMEM, SMEM),
        scratch_shapes=[
            pltpu.VMEM((count, 7, 2, tiles, LANES), F32),
            pltpu.SMEM((count, 8, LANES), F32),
            dma,
            dma,
        ],
        compiler_params=limit,
    )(same, other)
    moves = []
    for r in range(regions):
        for t in range(count):
            to = r + 1 - 2 * (t % 2)
            if 0 <= to < regions:
                moves.append((r * count + t, to * count + t))
    border = lax.ppermute(edge, ("region", "tile"), moves)
    square = pltpu.VMEM((LANES, LANES), F32)
    lists = [pltpu.SMEM((24,), I32)] * 2 + [pltpu.SMEM((24,), F32)] * 2
    first = pl.pallas_call(
        first_kernel,
        out_shape=jax.ShapeDtypeStruct((2, 88, LANES), F32),
        in_specs=[SMEM, SMEM, ANY, ANY, ANY],
        out_specs=VMEM,
        scratch_shapes=[
            pltpu.VMEM((count + 2, 6, 2, tiles, LANES), F32),
            pltpu.VMEM((6, 2, 24, LANES), F32),
            pltpu.VMEM((24, LANES), F32),
            pltpu.VMEM((24, LANES), F32),
            square,
            square,
            square,
            square,
            pltpu.SMEM((count, 8, LANES), F32),
            pltpu.SMEM((24, LANES), F32),
            pltpu.SMEM((56,), I32),
            pltpu.SMEM((56,), I32),
            *lists,
            dma,
            dma,
        ],
        compiler_params=limit,
    )(inverse, number, same, other, border)
    same_b, other_b = spread(first)
    wide = tiles * TILE
    betas, hats, residual = pl.pallas_call(
        second_kernel,
        out_shape=(
            jax.ShapeDtypeStruct((2, wide), F32),
            jax.ShapeDtypeStruct((2, wide), F32),
            jax.ShapeDtypeStruct((1, wide), F32),
        ),
        in_specs=[SMEM, SMEM, VMEM, ANY, ANY, ANY, ANY, SMEM],
        out_specs=(VMEM, VMEM, VMEM),
        scratch_shapes=[
            pltpu.VMEM((count + count // 2 + 1, 3, 2, tiles, LANES), F32),
            pltpu.VMEM((count, 2, 96, LANES), F32),
            pltpu.VMEM((2, 2, tiles, LANES), F32),
            pltpu.VMEM((tiles, LANES), F32),
            pltpu.VMEM((tiles, LANES), F32),
            square,
            square,
            square,
            square,
            pltpu.SMEM((count, 8, LANES), F32),
            *lists,
            pltpu.SMEM((24,), I32),
            pltpu.SMEM((24,), I32),
            dma,
            dma,
        ],
        compiler_params=limit,
    )(inverse, number, block, same, other, same_b, other_b, mine)
    return (betas, hats, residual.reshape(-1))


def solution(mesh):
    in_specs = (
        P(None, ("region", "tile")),
        P(None, ("region", "tile")),
        P(("region", "tile")),
        P(("region", "tile")),
        P(("region", "tile")),
        P(None, ("region", "tile")),
        P(None, ("region", "tile"), None),
        P("region", "tile"),
    )
    out_specs = (P(None, ("region", "tile")), P(None, ("region", "tile")), P(("region", "tile")))
    return jax.shard_map(body, mesh=mesh, in_specs=in_specs, out_specs=out_specs, check_vma=False)
```

```python
import functools

import jax
import jax.numpy as jnp
from jax import lax
from jax.experimental import pallas as pl
from jax.experimental.pallas import tpu as pltpu
from jax.sharding import PartitionSpec as P

TILE = 256
TX = 4
LANES = 128
TWO, EAST, NORTH, ONE, PART, PRICE, INFO = range(7)
SLOTS = 16
BASE = 32.0 * 1.4426950408889634
LABEL, COUNT, WIDTH, REACH = 0, 1, 2, 3
NEAR = [(a, b) for a in (-1, 0, 1) for b in (-1, 0, 1)]
F32, I32 = jnp.float32, jnp.int32
ANY = pl.BlockSpec(memory_space=pl.ANY)
SMEM = pl.BlockSpec(memory_space=pltpu.SMEM)
VMEM = pl.BlockSpec(memory_space=pltpu.VMEM)


def prepare_kernel(*refs):
    given, (out, mine), held, sem = refs[:8], refs[8:10], refs[10:18], refs[18]
    copies = [pltpu.make_async_copy(a, b, sem) for a, b in zip(given, held)]
    for copy in copies:
        copy.start()
    for copy in copies:
        copy.wait()
    off, des, tgt, sec, counts, widths, reach, cells = held
    lane = lax.broadcasted_iota(I32, (1, LANES), 1)
    packed = []
    for t in range(counts.shape[0]):
        row = jnp.zeros((1, LANES), F32)
        facts = [cells[0, t], counts[t], widths[0, t]] + [reach[e, 0, t] for e in range(9)]
        for k, fact in enumerate(facts):
            row = jnp.where(lane == k, fact.astype(F32), row)
        out[INFO, 0, t : t + 1, :] = row
        facts[WIDTH:] = [widths[1, t]] + [reach[e, 1, t] for e in range(9)]
        for k, fact in enumerate(facts + [jnp.int32(0)] * 4):
            mine[t * SLOTS + k] = fact
        packed.append(row)
        for h in range(2):
            at = slice(t * TILE + h * LANES, t * TILE + (h + 1) * LANES)
            live = lane + h * LANES < counts[t]
            one = jnp.where(live, des[0:1, at], 0.0)
            two = jnp.where(live, des[1:2, at], 0.0)
            price = tgt[0:1, at]
            out[EAST, h, t : t + 1, :] = off[0:1, at] - 0.5
            out[NORTH, h, t : t + 1, :] = off[1:2, at] - 0.5
            out[ONE, h, t : t + 1, :] = one
            out[PART, h, t : t + 1, :] = one * (price - two * sec[0:1, at])
            out[TWO, h, t : t + 1, :] = two
            out[PRICE, h, t : t + 1, :] = price
    for t in range(8):
        out[INFO, 1, t : t + 1, :] = packed[t] + pltpu.roll(packed[t + 8], LANES // 2, 1)
    out[INFO, 1, 8:16, :] = jnp.zeros((8, LANES), F32)


def split(number, size):
    return number >> (size.bit_length() - 1), number & (size - 1)


def fact(facts, number, k):
    block, slot = split(number, SLOTS)
    return facts[block, slot & 7, ((slot >> 3) << 6) + k]


def fetch(same, other, table, fields, sem):
    half = same.shape[0]
    return [
        pltpu.make_async_copy(
            held.at[:, pl.ds(0, fields)], table.at[pl.ds(side * half, half)], sem
        )
        for side, held in enumerate((same, other))
    ]


def fetch_facts(same, other, facts, sem):
    half = same.shape[0]
    return [
        pltpu.make_async_copy(held.at[:, INFO, 1, pl.ds(0, 8)], facts.at[pl.ds(side * half, half)], sem)
        for side, held in enumerate((same, other))
    ]


def invert(facts, inverse, number, cells):
    def step(s, carry):
        cell = fact(facts, s, LABEL).astype(I32)
        inverse[cell] = s
        number[cell] = fact(facts, s, COUNT).astype(I32)
        return carry

    lax.fori_loop(0, cells, step, 0, unroll=8)


def border_kernel(same, other, out, inverse, number, table, facts, sem, fact_sem):
    copies = fetch(same, other, table, 7, sem)
    fact_copies = fetch_facts(same, other, facts, fact_sem)
    for copy in fact_copies + copies:
        copy.start()
    for copy in fact_copies:
        copy.wait()
    cells = inverse.shape[0]
    rows = cells // TX
    per_pair = 8
    invert(facts, inverse, number, cells)
    for copy in copies:
        copy.wait()
    me = lax.axis_index("tile")
    odd = me & 1
    first = (me >> 1) * per_pair
    order = [(0, r) for r in range(1, 9)] + [(1, r) for r in range(1, 9)]
    order += [(0, 0), (0, 9), (1, 0), (1, 9)]
    for i, (away, r) in enumerate(order):
        column = jnp.where(odd == 1, away, TX - 1 - away)
        row = jnp.clip(first + r - 1, 0, rows - 1)
        source = inverse[column * rows + row]
        source = split(source, SLOTS)
        for f, field in enumerate((EAST, NORTH, ONE, PART, INFO)):
            out[:, f * 24 + i : f * 24 + i + 1, :] = row_of(table, field, source)
        if i < 8:
            for f, field in enumerate((TWO, PRICE)):
                out[:, 120 + 8 * f + i : 121 + 8 * f + i, :] = row_of(table, field, source)
    for f in range(5):
        out[:, f * 24 + 20 : f * 24 + 24, :] = jnp.zeros((2, 4, LANES), F32)


def row_of(table, field, source):
    return table[source[0], field, :, pl.ds(source[1], 1), :]


def records(tiles):
    shape = (2, tiles, LANES)
    number = lax.broadcasted_iota(I32, shape, 2) + LANES * lax.broadcasted_iota(I32, shape, 0)
    return number.astype(F32)


def columns_of(rows):
    pad = jnp.zeros((64 - rows.shape[1], LANES), F32)
    return jnp.concatenate([rows[0], pad, rows[1], pad], axis=0).T


def rows_of(columns, tiles):
    flat = columns.T
    return jnp.stack([flat[:tiles], flat[64 : 64 + tiles]])


def blocks_in(number):
    return (number + 63) >> 6


def spread_columns(tiles, number_of, east, north, columns):
    def lay(t, nb, values):
        i = (nb >> 1) * 64 + t
        for k, value in enumerate(values):
            wide = jnp.broadcast_to(value[:, i : i + 1], (64, LANES))
            columns[t, k, nb * 64 : nb * 64 + 64, :] = wide

    low = (east[0:64, :], north[0:64, :])
    for t in range(tiles):
        lay(t, 0, low)
    for t in range(tiles):
        number = number_of(t)

        @pl.when(number > 64)
        def _():
            lay(t, 1, (east[64:128, :], north[64:128, :]))

        @pl.when(number > 128)
        def _():
            lay(t, 2, (east[0:64, :], north[0:64, :]))
            lay(t, 3, (east[64:128, :], north[64:128, :]))


def collect_sums(tiles, number_of, sums, den_ref, num_ref):
    lane = lax.broadcasted_iota(I32, (64, LANES), 1)
    ones = jnp.ones((LANES, LANES), jnp.bfloat16)

    def total(values):
        high = values.astype(jnp.bfloat16)
        low = (values - high.astype(F32)).astype(jnp.bfloat16)
        return jnp.dot(high, ones, preferred_element_type=F32) + jnp.dot(
            low, ones, preferred_element_type=F32
        )

    zero = jnp.zeros((64, LANES), F32)
    for k, held in enumerate((den_ref, num_ref)):
        for nb in range(2):
            result = zero
            for t in range(tiles):
                x = total(sums[t, k, nb * 64 : nb * 64 + 64, :])
                result = jnp.where(lane == t, x, result)
            held[nb * 64 : nb * 64 + 64, :] = result

    def rest(t, carry):
        @pl.when(number_of(t) > 128)
        def _():
            for k, held in enumerate((den_ref, num_ref)):
                x = total(sums[t, k, 128:256, :])
                mine = lax.broadcasted_iota(I32, (128, LANES), 1) == 64 + t
                held[...] = jnp.where(mine, x, held[...])

        return carry

    lax.fori_loop(0, tiles, rest, 0)


STEP = 4


def sweep_tile(t, number, used, scale, columns, sums, table, part, cov, lists):
    words, steps = lists
    scale = jnp.broadcast_to(scale, (8, LANES))

    def block(nb, carry):
        at = pl.ds(pl.multiple_of(nb * 64, 64), 64)
        x = columns[t, 0, at, :].reshape(8, 8, LANES)
        y = columns[t, 1, at, :].reshape(8, 8, LANES)

        def some(p, sums_now):
            den, num = sums_now
            for k in range(STEP):
                i = STEP * p + k
                word = words[i]
                n, slot = split(word & 0xFFFF, SLOTS)
                row = pl.ds(slot, 1)
                h = (word >> 16) & 1
                e = word >> 20

                def wide(values):
                    return jnp.broadcast_to(values, (8, LANES))

                u = wide(table[n, EAST, h, row, :]) + steps[e]
                v = wide(table[n, NORTH, h, row, :]) + steps[9 + e]
                c = wide(table[n, cov, h, row, :])
                d = wide(part(i, n, h, row))
                q = scale * (u * u + v * v)
                w = jnp.exp2(x * u + y * v - q)
                den = den + w * (c * c)
                num = num + w * d
            return den, num

        zero = jnp.zeros((8, 8, LANES), F32)
        den, num = lax.fori_loop(0, (used + STEP - 1) // STEP, some, (zero, zero))
        sums[t, 0, at, :] = den.reshape(64, LANES)
        sums[t, 1, at, :] = num.reshape(64, LANES)
        return carry

    lax.fori_loop(0, blocks_in(number), block, 0)


def set_steps(steps):
    for e, (a, b) in enumerate(NEAR):
        steps[e] = jnp.float32(a)
        steps[9 + e] = jnp.float32(b)


def chunks_in(number):
    return (number > 0).astype(I32) + (number > LANES).astype(I32)


def first_kernel(
    inverse, number, same, other, border, out,
    table, own, scales, numbers, east, north, dens, nums, columns, sums,
    facts, border_facts, window, live, chunks, words, steps, sem, fact_sem,
):
    copies = fetch(same, other, table, 6, sem)
    fact_copies = fetch_facts(same, other, facts, fact_sem)
    cells = inverse.shape[0]
    rows = cells // TX
    blocks = cells // SLOTS
    empty = cells + 20
    for f, field in enumerate((EAST, NORTH, ONE, PART, INFO)):
        for k, size in enumerate((16, 8)):
            held = pl.ds(f * 24 + 16 * k, size)
            if field == INFO:
                to = border_facts.at[pl.ds(16 * k, size)]
                fact_copies.append(pltpu.make_async_copy(border.at[0, held], to, fact_sem))
            else:
                to = table.at[blocks + k, field, :, pl.ds(0, size)]
                copies.append(pltpu.make_async_copy(border.at[:, held], to, sem))
    for f, field in enumerate((TWO, PRICE)):
        to = table.at[blocks, field, :, pl.ds(0, 8)]
        copies.append(pltpu.make_async_copy(border.at[:, pl.ds(120 + 8 * f, 8)], to, sem))
    for copy in fact_copies + copies:
        copy.start()
    for copy in fact_copies:
        copy.wait()
    me = lax.axis_index("tile")
    odd = me & 1
    first = (me >> 1) * 8
    toward = 1 - 2 * odd
    order = [(0, r) for r in range(1, 9)] + [(1, r) for r in range(1, 9)]
    order += [(0, 0), (0, 9), (1, 0), (1, 9)]
    for u in range(5):
        for r in range(10):
            row = first + r - 1
            if u < 2:
                i = order.index((1 - u, r))
                source = cells + i
                held = border_facts[i, COUNT].astype(I32)
            else:
                column = jnp.where(odd == 1, 5 - u, u - 2)
                cell = column * rows + jnp.clip(row, 0, rows - 1)
                source = inverse[cell]
                held = number[cell]
            if r in (0, 9):
                held = jnp.where((row >= 0) & (row < rows), held, 0)
            window[u * 10 + r] = source
            live[u * 10 + r] = held
            chunks[u * 10 + r] = chunks_in(held)
    for copy in copies:
        copy.wait()
    tiles = 24

    def target_fact(t, target, k):
        inner = fact(facts, jnp.minimum(target, cells - 1), k)
        return jnp.where(t < 8, border_facts[jnp.minimum(t, 7), k], inner)

    def gather(t, carry):
        place = ((t >> 3) + 1) * 10 + (t & 7) + 1
        target = window[place]
        at = split(target, SLOTS)
        width = jnp.full((1, LANES), target_fact(t, target, WIDTH), F32)
        scales[pl.ds(t, 1), :] = BASE / (width * width)
        numbers[pl.ds(t, 1), :] = jnp.full((1, LANES), live[place].astype(F32), F32)
        for field in range(6):
            own[field, :, pl.ds(t, 1), :] = row_of(table, field, at)
        return carry

    lax.fori_loop(0, tiles, gather, 0, unroll=2)
    set_steps(steps)
    present = records(tiles) < numbers[...][None]
    scale_rows = scales[...][None]
    x, y = own[EAST], own[NORTH]
    east[...] = columns_of(2.0 * scale_rows * x)
    north[...] = columns_of(2.0 * scale_rows * y)
    dens[...] = jnp.zeros_like(dens)
    nums[...] = jnp.zeros_like(nums)

    def number_of(t):
        return live[((t >> 3) + 1) * 10 + (t & 7) + 1]

    spread_columns(tiles, number_of, east, north, columns)

    def each(t, carry):
        u = (t >> 3) + 1
        r = (t & 7) + 1
        target = window[u * 10 + r]
        number = live[u * 10 + r]
        used = jnp.int32(0)
        for e, (a, b) in enumerate(NEAR):
            place = (u + toward * a) * 10 + r + b
            word = window[place] + (e << 20)
            more = chunks[place]
            if e != 4:
                more = jnp.where(target_fact(t, target, REACH + e) > 0.5, more, 0)
            words[used] = word
            words[used + 1] = word + (1 << 16)
            used = used + more
        for k in range(STEP - 1):
            words[used + k] = jnp.int32(empty)
        lists = (words, steps)
        sweep_tile(
            t, number, used, scales[pl.ds(t, 1), :], columns, sums, table,
            lambda i, n, h, row: table[n, PART, h, row, :], ONE, lists,
        )
        return carry

    lax.fori_loop(0, tiles, each, 0)
    collect_sums(tiles, number_of, sums, dens, nums)
    shrink = jnp.exp2(-scale_rows * (x * x + y * y))
    inv = 1.0 / (1.0 + shrink * rows_of(dens[...], tiles))
    beta = jnp.where(present, shrink * rows_of(nums[...], tiles) * inv, 0.0)
    one, two = own[ONE], own[TWO]
    out[:, 0:24, :] = two * (own[PRICE] - one * beta)
    out[:, 24:40, :] = beta[:, 8:24]
    out[:, 40:56, :] = (one * one * inv)[:, 8:24]
    out[:, 56:64, :] = two[:, 0:8]
    out[:, 64:72, :] = x[:, 0:8]
    out[:, 72:80, :] = y[:, 0:8]
    out[:, 80:88, :] = jnp.broadcast_to(numbers[0:8, :][None], (2, 8, LANES))


def second_kernel(
    inverse, number, own_block, same, other, same_b, other_b, mine,
    betas, hats, residual,
    table, results, own, scales, numbers, east, north, dens, nums, columns, sums,
    border_facts, words, steps, spots, sem, fact_sem,
):
    copies = fetch(same, other, table, 3, sem)
    fact_copies = []
    half, _, _, tiles, _ = same.shape
    cells = inverse.shape[0]
    rows = cells // TX
    blocks = cells // SLOTS
    empty = cells + 2 * half * 8
    for side, held in enumerate((same_b, other_b)):
        at = pl.ds(side * half, half)
        copies.append(pltpu.make_async_copy(held, results.at[at, :, pl.ds(0, 88)], sem))
        fact_copies.append(
            pltpu.make_async_copy(held.at[:, 0, pl.ds(80, 8)], border_facts.at[at], fact_sem)
        )
    for copy in fact_copies + copies:
        copy.start()
    for t in range(tiles):
        width = jnp.full((1, LANES), mine[t * SLOTS + WIDTH].astype(F32), F32)
        scales[t : t + 1, :] = BASE / (width * width)
        numbers[t : t + 1, :] = jnp.full((1, LANES), mine[t * SLOTS + COUNT].astype(F32), F32)
    present = records(tiles) < numbers[...][None]
    scale_rows = scales[...][None]
    x, y = own_block[EAST], own_block[NORTH]
    east[...] = columns_of(2.0 * scale_rows * x)
    north[...] = columns_of(2.0 * scale_rows * y)
    dens[...] = jnp.zeros_like(dens)
    nums[...] = jnp.zeros_like(nums)

    def number_of(t):
        return mine[t * SLOTS + COUNT]

    spread_columns(tiles, number_of, east, north, columns)
    for copy in fact_copies:
        copy.wait()
    me = lax.axis_index("tile")
    for copy in copies:
        copy.wait()

    def lay(n, carry):
        at = pl.ds(pl.multiple_of((n & 1) * 8, 8), 8)
        for field in range(3):
            held = results[n, :, 56 + 8 * field : 64 + 8 * field, :]
            table[blocks + (n >> 1), field, :, at, :] = held
        return carry

    lax.fori_loop(0, 2 * half, lay, 0)
    for field in range(3):
        table[blocks + half, field, :, 0:8, :] = jnp.zeros((2, 8, LANES), F32)
    results[0, :, 88:96, :] = jnp.zeros((2, 8, LANES), F32)

    set_steps(steps)

    def place(low, depth, upper, r):
        k = (upper + 1 - low) ^ me
        n = (k & 1) * half + (k >> 1)
        return n, depth * 8 + r

    def side(column):
        low = (column < TX // 2).astype(I32)
        return low, jnp.where(low == 1, column + 1, TX - column)

    def each(t, carry):
        column, across = split(mine[t * SLOTS + LABEL], rows)
        used = jnp.int32(0)
        sides = [(column + a, *side(column + a)) for a in (-1, 0, 1)]
        lines = []
        for b in (-1, 0, 1):
            row = jnp.clip(across + b, 0, rows - 1)
            lines.append((row, row == across + b, (row >> 3) * 2, row & 7))
        for e, (a, b) in enumerate(NEAR):
            col, low, depth = sides[a + 1]
            row, inside, upper, r = lines[b + 1]
            n, at = place(low, depth, upper, r)
            in_strip = (col >= 0) & (col < TX)
            near = jnp.clip(col, 0, TX - 1) * rows + row
            source = jnp.where(in_strip, inverse[near], cells + n * 8 + r)
            live = jnp.where(in_strip, number[near], border_facts[n, r, 0].astype(I32))
            more = chunks_in(live)
            if e != 4:
                more = jnp.where(inside, more * mine[t * SLOTS + REACH + e], 0)
            word = source + (e << 20)
            words[used] = word
            words[used + 1] = word + (1 << 16)
            spots[used] = (n << 8) + at
            spots[used + 1] = (n << 8) + at
            used = used + more
        for k in range(STEP - 1):
            words[used + k] = jnp.int32(empty)
            spots[used + k] = jnp.int32(88)
        lists = (words, steps)
        n, at = place(*sides[1][1:], *lines[1][2:])
        own[0, :, pl.ds(t, 1), :] = results[n, :, pl.ds(16 + at, 1), :]
        own[1, :, pl.ds(t, 1), :] = results[n, :, pl.ds(32 + at, 1), :]

        def part(i, n, h, row):
            n, at = split(spots[i], 256)
            return results[n, h, pl.ds(at, 1), :]

        sweep_tile(
            t, mine[t * SLOTS + COUNT], used, scales[pl.ds(t, 1), :], columns, sums, table,
            part, TWO, lists,
        )
        return carry

    lax.fori_loop(0, tiles, each, 0)
    collect_sums(tiles, number_of, sums, dens, nums)
    shrink = jnp.exp2(-scale_rows * (x * x + y * y))
    inv = 1.0 / (1.0 + shrink * rows_of(dens[...], tiles))
    beta_two = jnp.where(present, shrink * rows_of(nums[...], tiles) * inv, 0.0)
    beta_one = own[0]
    one, two = own_block[ONE], own_block[TWO]
    left = jnp.where(present, own_block[PRICE] - one * beta_one - two * beta_two, 0.0)
    hat_two = two * two * inv
    for t in range(tiles):
        for h in range(2):
            at = slice(t * TILE + h * LANES, t * TILE + (h + 1) * LANES)
            betas[0:1, at] = beta_one[h, t : t + 1]
            betas[1:2, at] = beta_two[h, t : t + 1]
            hats[0:1, at] = own[1, h, t : t + 1, :]
            hats[1:2, at] = hat_two[h, t : t + 1]
            residual[0:1, at] = left[h, t : t + 1]


def swap(x, k):
    count = lax.axis_size("tile")
    return lax.ppermute(x, "tile", [(i, i ^ k) for i in range(count)])


def spread(block):
    count = lax.axis_size("tile")
    same = jnp.stack([block] + [swap(block, k) for k in range(2, count, 2)])
    return same, swap(same, 1)


def body(offsets, design, target, beta_second, counts, kernel_width, reach, assignment):
    tiles = counts.shape[0]
    count = lax.axis_size("tile")
    regions = lax.axis_size("region")
    cells = tiles * count
    limit = pltpu.CompilerParams(vmem_limit_bytes=48 * 1024 * 1024)
    price = target.reshape(1, -1)
    wide = tiles * TILE
    given = (
        offsets, design, price, beta_second.reshape(1, -1),
        counts, kernel_width, reach.transpose(2, 0, 1), assignment,
    )
    block, mine = pl.pallas_call(
        prepare_kernel,
        out_shape=(
            pltpu.VMEM((7, 2, tiles, LANES), F32),
            jax.ShapeDtypeStruct((tiles * SLOTS,), I32),
        ),
        in_specs=[pl.BlockSpec(memory_space=pltpu.HBM)] * 8,
        out_specs=(VMEM, SMEM),
        scratch_shapes=[pltpu.VMEM((2, wide), F32)] * 2
        + [pltpu.VMEM((1, wide), F32)] * 2
        + [
            pltpu.SMEM((tiles,), I32),
            pltpu.SMEM((2, tiles), I32),
            pltpu.SMEM((9, 2, tiles), I32),
            pltpu.SMEM((1, tiles), I32),
            pltpu.SemaphoreType.DMA,
        ],
        compiler_params=limit,
    )(*[pltpu.with_memory_space_constraint(x, pltpu.HBM) for x in given])
    same, other = spread(block)
    dma = pltpu.SemaphoreType.DMA
    edge, inverse, number = pl.pallas_call(
        border_kernel,
        out_shape=(
            jax.ShapeDtypeStruct((2, 136, LANES), F32),
            jax.ShapeDtypeStruct((cells,), I32),
            jax.ShapeDtypeStruct((cells,), I32),
        ),
        in_specs=[ANY, ANY],
        out_specs=(VMEM, SMEM, SMEM),
        scratch_shapes=[
            pltpu.VMEM((count, 7, 2, tiles, LANES), F32),
            pltpu.SMEM((count, 8, LANES), F32),
            dma,
            dma,
        ],
        compiler_params=limit,
    )(same, other)
    moves = []
    for r in range(regions):
        for t in range(count):
            to = r + 1 - 2 * (t % 2)
            if 0 <= to < regions:
                moves.append((r * count + t, to * count + t))
    border = lax.ppermute(edge, ("region", "tile"), moves)
    square = pltpu.VMEM((LANES, LANES), F32)
    lists = [pltpu.SMEM((24,), I32), pltpu.SMEM((18,), F32)]
    first = pl.pallas_call(
        first_kernel,
        out_shape=jax.ShapeDtypeStruct((2, 88, LANES), F32),
        in_specs=[SMEM, SMEM, ANY, ANY, ANY],
        out_specs=VMEM,
        scratch_shapes=[
            pltpu.VMEM((count + 2, 6, 2, tiles, LANES), F32),
            pltpu.VMEM((6, 2, 24, LANES), F32),
            pltpu.VMEM((24, LANES), F32),
            pltpu.VMEM((24, LANES), F32),
            square,
            square,
            square,
            square,
            pltpu.VMEM((24, 2, TILE, LANES), F32),
            pltpu.VMEM((24, 2, TILE, LANES), F32),
            pltpu.SMEM((count, 8, LANES), F32),
            pltpu.SMEM((24, LANES), F32),
            *[pltpu.SMEM((56,), I32)] * 3,
            *lists,
            dma,
            dma,
        ],
        compiler_params=limit,
    )(inverse, number, same, other, border)
    same_b, other_b = spread(first)
    betas, hats, residual = pl.pallas_call(
        second_kernel,
        out_shape=(
            jax.ShapeDtypeStruct((2, wide), F32),
            jax.ShapeDtypeStruct((2, wide), F32),
            jax.ShapeDtypeStruct((1, wide), F32),
        ),
        in_specs=[SMEM, SMEM, VMEM, ANY, ANY, ANY, ANY, SMEM],
        out_specs=(VMEM, VMEM, VMEM),
        scratch_shapes=[
            pltpu.VMEM((count + count // 2 + 1, 3, 2, tiles, LANES), F32),
            pltpu.VMEM((count, 2, 96, LANES), F32),
            pltpu.VMEM((2, 2, tiles, LANES), F32),
            pltpu.VMEM((tiles, LANES), F32),
            pltpu.VMEM((tiles, LANES), F32),
            square,
            square,
            square,
            square,
            pltpu.VMEM((tiles, 2, TILE, LANES), F32),
            pltpu.VMEM((tiles, 2, TILE, LANES), F32),
            pltpu.SMEM((count, 8, LANES), F32),
            *lists,
            pltpu.SMEM((24,), I32),
            dma,
            dma,
        ],
        compiler_params=limit,
    )(inverse, number, block, same, other, same_b, other_b, mine)
    return (betas, hats, residual.reshape(-1))


def solution(mesh):
    in_specs = (
        P(None, ("region", "tile")),
        P(None, ("region", "tile")),
        P(("region", "tile")),
        P(("region", "tile")),
        P(("region", "tile")),
        P(None, ("region", "tile")),
        P(None, ("region", "tile"), None),
        P("region", "tile"),
    )
    out_specs = (P(None, ("region", "tile")), P(None, ("region", "tile")), P(("region", "tile")))
    return jax.shard_map(body, mesh=mesh, in_specs=in_specs, out_specs=out_specs, check_vma=False)
```

```python
import functools

import jax
import jax.numpy as jnp
from jax import lax
from jax.experimental import pallas as pl
from jax.experimental.pallas import tpu as pltpu
from jax.sharding import PartitionSpec as P

TILE = 256
TX = 4
LANES = 128
TWO, EAST, NORTH, ONE, PART, PRICE, INFO = range(7)
SLOTS = 16
BASE = 32.0 * 1.4426950408889634
LABEL, COUNT, WIDTH, REACH = 0, 1, 2, 3
NEAR = [(a, b) for a in (-1, 0, 1) for b in (-1, 0, 1)]
F32, I32 = jnp.float32, jnp.int32
ANY = pl.BlockSpec(memory_space=pl.ANY)
SMEM = pl.BlockSpec(memory_space=pltpu.SMEM)
VMEM = pl.BlockSpec(memory_space=pltpu.VMEM)


def prepare_kernel(*refs):
    given, (out, mine), held, sem = refs[:8], refs[8:10], refs[10:18], refs[18]
    copies = [pltpu.make_async_copy(a, b, sem) for a, b in zip(given, held)]
    for copy in copies:
        copy.start()
    for copy in copies:
        copy.wait()
    off, des, tgt, sec, counts, widths, reach, cells = held
    lane = lax.broadcasted_iota(I32, (1, LANES), 1)
    packed = []
    for t in range(counts.shape[0]):
        row = jnp.zeros((1, LANES), F32)
        facts = [cells[0, t], counts[t], widths[0, t]] + [reach[e, 0, t] for e in range(9)]
        for k, fact in enumerate(facts):
            row = jnp.where(lane == k, fact.astype(F32), row)
        out[INFO, 0, t : t + 1, :] = row
        facts[WIDTH:] = [widths[1, t]] + [reach[e, 1, t] for e in range(9)]
        for k, fact in enumerate(facts + [jnp.int32(0)] * 4):
            mine[t * SLOTS + k] = fact
        packed.append(row)
        for h in range(2):
            at = slice(t * TILE + h * LANES, t * TILE + (h + 1) * LANES)
            live = lane + h * LANES < counts[t]
            one = jnp.where(live, des[0:1, at], 0.0)
            two = jnp.where(live, des[1:2, at], 0.0)
            price = tgt[0:1, at]
            out[EAST, h, t : t + 1, :] = off[0:1, at] - 0.5
            out[NORTH, h, t : t + 1, :] = off[1:2, at] - 0.5
            out[ONE, h, t : t + 1, :] = one
            out[PART, h, t : t + 1, :] = one * (price - two * sec[0:1, at])
            out[TWO, h, t : t + 1, :] = two
            out[PRICE, h, t : t + 1, :] = price
    for t in range(8):
        out[INFO, 1, t : t + 1, :] = packed[t] + pltpu.roll(packed[t + 8], LANES // 2, 1)
    out[INFO, 1, 8:16, :] = jnp.zeros((8, LANES), F32)


def split(number, size):
    return number >> (size.bit_length() - 1), number & (size - 1)


def fact(facts, number, k):
    block, slot = split(number, SLOTS)
    return facts[block, slot & 7, ((slot >> 3) << 6) + k]


def fetch(same, other, table, fields, sem):
    half = same.shape[0]
    return [
        pltpu.make_async_copy(
            held.at[:, pl.ds(0, fields)], table.at[pl.ds(side * half, half)], sem
        )
        for side, held in enumerate((same, other))
    ]


def fetch_facts(same, other, facts, sem):
    half = same.shape[0]
    return [
        pltpu.make_async_copy(held.at[:, INFO, 1, pl.ds(0, 8)], facts.at[pl.ds(side * half, half)], sem)
        for side, held in enumerate((same, other))
    ]


def invert(facts, inverse, number, cells):
    def step(s, carry):
        cell = fact(facts, s, LABEL).astype(I32)
        inverse[cell] = s
        number[cell] = fact(facts, s, COUNT).astype(I32)
        return carry

    lax.fori_loop(0, cells, step, 0, unroll=8)


ORDER = [(0, r) for r in range(1, 9)] + [(1, r) for r in range(1, 9)]
ORDER += [(0, 0), (0, 9), (1, 0), (1, 9)]
NEAR_ROWS, EDGE_ROWS, SPARE = 32, 24, 30


def border_kernel(same, other, out, inverse, number, facts, fact_sem):
    fact_copies = fetch_facts(same, other, facts, fact_sem)
    for copy in fact_copies:
        copy.start()
    for copy in fact_copies:
        copy.wait()
    cells = inverse.shape[0]
    rows = cells // TX
    invert(facts, inverse, number, cells)
    me = lax.axis_index("tile")
    odd = me & 1
    first = (me >> 1) * 8
    for i, (away, r) in enumerate(ORDER):
        column = jnp.where(odd == 1, away, TX - 1 - away)
        row = jnp.clip(first + r - 1, 0, rows - 1)
        held = rows_at(same, other, inverse[column * rows + row])
        for f, field in enumerate((EAST, NORTH, ONE, PART, INFO)):
            out[:, f * 24 + i : f * 24 + i + 1, :] = held[field]
        if i < 8:
            for f, field in enumerate((TWO, PRICE)):
                out[:, 120 + 8 * f + i : 121 + 8 * f + i, :] = held[field]
    for f in range(5):
        out[:, f * 24 + 20 : f * 24 + 24, :] = jnp.zeros((2, 4, LANES), F32)


def rows_at(same, other, source):
    half = same.shape[0]
    block, slot = split(source, SLOTS)
    at = (block & (half - 1), slice(None), slice(None), pl.ds(slot, 1), slice(None))
    return jnp.where(block >= half, other[at], same[at])


def near_kernel(inverse, number, same, other, near, columns, east, north):
    me = lax.axis_index("tile")
    odd = me & 1
    first = (me >> 1) * 8
    rows = inverse.shape[0] // TX
    for u in range(3):
        column = jnp.where(odd == 1, TX - 1 - u, u)

        def gather(r, carry):
            row = jnp.clip(first + r - 1, 0, rows - 1)
            held = rows_at(same, other, inverse[column * rows + row])
            near[:, :, pl.ds(u * 10 + r, 1), :] = held
            return carry

        lax.fori_loop(0, 10, gather, 0, unroll=2)
    near[:, :, SPARE:NEAR_ROWS, :] = jnp.zeros((7, 2, NEAR_ROWS - SPARE, LANES), F32)

    def targets(field):
        return jnp.concatenate([near[field, :, 1:9, :], near[field, :, 11:19, :]], axis=1)

    info = targets(INFO)[0]
    scale = scale_of(info[:, WIDTH : WIDTH + 1])[None]
    east[...] = columns_of(2.0 * scale * targets(EAST))
    north[...] = columns_of(2.0 * scale * targets(NORTH))

    def number_of(t):
        return number[jnp.where(odd == 1, TX - 1 - t // 8, t // 8) * rows + first + t % 8]

    spread_columns(16, number_of, east, north, columns)


def scale_of(width):
    return jnp.broadcast_to(BASE / (width * width), (width.shape[0], LANES))


def own_columns_kernel(block, mine, columns, scales, east, north):
    tiles = block.shape[2]
    for t in range(tiles):
        width = jnp.full((1, LANES), mine[t * SLOTS + WIDTH].astype(F32), F32)
        scales[t : t + 1, :] = BASE / (width * width)
    scale = scales[...][None]
    east[...] = columns_of(2.0 * scale * block[EAST])
    north[...] = columns_of(2.0 * scale * block[NORTH])
    spread_columns(tiles, lambda t: mine[t * SLOTS + COUNT], east, north, columns)


def records(tiles):
    shape = (2, tiles, LANES)
    number = lax.broadcasted_iota(I32, shape, 2) + LANES * lax.broadcasted_iota(I32, shape, 0)
    return number.astype(F32)


def columns_of(rows):
    pad = jnp.zeros((64 - rows.shape[1], LANES), F32)
    return jnp.concatenate([rows[0], pad, rows[1], pad], axis=0).T


def rows_of(low, high, tiles):
    low, high = low.T, high.T
    return [jnp.stack([low[k : k + tiles], high[k : k + tiles]]) for k in (0, 64)]


def blocks_in(number):
    return (number + 63) >> 6


def spread_columns(tiles, number_of, east, north, columns):
    def lay(t, nb, values):
        i = (nb >> 1) * 64 + t
        for k, value in enumerate(values):
            wide = jnp.broadcast_to(value[:, i : i + 1], (64, LANES))
            columns[t, k, nb * 64 : nb * 64 + 64, :] = wide

    low = (east[0:64, :], north[0:64, :])
    for t in range(tiles):
        lay(t, 0, low)
    for t in range(tiles):
        number = number_of(t)

        @pl.when(number > 64)
        def _():
            lay(t, 1, (east[64:128, :], north[64:128, :]))

        @pl.when(number > 128)
        def _():
            lay(t, 2, (east[0:64, :], north[0:64, :]))
            lay(t, 3, (east[64:128, :], north[64:128, :]))


def collect_sums(tiles, number_of, sums, low_ref, high_ref):
    split_at = lax.broadcasted_iota(I32, (2 * LANES, LANES), 0) // LANES
    sides = lax.broadcasted_iota(I32, (2 * LANES, LANES), 1) // 64
    ones = (split_at == sides).astype(F32).astype(jnp.bfloat16)
    lane = lax.broadcasted_iota(I32, (64, LANES), 1) & 63

    def total(values):
        high = values.astype(jnp.bfloat16)
        low = (values - high.astype(F32)).astype(jnp.bfloat16)
        return jnp.dot(high, ones, preferred_element_type=F32) + jnp.dot(
            low, ones, preferred_element_type=F32
        )

    for nb in range(2):
        result = jnp.zeros((64, LANES), F32)
        for t in range(tiles):
            x = total(sums[t, nb * 64 : nb * 64 + 64, :])
            result = jnp.where(lane == t, x, result)
        low_ref[nb * 64 : nb * 64 + 64, :] = result
    high_ref[...] = jnp.zeros_like(high_ref)

    def rest(t, carry):
        @pl.when(number_of(t) > 128)
        def _():
            x = total(sums[t, 128:256, :])
            mine = lax.broadcasted_iota(I32, (128, LANES), 1) & 63
            high_ref[...] = jnp.where(mine == t, x, high_ref[...])

        return carry

    lax.fori_loop(0, tiles, rest, 0)


STEP = 4


def sweep_tile(t, at_column, number, used, scale, columns, sums, rows_for, lists):
    words, steps = lists
    scale = jnp.broadcast_to(scale, (8, LANES))

    def block(nb, carry):
        at = pl.ds(pl.multiple_of(nb * 64, 64), 64)
        x = columns[at_column, 0, at, :].reshape(8, 8, LANES)
        y = columns[at_column, 1, at, :].reshape(8, 8, LANES)

        def some(p, sums_now):
            den, num = sums_now
            for k in range(STEP):
                i = STEP * p + k
                word = words[i]
                e = word >> 20
                u, v, c, d = rows_for(i, word & 0xFFFF, (word >> 16) & 1)
                u = jnp.broadcast_to(u, (8, LANES)) + steps[e]
                v = jnp.broadcast_to(v, (8, LANES)) + steps[9 + e]
                c = jnp.broadcast_to(c, (8, LANES))
                d = jnp.broadcast_to(d, (8, LANES))
                fade = jnp.exp2(-scale * (u * u + v * v))
                w = jnp.exp2(x * u + y * v)
                den = den + w * (c * c * fade)
                num = num + w * (d * fade)
            return den, num

        zero = jnp.zeros((8, 8, LANES), F32)
        den, num = lax.fori_loop(0, (used + STEP - 1) // STEP, some, (zero, zero))
        sums[t, at, 0:LANES] = den.reshape(64, LANES)
        sums[t, at, LANES : 2 * LANES] = num.reshape(64, LANES)
        return carry

    lax.fori_loop(0, blocks_in(number), block, 0)


def set_steps(steps):
    for e, (a, b) in enumerate(NEAR):
        steps[e] = jnp.float32(a)
        steps[9 + e] = jnp.float32(b)


def chunks_in(number):
    return (number > 0).astype(I32) + (number > LANES).astype(I32)


def first_kernel(
    number, near, near_columns, border, out,
    table, own, east, north, low, high, columns, sums,
    facts, window, live, chunks, words, steps, sem, fact_sem,
):
    cells = number.shape[0]
    rows = cells // TX
    near_at, edge_at = pl.ds(0, NEAR_ROWS), pl.ds(NEAR_ROWS, EDGE_ROWS)
    copies = [pltpu.make_async_copy(near.at[pl.ds(0, 6)], table.at[:, :, near_at], sem)]
    fact_copies = [
        pltpu.make_async_copy(near.at[INFO, 0], facts.at[near_at], fact_sem),
        pltpu.make_async_copy(border.at[0, pl.ds(4 * 24, 24)], facts.at[edge_at], fact_sem),
    ]
    for f, field in enumerate((EAST, NORTH, ONE, PART)):
        held = border.at[:, pl.ds(f * 24, 24)]
        copies.append(pltpu.make_async_copy(held, table.at[field, :, edge_at], sem))
    for f, field in enumerate((TWO, PRICE)):
        held = border.at[:, pl.ds(120 + 8 * f, 8)]
        copies.append(pltpu.make_async_copy(held, table.at[field, :, pl.ds(NEAR_ROWS, 8)], sem))
    for copy in fact_copies + copies:
        copy.start()
    for copy in fact_copies:
        copy.wait()
    me = lax.axis_index("tile")
    odd = me & 1
    first = (me >> 1) * 8
    toward = 1 - 2 * odd
    for u in range(5):
        for r in range(10):
            row = first + r - 1
            if u < 2:
                source = NEAR_ROWS + ORDER.index((1 - u, r))
                held = facts[source, COUNT].astype(I32)
            else:
                source = (u - 2) * 10 + r
                column = jnp.where(odd == 1, 5 - u, u - 2)
                held = number[column * rows + jnp.clip(row, 0, rows - 1)]
            if r in (0, 9):
                held = jnp.where((row >= 0) & (row < rows), held, 0)
            window[u * 10 + r] = jnp.int32(source)
            live[u * 10 + r] = held
            chunks[u * 10 + r] = chunks_in(held)
    set_steps(steps)
    for copy in copies:
        copy.wait()
    tiles = 24
    edge_info = border[0, 4 * 24 : 4 * 24 + 8, :]
    info = jnp.concatenate([edge_info, near[INFO, 0, 1:9, :], near[INFO, 0, 11:19, :]], axis=0)
    scales = scale_of(info[:, WIDTH : WIDTH + 1])
    counts = jnp.broadcast_to(info[:, COUNT : COUNT + 1], (tiles, LANES))

    def of_targets(field):
        parts = [table[field, :, 32:40, :], table[field, :, 1:9, :], table[field, :, 11:19, :]]
        return jnp.concatenate(parts, axis=1)

    present = records(tiles) < counts[None]
    scale_rows = scales[None]
    own[...] = scales
    x, y = of_targets(EAST), of_targets(NORTH)
    east[...] = columns_of(2.0 * scale_rows[:, 0:8] * x[:, 0:8])
    north[...] = columns_of(2.0 * scale_rows[:, 0:8] * y[:, 0:8])

    def number_of(t):
        return live[((t >> 3) + 1) * 10 + (t & 7) + 1]

    spread_columns(8, number_of, east, north, columns)

    def rows_for(i, source, h):
        at = pl.ds(source, 1)
        return [table[field, h, at, :] for field in (EAST, NORTH, ONE, PART)]

    def each(t, carry, held, skip):
        u = (t >> 3) + 1
        r = (t & 7) + 1
        target = window[u * 10 + r]
        used = jnp.int32(0)
        for e, (a, b) in enumerate(NEAR):
            place = (u + toward * a) * 10 + r + b
            word = window[place] + (e << 20)
            more = chunks[place]
            if e != 4:
                more = jnp.where(facts[target, REACH + e] > 0.5, more, 0)
            words[used] = word
            words[used + 1] = word + (1 << 16)
            used = used + more
        for k in range(STEP - 1):
            words[used + k] = jnp.int32(SPARE)
        sweep_tile(
            t, t - skip, number_of(t), used, own[pl.ds(t, 1), :], held, sums,
            rows_for, (words, steps),
        )
        return carry

    lax.fori_loop(0, 8, lambda t, c: each(t, c, columns, 0), 0)
    lax.fori_loop(8, tiles, lambda t, c: each(t, c, near_columns, 8), 0)
    collect_sums(tiles, number_of, sums, low, high)
    shrink = jnp.exp2(-scale_rows * (x * x + y * y))
    den, num = rows_of(low[...], high[...], tiles)
    inv = 1.0 / (1.0 + shrink * den)
    beta = jnp.where(present, shrink * num * inv, 0.0)
    one, two = of_targets(ONE), of_targets(TWO)
    out[:, 0:24, :] = two * (of_targets(PRICE) - one * beta)
    out[:, 24:40, :] = beta[:, 8:24]
    out[:, 40:56, :] = jnp.where(present, one * one * inv, 0.0)[:, 8:24]
    out[:, 56:64, :] = two[:, 0:8]
    out[:, 64:72, :] = x[:, 0:8]
    out[:, 72:80, :] = y[:, 0:8]
    out[:, 80:88, :] = jnp.broadcast_to(counts[0:8][None], (2, 8, LANES))


def second_kernel(
    inverse, number, own_block, columns, same, other, same_b, other_b, mine,
    betas, hats, residual,
    table, results, own, scales, numbers, low, high, sums,
    border_facts, words, steps, spots, sem, fact_sem,
):
    copies = fetch(same, other, table, 3, sem)
    fact_copies = []
    half, _, _, tiles, _ = same.shape
    cells = inverse.shape[0]
    rows = cells // TX
    blocks = cells // SLOTS
    empty = cells + 2 * half * 8
    for side, held in enumerate((same_b, other_b)):
        at = pl.ds(side * half, half)
        copies.append(pltpu.make_async_copy(held, results.at[at, :, pl.ds(0, 88)], sem))
        fact_copies.append(
            pltpu.make_async_copy(held.at[:, 0, pl.ds(80, 8)], border_facts.at[at], fact_sem)
        )
    for copy in fact_copies + copies:
        copy.start()
    for t in range(tiles):
        width = jnp.full((1, LANES), mine[t * SLOTS + WIDTH].astype(F32), F32)
        scales[t : t + 1, :] = BASE / (width * width)
        numbers[t : t + 1, :] = jnp.full((1, LANES), mine[t * SLOTS + COUNT].astype(F32), F32)
    present = records(tiles) < numbers[...][None]
    scale_rows = scales[...][None]
    x, y = own_block[EAST], own_block[NORTH]

    def number_of(t):
        return mine[t * SLOTS + COUNT]

    for copy in fact_copies:
        copy.wait()
    me = lax.axis_index("tile")
    for copy in copies:
        copy.wait()

    def lay(n, carry):
        at = pl.ds(pl.multiple_of((n & 1) * 8, 8), 8)
        for field in range(3):
            held = results[n, :, 56 + 8 * field : 64 + 8 * field, :]
            table[blocks + (n >> 1), field, :, at, :] = held
        return carry

    lax.fori_loop(0, 2 * half, lay, 0)
    for field in range(3):
        table[blocks + half, field, :, 0:8, :] = jnp.zeros((2, 8, LANES), F32)
    results[0, :, 88:96, :] = jnp.zeros((2, 8, LANES), F32)

    set_steps(steps)

    def place(low, depth, upper, r):
        k = (upper + 1 - low) ^ me
        n = (k & 1) * half + (k >> 1)
        return n, depth * 8 + r

    def side(column):
        low = (column < TX // 2).astype(I32)
        return low, jnp.where(low == 1, column + 1, TX - column)

    def rows_for(i, source, h):
        n, slot = split(source, SLOTS)
        m, at = split(spots[i], 256)
        held = [table[n, field, h, pl.ds(slot, 1), :] for field in (EAST, NORTH, TWO)]
        return [*held, results[m, h, pl.ds(at, 1), :]]

    def each(t, carry):
        column, across = split(mine[t * SLOTS + LABEL], rows)
        used = jnp.int32(0)
        sides = [(column + a, *side(column + a)) for a in (-1, 0, 1)]
        lines = []
        for b in (-1, 0, 1):
            row = jnp.clip(across + b, 0, rows - 1)
            lines.append((row, row == across + b, (row >> 3) * 2, row & 7))
        for e, (a, b) in enumerate(NEAR):
            col, low, depth = sides[a + 1]
            row, inside, upper, r = lines[b + 1]
            n, at = place(low, depth, upper, r)
            in_strip = (col >= 0) & (col < TX)
            near = jnp.clip(col, 0, TX - 1) * rows + row
            source = jnp.where(in_strip, inverse[near], cells + n * 8 + r)
            live = jnp.where(in_strip, number[near], border_facts[n, r, 0].astype(I32))
            more = chunks_in(live)
            if e != 4:
                more = jnp.where(inside, more * mine[t * SLOTS + REACH + e], 0)
            word = source + (e << 20)
            words[used] = word
            words[used + 1] = word + (1 << 16)
            spots[used] = (n << 8) + at
            spots[used + 1] = (n << 8) + at
            used = used + more
        for k in range(STEP - 1):
            words[used + k] = jnp.int32(empty)
            spots[used + k] = jnp.int32(88)
        n, at = place(*sides[1][1:], *lines[1][2:])
        own[0, :, pl.ds(t, 1), :] = results[n, :, pl.ds(16 + at, 1), :]
        own[1, :, pl.ds(t, 1), :] = results[n, :, pl.ds(32 + at, 1), :]

        sweep_tile(
            t, t, number_of(t), used, scales[pl.ds(t, 1), :], columns, sums,
            rows_for, (words, steps),
        )
        return carry

    lax.fori_loop(0, tiles, each, 0)
    collect_sums(tiles, number_of, sums, low, high)
    shrink = jnp.exp2(-scale_rows * (x * x + y * y))
    den, num = rows_of(low[...], high[...], tiles)
    inv = 1.0 / (1.0 + shrink * den)
    beta_two = jnp.where(present, shrink * num * inv, 0.0)
    beta_one = own[0]
    one, two = own_block[ONE], own_block[TWO]
    left = jnp.where(present, own_block[PRICE] - one * beta_one - two * beta_two, 0.0)
    hat_two = jnp.where(present, two * two * inv, 0.0)
    for t in range(tiles):
        for h in range(2):
            at = slice(t * TILE + h * LANES, t * TILE + (h + 1) * LANES)
            betas[0:1, at] = beta_one[h, t : t + 1]
            betas[1:2, at] = beta_two[h, t : t + 1]
            hats[0:1, at] = own[1, h, t : t + 1, :]
            hats[1:2, at] = hat_two[h, t : t + 1]
            residual[0:1, at] = left[h, t : t + 1]


def swap(x, k):
    count = lax.axis_size("tile")
    return lax.ppermute(x, "tile", [(i, i ^ k) for i in range(count)])


def spread(block):
    count = lax.axis_size("tile")
    same = jnp.stack([block] + [swap(block, k) for k in range(2, count, 2)])
    return same, swap(same, 1)


def body(offsets, design, target, beta_second, counts, kernel_width, reach, assignment):
    tiles = counts.shape[0]
    count = lax.axis_size("tile")
    regions = lax.axis_size("region")
    cells = tiles * count
    limit = pltpu.CompilerParams(vmem_limit_bytes=24 * 1024 * 1024)
    price = target.reshape(1, -1)
    wide = tiles * TILE
    given = (
        offsets, design, price, beta_second.reshape(1, -1),
        counts, kernel_width, reach.transpose(2, 0, 1), assignment,
    )
    block, mine = pl.pallas_call(
        prepare_kernel,
        out_shape=(
            pltpu.VMEM((7, 2, tiles, LANES), F32),
            jax.ShapeDtypeStruct((tiles * SLOTS,), I32),
        ),
        in_specs=[pl.BlockSpec(memory_space=pltpu.HBM)] * 8,
        out_specs=(VMEM, SMEM),
        scratch_shapes=[pltpu.VMEM((2, wide), F32)] * 2
        + [pltpu.VMEM((1, wide), F32)] * 2
        + [
            pltpu.SMEM((tiles,), I32),
            pltpu.SMEM((2, tiles), I32),
            pltpu.SMEM((9, 2, tiles), I32),
            pltpu.SMEM((1, tiles), I32),
            pltpu.SemaphoreType.DMA,
        ],
        compiler_params=limit,
    )(*[pltpu.with_memory_space_constraint(x, pltpu.HBM) for x in given])
    square = pltpu.VMEM((LANES, LANES), F32)
    own_columns = pl.pallas_call(
        own_columns_kernel,
        out_shape=pltpu.VMEM((tiles, 2, TILE, LANES), F32),
        in_specs=[VMEM, SMEM],
        out_specs=VMEM,
        scratch_shapes=[pltpu.VMEM((tiles, LANES), F32), square, square],
        compiler_params=limit,
        cost_estimate=pl.CostEstimate(flops=4000000, bytes_accessed=4000000, transcendentals=0),
    )(block, mine)
    same, other = spread(block)
    dma = pltpu.SemaphoreType.DMA
    edge, inverse, number = pl.pallas_call(
        border_kernel,
        out_shape=(
            jax.ShapeDtypeStruct((2, 136, LANES), F32),
            jax.ShapeDtypeStruct((cells,), I32),
            jax.ShapeDtypeStruct((cells,), I32),
        ),
        in_specs=[VMEM, VMEM],
        out_specs=(VMEM, SMEM, SMEM),
        scratch_shapes=[pltpu.SMEM((count, 8, LANES), F32), dma],
        compiler_params=limit,
    )(same, other)
    near, near_columns = pl.pallas_call(
        near_kernel,
        out_shape=(
            pltpu.VMEM((7, 2, NEAR_ROWS, LANES), F32),
            pltpu.VMEM((16, 2, TILE, LANES), F32),
        ),
        in_specs=[SMEM, SMEM, VMEM, VMEM],
        out_specs=(VMEM, VMEM),
        scratch_shapes=[square, square],
        compiler_params=limit,
        cost_estimate=pl.CostEstimate(flops=4000000, bytes_accessed=4000000, transcendentals=0),
    )(inverse, number, same, other)
    moves = []
    for r in range(regions):
        for t in range(count):
            to = r + 1 - 2 * (t % 2)
            if 0 <= to < regions:
                moves.append((r * count + t, to * count + t))
    border = lax.ppermute(edge, ("region", "tile"), moves)
    lists = [pltpu.SMEM((24,), I32), pltpu.SMEM((18,), F32)]
    first = pl.pallas_call(
        first_kernel,
        out_shape=jax.ShapeDtypeStruct((2, 88, LANES), F32),
        in_specs=[SMEM, VMEM, VMEM, VMEM],
        out_specs=VMEM,
        scratch_shapes=[
            pltpu.VMEM((6, 2, NEAR_ROWS + EDGE_ROWS, LANES), F32),
            pltpu.VMEM((24, LANES), F32),
            square,
            square,
            square,
            square,
            pltpu.VMEM((8, 2, TILE, LANES), F32),
            pltpu.VMEM((24, TILE, 2 * LANES), F32),
            pltpu.SMEM((NEAR_ROWS + EDGE_ROWS, LANES), F32),
            *[pltpu.SMEM((56,), I32)] * 3,
            *lists,
            dma,
            dma,
        ],
        compiler_params=limit,
    )(number, near, near_columns, border)
    same_b, other_b = spread(first)
    betas, hats, residual = pl.pallas_call(
        second_kernel,
        out_shape=(
            jax.ShapeDtypeStruct((2, wide), F32),
            jax.ShapeDtypeStruct((2, wide), F32),
            jax.ShapeDtypeStruct((1, wide), F32),
        ),
        in_specs=[SMEM, SMEM, VMEM, VMEM, ANY, ANY, ANY, ANY, SMEM],
        out_specs=(VMEM, VMEM, VMEM),
        scratch_shapes=[
            pltpu.VMEM((count + count // 2 + 1, 3, 2, tiles, LANES), F32),
            pltpu.VMEM((count, 2, 96, LANES), F32),
            pltpu.VMEM((2, 2, tiles, LANES), F32),
            pltpu.VMEM((tiles, LANES), F32),
            pltpu.VMEM((tiles, LANES), F32),
            square,
            square,
            pltpu.VMEM((tiles, TILE, 2 * LANES), F32),
            pltpu.SMEM((count, 8, LANES), F32),
            *lists,
            pltpu.SMEM((24,), I32),
            dma,
            dma,
        ],
        compiler_params=limit,
    )(inverse, number, block, own_columns, same, other, same_b, other_b, mine)
    return (betas, hats, residual.reshape(-1))


def solution(mesh):
    in_specs = (
        P(None, ("region", "tile")),
        P(None, ("region", "tile")),
        P(("region", "tile")),
        P(("region", "tile")),
        P(("region", "tile")),
        P(None, ("region", "tile")),
        P(None, ("region", "tile"), None),
        P("region", "tile"),
    )
    out_specs = (P(None, ("region", "tile")), P(None, ("region", "tile")), P(("region", "tile")))
    return jax.shard_map(body, mesh=mesh, in_specs=in_specs, out_specs=out_specs, check_vma=False)
```

```python
import functools

import jax
import jax.numpy as jnp
from jax import lax
from jax.experimental import pallas as pl
from jax.experimental.pallas import tpu as pltpu
from jax.sharding import PartitionSpec as P

TILE = 256
TX = 4
LANES = 128
TWO, EAST, NORTH, ONE, PART, PRICE, INFO = range(7)
SLOTS = 16
BASE = 32.0 * 1.4426950408889634
LABEL, COUNT, WIDTH, REACH = 0, 1, 2, 3
NEAR = [(a, b) for a in (-1, 0, 1) for b in (-1, 0, 1)]
F32, I32 = jnp.float32, jnp.int32
ANY = pl.BlockSpec(memory_space=pl.ANY)
SMEM = pl.BlockSpec(memory_space=pltpu.SMEM)
VMEM = pl.BlockSpec(memory_space=pltpu.VMEM)


def prepare_kernel(*refs):
    given, (out, mine), held, sem = refs[:8], refs[8:10], refs[10:18], refs[18]
    copies = [pltpu.make_async_copy(a, b, sem) for a, b in zip(given, held)]
    for copy in copies:
        copy.start()
    for copy in copies:
        copy.wait()
    off, des, tgt, sec, counts, widths, reach, cells = held
    lane = lax.broadcasted_iota(I32, (1, LANES), 1)
    for t in range(counts.shape[0]):
        row = jnp.zeros((1, LANES), F32)
        facts = [cells[0, t], counts[t], widths[0, t]] + [reach[e, 0, t] for e in range(9)]
        for k, fact in enumerate(facts):
            row = jnp.where(lane == k, fact.astype(F32), row)
        out[INFO, 0, t : t + 1, :] = row
        for k, value in enumerate([widths[1, t]] + [reach[e, 1, t] for e in range(9)]):
            row = jnp.where(lane == WIDTH + k, value.astype(F32), row)
        mine[t : t + 1, :] = row
        for h in range(2):
            at = slice(t * TILE + h * LANES, t * TILE + (h + 1) * LANES)
            live = lane + h * LANES < counts[t]
            one = jnp.where(live, des[0:1, at], 0.0)
            two = jnp.where(live, des[1:2, at], 0.0)
            price = tgt[0:1, at]
            out[EAST, h, t : t + 1, :] = off[0:1, at] - 0.5
            out[NORTH, h, t : t + 1, :] = off[1:2, at] - 0.5
            out[ONE, h, t : t + 1, :] = one
            out[PART, h, t : t + 1, :] = one * (price - two * sec[0:1, at])
            out[TWO, h, t : t + 1, :] = two
            out[PRICE, h, t : t + 1, :] = price
    out[INFO, 1] = jnp.zeros_like(out[INFO, 1])


def split(number, size):
    return number >> (size.bit_length() - 1), number & (size - 1)


def fetch(same, other, table, fields, sem):
    half = same.shape[0]
    return [
        pltpu.make_async_copy(
            held.at[:, pl.ds(0, fields)], table.at[pl.ds(side * half, half)], sem
        )
        for side, held in enumerate((same, other))
    ]


ORDER = [(0, r) for r in range(1, 9)] + [(1, r) for r in range(1, 9)]
ORDER += [(0, 0), (0, 9), (1, 0), (1, 9)]
NEAR_ROWS, EDGE_ROWS, SPARE = 32, 24, 30


def wanted_cells(rows):
    me = lax.axis_index("tile")
    odd = me & 1
    first = (me >> 1) * 8
    i = lax.broadcasted_iota(I32, (64, LANES), 0)
    u = (i >= 10).astype(I32) + (i >= 20).astype(I32)
    j = i - NEAR_ROWS
    away = jnp.where(j < 16, j >> 3, (j >> 1) & 1)
    own = i < NEAR_ROWS
    r = jnp.where(own, i - 10 * u, jnp.where(j < 16, (j & 7) + 1, (j & 1) * 9))
    low = jnp.where(own, u, TX - 1 - away)
    column = jnp.where(odd == 1, TX - 1 - low, low)
    cell = column * rows + jnp.clip(first + r - 1, 0, rows - 1)
    none = (i == SPARE) | (i == SPARE + 1) | (j >= len(ORDER))
    return jnp.where(none, -1, cell).astype(F32)


def border_kernel(same, other, out, near):
    half = same.shape[0]
    cells = 2 * half * SLOTS

    def plane(field, h):
        parts = [x[:, field, h].reshape(half * SLOTS, LANES) for x in (same, other)]
        return jnp.concatenate(parts, axis=0)

    info = plane(INFO, 0)
    wanted = wanted_cells(cells // TX)
    hot = []
    for k in range(0, cells, LANES):
        labels = info[k : k + LANES].T[LABEL : LABEL + 1]
        hot.append((jnp.broadcast_to(labels, wanted.shape) == wanted).astype(F32))
    hot = jnp.concatenate(hot, axis=1).astype(jnp.bfloat16)

    def pick(values, pieces):
        total = jnp.zeros((64, LANES), F32)
        for _ in range(pieces):
            piece = values.astype(jnp.bfloat16)
            values = values - piece.astype(F32)
            total = total + jnp.dot(hot, piece, preferred_element_type=F32)
        return total

    for field in (EAST, NORTH, ONE, PART, INFO, TWO, PRICE):
        for h in range(2):
            if field != INFO:
                got = pick(plane(field, h), 3)
            elif h == 0:
                got = pick(info, 1)
            near[field, h] = got[0:NEAR_ROWS]
            edge = got[NEAR_ROWS : NEAR_ROWS + EDGE_ROWS]
            if field in (TWO, PRICE):
                f = (TWO, PRICE).index(field)
                out[h, 120 + 8 * f : 128 + 8 * f, :] = edge[0:8]
            else:
                f = (EAST, NORTH, ONE, PART, INFO).index(field)
                out[h, f * 24 : f * 24 + 24, :] = edge


def targets_of(near, field):
    return jnp.concatenate([near[field, :, 1:9, :], near[field, :, 11:19, :]], axis=1)


def near_kernel(near, columns, east, north, facts, sem):
    copy = pltpu.make_async_copy(near.at[INFO, 0], facts, sem)
    copy.start()
    info = targets_of(near, INFO)[0]
    scale = scale_of(info[:, WIDTH : WIDTH + 1])[None]
    east[...] = columns_of(2.0 * scale * targets_of(near, EAST))
    north[...] = columns_of(2.0 * scale * targets_of(near, NORTH))

    def number_of(t):
        return facts[(t >> 3) * 10 + (t & 7) + 1, COUNT].astype(I32)

    spread_columns(16, number_of, east, north, columns, copy.wait)


USED, LIVE, HOLDER, HELD_AT = 100, 101, 102, 103


def column_of(info, k):
    return jnp.broadcast_to(info[:, k : k + 1], (info.shape[0], LANES))


def chunks_in(number):
    return (number > 0.0).astype(I32) + (number > LANES).astype(I32)


def list_chunks(entries, number, spare):
    lane = lax.broadcasted_iota(I32, number.shape, 1)
    words = jnp.full(number.shape, spare, I32)
    used = jnp.zeros(number.shape, I32)
    for word, chunks in entries:
        words = jnp.where((lane == used) & (chunks > 0), word, words)
        words = jnp.where((lane == used + 1) & (chunks > 1), word + (1 << 10), words)
        used = used + chunks
    words = jnp.where(lane == USED, used, words)
    return jnp.where(lane == LIVE, number.astype(I32), words)


def place_of(column, row, me, half):
    low = (column < TX // 2).astype(I32)
    depth = jnp.where(low == 1, column + 1, TX - column)
    k = ((row >> 3) * 2 + 1 - low) ^ me
    return (k & 1) * half + (k >> 1), depth * 8 + (row & 7)


def scale_of(width):
    return jnp.broadcast_to(BASE / (width * width), (width.shape[0], LANES))


def own_columns_kernel(block, mine, columns, east, north, facts, sem):
    copy = pltpu.make_async_copy(mine, facts, sem)
    copy.start()
    scale = scale_of(mine[:, WIDTH : WIDTH + 1])[None]
    east[...] = columns_of(2.0 * scale * block[EAST])
    north[...] = columns_of(2.0 * scale * block[NORTH])

    def number_of(t):
        return facts[t, COUNT].astype(I32)

    spread_columns(block.shape[2], number_of, east, north, columns, copy.wait)


def records(tiles):
    shape = (2, tiles, LANES)
    number = lax.broadcasted_iota(I32, shape, 2) + LANES * lax.broadcasted_iota(I32, shape, 0)
    return number.astype(F32)


def columns_of(rows):
    pad = jnp.zeros((64 - rows.shape[1], LANES), F32)
    return jnp.concatenate([rows[0], pad, rows[1], pad], axis=0).T


def rows_of(low, high, tiles):
    low, high = low.T, high.T
    return [jnp.stack([low[k : k + tiles], high[k : k + tiles]]) for k in (0, 64)]


def blocks_in(number):
    return (number + 63) >> 6


def spread_columns(tiles, number_of, east, north, columns, ready=None):
    def lay(t, nb, values):
        i = (nb >> 1) * 64 + t
        for k, value in enumerate(values):
            wide = jnp.broadcast_to(value[:, i : i + 1], (64, LANES))
            columns[t, k, nb * 64 : nb * 64 + 64, :] = wide

    low = (east[0:64, :], north[0:64, :])
    for t in range(tiles):
        lay(t, 0, low)
    if ready is not None:
        ready()
    for t in range(tiles):
        number = number_of(t)

        @pl.when(number > 64)
        def _():
            lay(t, 1, (east[64:128, :], north[64:128, :]))

        @pl.when(number > 128)
        def _():
            lay(t, 2, (east[0:64, :], north[0:64, :]))
            lay(t, 3, (east[64:128, :], north[64:128, :]))


def collect_sums(tiles, number_of, sums, low_ref, high_ref):
    split_at = lax.broadcasted_iota(I32, (2 * LANES, LANES), 0) // LANES
    sides = lax.broadcasted_iota(I32, (2 * LANES, LANES), 1) // 64
    ones = (split_at == sides).astype(F32).astype(jnp.bfloat16)
    lane = lax.broadcasted_iota(I32, (64, LANES), 1) & 63

    def total(values):
        high = values.astype(jnp.bfloat16)
        low = (values - high.astype(F32)).astype(jnp.bfloat16)
        return jnp.dot(high, ones, preferred_element_type=F32) + jnp.dot(
            low, ones, preferred_element_type=F32
        )

    for nb in range(2):
        result = jnp.zeros((64, LANES), F32)
        for t in range(tiles):
            x = total(sums[t, nb * 64 : nb * 64 + 64, :])
            result = jnp.where(lane == t, x, result)
        low_ref[nb * 64 : nb * 64 + 64, :] = result
    high_ref[...] = jnp.zeros_like(high_ref)

    def rest(t, carry):
        @pl.when(number_of(t) > 128)
        def _():
            x = total(sums[t, 128:256, :])
            mine = lax.broadcasted_iota(I32, (128, LANES), 1) & 63
            high_ref[...] = jnp.where(mine == t, x, high_ref[...])

        return carry

    lax.fori_loop(0, tiles, rest, 0)


STEP = 2


def sweep_tile(t, at_column, scale, columns, sums, words, rows_for, steps):
    scale = jnp.broadcast_to(scale, (8, LANES))

    def block(nb, carry):
        at = pl.ds(pl.multiple_of(nb * 64, 64), 64)
        x = columns[at_column, 0, at, :].reshape(8, 8, LANES)
        y = columns[at_column, 1, at, :].reshape(8, 8, LANES)

        def some(p, sums_now):
            den, num = sums_now
            for k in range(STEP):
                word = words[t, STEP * p + k]
                e = (word >> 11) & 15
                u, v, c, d = rows_for(word)
                u = jnp.broadcast_to(u, (8, LANES)) + steps[e]
                v = jnp.broadcast_to(v, (8, LANES)) + steps[9 + e]
                c = jnp.broadcast_to(c, (8, LANES))
                d = jnp.broadcast_to(d, (8, LANES))
                fade = jnp.exp2(-scale * (u * u + v * v))
                w = jnp.exp2(x * u + y * v)
                den = den + w * (c * c * fade)
                num = num + w * (d * fade)
            return den, num

        zero = jnp.zeros((8, 8, LANES), F32)
        steps_used = (words[t, USED] + STEP - 1) // STEP
        den, num = lax.fori_loop(0, steps_used, some, (zero, zero))
        sums[t, at, 0:LANES] = den.reshape(64, LANES)
        sums[t, at, LANES : 2 * LANES] = num.reshape(64, LANES)
        return carry

    lax.fori_loop(0, blocks_in(words[t, LIVE]), block, 0)


def set_steps(steps):
    for e, (a, b) in enumerate(NEAR):
        steps[e] = jnp.float32(a)
        steps[9 + e] = jnp.float32(b)


def first_lists(near_info, edge_info, rows):
    me = lax.axis_index("tile")
    odd = me & 1
    first = (me >> 1) * 8
    near_live, edge_live = column_of(near_info, COUNT), column_of(edge_info, COUNT)
    step = lax.broadcasted_iota(I32, (8, LANES), 0)
    on_map = [(first > 0).astype(F32), (first + 8 < rows).astype(F32)]
    lines = []
    for u in range(5):
        if u < 2:
            away = 1 - u
            parts = [edge_live[i : i + n] for i, n in ((16 + 2 * away, 1), (8 * away, 8), (17 + 2 * away, 1))]
        else:
            parts = [near_live[10 * (u - 2) + i : 10 * (u - 2) + i + n] for i, n in ((0, 1), (1, 8), (9, 1))]
        lines.append(jnp.concatenate([parts[0] * on_map[0], parts[1], parts[2] * on_map[1]], axis=0))

    def source(u, b):
        if u >= 2:
            return (u - 2) * 10 + 1 + b + step
        start = NEAR_ROWS + 8 * (1 - u)
        at = start + b + step
        if b == 0:
            return at
        corner = NEAR_ROWS + 16 + 2 * (1 - u) + (b + 1) // 2
        return jnp.where(step == (0 if b < 0 else 7), corner, at)

    result = []
    for j, info in enumerate((edge_info[0:8], near_info[1:9], near_info[11:19])):
        entries = []
        for du in (-1, 0, 1):
            for b in (-1, 0, 1):
                here, there = 3 * (du + 1) + b + 1, 3 * (1 - du) + b + 1
                e = jnp.where(odd == 1, there, here)
                chunks = chunks_in(lines[j + 1 + du][1 + b : 9 + b])
                if here != 4:
                    taken = jnp.where(odd == 1, column_of(info, REACH + there), column_of(info, REACH + here))
                    chunks = jnp.where(taken > 0.5, chunks, 0)
                entries.append((source(j + 1 + du, b) + (e << 11), chunks))
        result.append(list_chunks(entries, column_of(info, COUNT), SPARE))
    return jnp.concatenate(result, axis=0)


def first_kernel(
    near, near_columns, border, out,
    table, own, east, north, low, high, columns, sums, listed,
    words, steps, sem, word_sem,
):
    rows = lax.axis_size("tile") * SLOTS // TX
    near_at, edge_at = pl.ds(0, NEAR_ROWS), pl.ds(NEAR_ROWS, EDGE_ROWS)
    copies = [pltpu.make_async_copy(near.at[pl.ds(0, 6)], table.at[:, :, near_at], sem)]
    for f, field in enumerate((EAST, NORTH, ONE, PART)):
        held = border.at[:, pl.ds(f * 24, 24)]
        copies.append(pltpu.make_async_copy(held, table.at[field, :, edge_at], sem))
    for f, field in enumerate((TWO, PRICE)):
        held = border.at[:, pl.ds(120 + 8 * f, 8)]
        copies.append(pltpu.make_async_copy(held, table.at[field, :, pl.ds(NEAR_ROWS, 8)], sem))
    for copy in copies:
        copy.start()
    near_info, edge_info = near[INFO, 0], border[0, 4 * 24 : 5 * 24, :]
    listed[...] = first_lists(near_info, edge_info, rows)
    word_copy = pltpu.make_async_copy(listed, words, word_sem)
    word_copy.start()
    set_steps(steps)
    tiles = 24
    info = jnp.concatenate([edge_info[0:8], near_info[1:9], near_info[11:19]], axis=0)
    scales = scale_of(info[:, WIDTH : WIDTH + 1])
    counts = column_of(info, COUNT)
    for copy in copies:
        copy.wait()

    def of_targets(field):
        parts = [table[field, :, 32:40, :], table[field, :, 1:9, :], table[field, :, 11:19, :]]
        return jnp.concatenate(parts, axis=1)

    present = records(tiles) < counts[None]
    scale_rows = scales[None]
    own[...] = scales
    x, y = of_targets(EAST), of_targets(NORTH)
    east[...] = columns_of(2.0 * scale_rows[:, 0:8] * x[:, 0:8])
    north[...] = columns_of(2.0 * scale_rows[:, 0:8] * y[:, 0:8])

    def number_of(t):
        return words[t, LIVE]

    spread_columns(8, number_of, east, north, columns, word_copy.wait)

    def rows_for(word):
        at, h = pl.ds(word & 1023, 1), (word >> 10) & 1
        return [table[field, h, at, :] for field in (EAST, NORTH, ONE, PART)]

    def each(t, carry, held, skip):
        sweep_tile(t, t - skip, own[pl.ds(t, 1), :], held, sums, words, rows_for, steps)
        return carry

    lax.fori_loop(0, 8, lambda t, c: each(t, c, columns, 0), 0)
    lax.fori_loop(8, tiles, lambda t, c: each(t, c, near_columns, 8), 0)
    collect_sums(tiles, number_of, sums, low, high)
    shrink = jnp.exp2(-scale_rows * (x * x + y * y))
    den, num = rows_of(low[...], high[...], tiles)
    inv = 1.0 / (1.0 + shrink * den)
    beta = jnp.where(present, shrink * num * inv, 0.0)
    one, two = of_targets(ONE), of_targets(TWO)
    out[:, 0:24, :] = two * (of_targets(PRICE) - one * beta)
    out[:, 24:40, :] = beta[:, 8:24]
    out[:, 40:56, :] = jnp.where(present, one * one * inv, 0.0)[:, 8:24]
    out[:, 56:64, :] = two[:, 0:8]
    out[:, 64:72, :] = x[:, 0:8]
    out[:, 72:80, :] = y[:, 0:8]
    out[:, 80:88, :] = jnp.broadcast_to(counts[0:8][None], (2, 8, LANES))


def second_lists(mine, same, other, same_b, other_b):
    half = same.shape[0]
    cells = 2 * half * SLOTS
    rows = cells // TX
    edge = 2 * half * 8
    padded = -(-edge // LANES) * LANES
    me = lax.axis_index("tile")
    info = jnp.concatenate([x[:, INFO, 0].reshape(half * SLOTS, LANES) for x in (same, other)], axis=0)
    keys = [info[k : k + LANES].T[LABEL : LABEL + 1] + rows for k in range(0, cells, LANES)]
    at = lax.broadcasted_iota(I32, (1, padded), 1)
    n = at >> 3
    device = (((n & (half - 1)) << 1) | (n >= half).astype(I32)) ^ me
    row = (device >> 1) * 8 + (at & 7)
    key = jnp.where((device & 1) == 1, (TX + 1) * rows + row, row)
    keys.append(jnp.where(at < edge, key, -1).astype(F32))
    keys = jnp.concatenate(keys, axis=1)
    total = cells + padded
    edge_live = [x[k, 0, 80:88, :] for x in (same_b, other_b) for k in range(half)]
    if padded > edge:
        edge_live.append(jnp.zeros((padded - edge, LANES), F32))
    live = jnp.concatenate([column_of(info, COUNT), *edge_live], axis=0)
    index = lax.broadcasted_iota(I32, (total, LANES), 0)
    cell = column_of(mine, LABEL).astype(I32)
    column, across = split(cell, rows)
    hot = []
    for a, b in NEAR:
        row = across + b
        wanted = jnp.where((row >= 0) & (row < rows), (column + a + 1) * rows + row, -2).astype(F32)
        parts = [keys[:, k : k + LANES] == wanted for k in range(0, total, LANES)]
        hot.append(jnp.concatenate([p.astype(F32) for p in parts], axis=1))
    hot = jnp.concatenate(hot, axis=0).astype(jnp.bfloat16)

    def look_up(values):
        return jnp.dot(hot, values.astype(F32).astype(jnp.bfloat16), preferred_element_type=F32)

    blocks, slots = look_up(index >> 4), look_up(index & 15)
    lives = look_up(live)
    tiles = mine.shape[0]
    entries = []
    for e, (a, b) in enumerate(NEAR):
        at = slice(e * tiles, (e + 1) * tiles)
        chunks = chunks_in(lives[at])
        if e != 4:
            chunks = jnp.where(column_of(mine, REACH + e) > 0.5, chunks, 0)
        source = blocks[at].astype(I32) * SLOTS + slots[at].astype(I32)
        n, spot = place_of(column + a, across + b, me, half)
        entries.append((source + (e << 11) + (n << 15) + (spot << 20), chunks))
    spare = cells + edge + (88 << 20)
    words = list_chunks(entries, column_of(mine, COUNT), spare)
    lane = lax.broadcasted_iota(I32, words.shape, 1)
    n, spot = place_of(column, across, me, half)
    words = jnp.where(lane == HOLDER, n, words)
    return jnp.where(lane == HELD_AT, spot, words)


def second_kernel(
    own_block, mine, columns, same, other, same_b, other_b,
    betas, hats, residual,
    table, results, own, scales, low, high, sums, listed,
    words, steps, sem, word_sem,
):
    copies = fetch(same, other, table, 3, sem)
    half, _, _, tiles, _ = same.shape
    blocks = 2 * half
    for side, held in enumerate((same_b, other_b)):
        at = pl.ds(side * half, half)
        copies.append(pltpu.make_async_copy(held, results.at[at, :, pl.ds(0, 88)], sem))
    for copy in copies:
        copy.start()
    listed[...] = second_lists(mine, same, other, same_b, other_b)
    word_copy = pltpu.make_async_copy(listed, words, word_sem)
    word_copy.start()
    set_steps(steps)
    scales[...] = scale_of(mine[:, WIDTH : WIDTH + 1])
    present = records(tiles) < column_of(mine, COUNT)[None]
    scale_rows = scales[...][None]
    x, y = own_block[EAST], own_block[NORTH]

    def number_of(t):
        return words[t, LIVE]

    for n in range(2 * half):
        held = (same_b if n < half else other_b).at[n % half]
        for field in range(3):
            table[blocks + n // 2, field, :, n % 2 * 8 : n % 2 * 8 + 8, :] = held[
                :, 56 + 8 * field : 64 + 8 * field, :
            ]
    for field in range(3):
        table[blocks + half, field, :, 0:8, :] = jnp.zeros((2, 8, LANES), F32)
    results[0, :, 88:96, :] = jnp.zeros((2, 8, LANES), F32)
    for copy in copies:
        copy.wait()
    word_copy.wait()

    def rows_for(word):
        n, slot = split(word & 1023, SLOTS)
        h = (word >> 10) & 1
        held = [table[n, field, h, pl.ds(slot, 1), :] for field in (EAST, NORTH, TWO)]
        return [*held, results[(word >> 15) & 31, h, pl.ds(word >> 20, 1), :]]

    def each(t, carry):
        n, at = words[t, HOLDER], words[t, HELD_AT]
        own[0, :, pl.ds(t, 1), :] = results[n, :, pl.ds(16 + at, 1), :]
        own[1, :, pl.ds(t, 1), :] = results[n, :, pl.ds(32 + at, 1), :]
        sweep_tile(t, t, scales[pl.ds(t, 1), :], columns, sums, words, rows_for, steps)
        return carry

    lax.fori_loop(0, tiles, each, 0)
    collect_sums(tiles, number_of, sums, low, high)
    shrink = jnp.exp2(-scale_rows * (x * x + y * y))
    den, num = rows_of(low[...], high[...], tiles)
    inv = 1.0 / (1.0 + shrink * den)
    beta_two = jnp.where(present, shrink * num * inv, 0.0)
    beta_one = own[0]
    one, two = own_block[ONE], own_block[TWO]
    left = jnp.where(present, own_block[PRICE] - one * beta_one - two * beta_two, 0.0)
    hat_two = jnp.where(present, two * two * inv, 0.0)
    for t in range(tiles):
        for h in range(2):
            at = slice(t * TILE + h * LANES, t * TILE + (h + 1) * LANES)
            betas[0:1, at] = beta_one[h, t : t + 1]
            betas[1:2, at] = beta_two[h, t : t + 1]
            hats[0:1, at] = own[1, h, t : t + 1, :]
            hats[1:2, at] = hat_two[h, t : t + 1]
            residual[0:1, at] = left[h, t : t + 1]


def swap(x, k):
    count = lax.axis_size("tile")
    return lax.ppermute(x, "tile", [(i, i ^ k) for i in range(count)])


def spread(block):
    count = lax.axis_size("tile")
    same = jnp.stack([block] + [swap(block, k) for k in range(2, count, 2)])
    return same, swap(same, 1)


def body(offsets, design, target, beta_second, counts, kernel_width, reach, assignment):
    tiles = counts.shape[0]
    count = lax.axis_size("tile")
    regions = lax.axis_size("region")
    cells = tiles * count
    limit = pltpu.CompilerParams(vmem_limit_bytes=24 * 1024 * 1024)
    price = target.reshape(1, -1)
    wide = tiles * TILE
    given = (
        offsets, design, price, beta_second.reshape(1, -1),
        counts, kernel_width, reach.transpose(2, 0, 1), assignment,
    )
    block, mine = pl.pallas_call(
        prepare_kernel,
        out_shape=(
            pltpu.VMEM((7, 2, tiles, LANES), F32),
            pltpu.VMEM((tiles, LANES), F32),
        ),
        in_specs=[pl.BlockSpec(memory_space=pltpu.HBM)] * 8,
        out_specs=(VMEM, VMEM),
        scratch_shapes=[pltpu.VMEM((2, wide), F32)] * 2
        + [pltpu.VMEM((1, wide), F32)] * 2
        + [
            pltpu.SMEM((tiles,), I32),
            pltpu.SMEM((2, tiles), I32),
            pltpu.SMEM((9, 2, tiles), I32),
            pltpu.SMEM((1, tiles), I32),
            pltpu.SemaphoreType.DMA,
        ],
        compiler_params=limit,
    )(*[pltpu.with_memory_space_constraint(x, pltpu.HBM) for x in given])
    square = pltpu.VMEM((LANES, LANES), F32)
    dma = pltpu.SemaphoreType.DMA
    own_columns = pl.pallas_call(
        own_columns_kernel,
        out_shape=pltpu.VMEM((tiles, 2, TILE, LANES), F32),
        in_specs=[VMEM, VMEM],
        out_specs=VMEM,
        scratch_shapes=[square, square, pltpu.SMEM((tiles, LANES), F32), dma],
        compiler_params=limit,
        cost_estimate=pl.CostEstimate(flops=4000000, bytes_accessed=4000000, transcendentals=0),
    )(block, mine)
    same, other = spread(block)
    edge, near = pl.pallas_call(
        border_kernel,
        out_shape=(
            jax.ShapeDtypeStruct((2, 136, LANES), F32),
            pltpu.VMEM((7, 2, NEAR_ROWS, LANES), F32),
        ),
        in_specs=[VMEM, VMEM],
        out_specs=(VMEM, VMEM),
        compiler_params=limit,
    )(same, other)
    near_columns = pl.pallas_call(
        near_kernel,
        out_shape=pltpu.VMEM((16, 2, TILE, LANES), F32),
        in_specs=[VMEM],
        out_specs=VMEM,
        scratch_shapes=[square, square, pltpu.SMEM((NEAR_ROWS, LANES), F32), dma],
        compiler_params=limit,
        cost_estimate=pl.CostEstimate(flops=4000000, bytes_accessed=4000000, transcendentals=0),
    )(near)
    moves = []
    for r in range(regions):
        for t in range(count):
            to = r + 1 - 2 * (t % 2)
            if 0 <= to < regions:
                moves.append((r * count + t, to * count + t))
    border = lax.ppermute(edge, ("region", "tile"), moves)
    first = pl.pallas_call(
        first_kernel,
        out_shape=jax.ShapeDtypeStruct((2, 88, LANES), F32),
        in_specs=[VMEM, VMEM, VMEM],
        out_specs=VMEM,
        scratch_shapes=[
            pltpu.VMEM((6, 2, NEAR_ROWS + EDGE_ROWS, LANES), F32),
            pltpu.VMEM((24, LANES), F32),
            square,
            square,
            square,
            square,
            pltpu.VMEM((8, 2, TILE, LANES), F32),
            pltpu.VMEM((24, TILE, 2 * LANES), F32),
            pltpu.VMEM((24, LANES), I32),
            pltpu.SMEM((24, LANES), I32),
            pltpu.SMEM((18,), F32),
            dma,
            dma,
        ],
        compiler_params=limit,
    )(near, near_columns, border)
    same_b, other_b = spread(first)
    betas, hats, residual = pl.pallas_call(
        second_kernel,
        out_shape=(
            jax.ShapeDtypeStruct((2, wide), F32),
            jax.ShapeDtypeStruct((2, wide), F32),
            jax.ShapeDtypeStruct((1, wide), F32),
        ),
        in_specs=[VMEM] * 7,
        out_specs=(VMEM, VMEM, VMEM),
        scratch_shapes=[
            pltpu.VMEM((count + count // 2 + 1, 3, 2, tiles, LANES), F32),
            pltpu.VMEM((count, 2, 96, LANES), F32),
            pltpu.VMEM((2, 2, tiles, LANES), F32),
            pltpu.VMEM((tiles, LANES), F32),
            square,
            square,
            pltpu.VMEM((tiles, TILE, 2 * LANES), F32),
            pltpu.VMEM((tiles, LANES), I32),
            pltpu.SMEM((tiles, LANES), I32),
            pltpu.SMEM((18,), F32),
            dma,
            dma,
        ],
        compiler_params=limit,
    )(block, mine, own_columns, same, other, same_b, other_b)
    return (betas, hats, residual.reshape(-1))


def solution(mesh):
    in_specs = (
        P(None, ("region", "tile")),
        P(None, ("region", "tile")),
        P(("region", "tile")),
        P(("region", "tile")),
        P(("region", "tile")),
        P(None, ("region", "tile")),
        P(None, ("region", "tile"), None),
        P("region", "tile"),
    )
    out_specs = (P(None, ("region", "tile")), P(None, ("region", "tile")), P(("region", "tile")))
    return jax.shard_map(body, mesh=mesh, in_specs=in_specs, out_specs=out_specs, check_vma=False)
```

```python
import functools

import jax
import jax.numpy as jnp
from jax import lax
from jax.experimental import pallas as pl
from jax.experimental.pallas import tpu as pltpu
from jax.sharding import PartitionSpec as P

TILE = 256
TX = 4
LANES = 128
TWO, EAST, NORTH, ONE, PART, PRICE, INFO = range(7)
SLOTS = 16
BASE = 32.0 * 1.4426950408889634
LABEL, COUNT, WIDTH, REACH = 0, 1, 2, 3
NEAR = [(a, b) for a in (-1, 0, 1) for b in (-1, 0, 1)]
F32, I32 = jnp.float32, jnp.int32
ANY = pl.BlockSpec(memory_space=pl.ANY)
SMEM = pl.BlockSpec(memory_space=pltpu.SMEM)
VMEM = pl.BlockSpec(memory_space=pltpu.VMEM)


def prepare_kernel(*refs):
    given, (out, mine), held, sem = refs[:8], refs[8:10], refs[10:18], refs[18]
    copies = [pltpu.make_async_copy(a, b, sem) for a, b in zip(given, held)]
    for copy in copies:
        copy.start()
    for copy in copies:
        copy.wait()
    off, des, tgt, sec, counts, widths, reach, cells = held
    lane = lax.broadcasted_iota(I32, (1, LANES), 1)
    for t in range(counts.shape[0]):
        row = jnp.zeros((1, LANES), F32)
        facts = [cells[0, t], counts[t], widths[0, t]] + [reach[e, 0, t] for e in range(9)]
        for k, fact in enumerate(facts):
            row = jnp.where(lane == k, fact.astype(F32), row)
        out[INFO, 0, t : t + 1, :] = row
        for k, value in enumerate([widths[1, t]] + [reach[e, 1, t] for e in range(9)]):
            row = jnp.where(lane == WIDTH + k, value.astype(F32), row)
        mine[t : t + 1, :] = row
        for h in range(2):
            at = slice(t * TILE + h * LANES, t * TILE + (h + 1) * LANES)
            live = lane + h * LANES < counts[t]
            one = jnp.where(live, des[0:1, at], 0.0)
            two = jnp.where(live, des[1:2, at], 0.0)
            price = tgt[0:1, at]
            out[EAST, h, t : t + 1, :] = off[0:1, at] - 0.5
            out[NORTH, h, t : t + 1, :] = off[1:2, at] - 0.5
            out[ONE, h, t : t + 1, :] = one
            out[PART, h, t : t + 1, :] = one * (price - two * sec[0:1, at])
            out[TWO, h, t : t + 1, :] = two
            out[PRICE, h, t : t + 1, :] = price
    out[INFO, 1] = jnp.zeros_like(out[INFO, 1])


def split(number, size):
    return number >> (size.bit_length() - 1), number & (size - 1)


def fetch(same, other, table, fields, sem):
    half = same.shape[0]
    return [
        pltpu.make_async_copy(
            held.at[:, pl.ds(0, fields)], table.at[pl.ds(side * half, half), pl.ds(0, fields)], sem
        )
        for side, held in enumerate((same, other))
    ]


ORDER = [(0, r) for r in range(1, 9)] + [(1, r) for r in range(1, 9)]
ORDER += [(0, 0), (0, 9), (1, 0), (1, 9)]
NEAR_ROWS, EDGE_ROWS, SPARE = 32, 24, 30


def wanted_cells(rows):
    me = lax.axis_index("tile")
    odd = me & 1
    first = (me >> 1) * 8
    i = lax.broadcasted_iota(I32, (64, LANES), 0)
    u = (i >= 10).astype(I32) + (i >= 20).astype(I32)
    j = i - NEAR_ROWS
    away = jnp.where(j < 16, j >> 3, (j >> 1) & 1)
    own = i < NEAR_ROWS
    r = jnp.where(own, i - 10 * u, jnp.where(j < 16, (j & 7) + 1, (j & 1) * 9))
    low = jnp.where(own, u, TX - 1 - away)
    column = jnp.where(odd == 1, TX - 1 - low, low)
    cell = column * rows + jnp.clip(first + r - 1, 0, rows - 1)
    none = (i == SPARE) | (i == SPARE + 1) | (j >= len(ORDER))
    return jnp.where(none, -1, cell).astype(F32)


def border_kernel(same, other, out, near):
    half = same.shape[0]
    cells = 2 * half * SLOTS

    def plane(field, h):
        parts = [x[:, field, h].reshape(half * SLOTS, LANES) for x in (same, other)]
        return jnp.concatenate(parts, axis=0)

    info = plane(INFO, 0)
    wanted = wanted_cells(cells // TX)
    hot = []
    for k in range(0, cells, LANES):
        labels = info[k : k + LANES].T[LABEL : LABEL + 1]
        hot.append((jnp.broadcast_to(labels, wanted.shape) == wanted).astype(F32))
    hot = jnp.concatenate(hot, axis=1).astype(jnp.bfloat16)

    def pick(values, pieces):
        total = jnp.zeros((64, LANES), F32)
        for _ in range(pieces):
            piece = values.astype(jnp.bfloat16)
            values = values - piece.astype(F32)
            total = total + jnp.dot(hot, piece, preferred_element_type=F32)
        return total

    for field in (EAST, NORTH, ONE, PART, INFO, TWO, PRICE):
        for h in range(2):
            if field != INFO:
                got = pick(plane(field, h), 3)
            elif h == 0:
                got = pick(info, 1)
            near[field, h] = got[0:NEAR_ROWS]
            edge = got[NEAR_ROWS : NEAR_ROWS + EDGE_ROWS]
            if field in (TWO, PRICE):
                f = (TWO, PRICE).index(field)
                out[h, 120 + 8 * f : 128 + 8 * f, :] = edge[0:8]
            else:
                f = (EAST, NORTH, ONE, PART, INFO).index(field)
                out[h, f * 24 : f * 24 + 24, :] = edge


def targets_of(near, field):
    return jnp.concatenate([near[field, :, 1:9, :], near[field, :, 11:19, :]], axis=1)


def near_kernel(near, columns, east, north, facts, sem):
    copy = pltpu.make_async_copy(near.at[INFO, 0], facts, sem)
    copy.start()
    info = targets_of(near, INFO)[0]
    scale = scale_of(info[:, WIDTH : WIDTH + 1])[None]
    east[...] = columns_of(2.0 * scale * targets_of(near, EAST))
    north[...] = columns_of(2.0 * scale * targets_of(near, NORTH))

    def number_of(t):
        return facts[(t >> 3) * 10 + (t & 7) + 1, COUNT].astype(I32)

    spread_columns(16, number_of, east, north, columns, copy.wait)


USED, LIVE, HOLDER, HELD_AT = 100, 101, 102, 103


def column_of(info, k):
    return jnp.broadcast_to(info[:, k : k + 1], (info.shape[0], LANES))


def halves_in(number):
    return sum((number > 64.0 * q).astype(I32) for q in range(4))


def list_halves(entries, number, spare, other, half_at, spare_given=0, given_at=(0, 0)):
    lane = lax.broadcasted_iota(I32, number.shape, 1)
    rows = jnp.full(number.shape, spare, I32)
    givens = jnp.full(number.shape, spare_given, I32)
    east, north = jnp.zeros(number.shape, F32), jnp.zeros(number.shape, F32)
    used = jnp.zeros(number.shape, I32)
    for row, given, a, b, halves in entries:
        moved = used & 1
        row = row + moved * other
        given = given + moved * given_at[0]
        for q in range(4):
            here = (lane == used + q) & (halves > q)
            rows = jnp.where(here, row + (q >> 1) * half_at, rows)
            givens = jnp.where(here, given + (q >> 1) * given_at[1], givens)
        here = (lane >= used) & (lane < used + halves)
        east = jnp.where(here, a, east)
        north = jnp.where(here, b, north)
        used = used + halves
    rows = jnp.where(lane == USED, used, rows)
    rows = jnp.where(lane == LIVE, number.astype(I32), rows)
    return rows, givens, east, north


def turned(values):
    flat = pltpu.roll(values.reshape(-1, LANES), LANES // 2, 1)
    return flat.reshape(values.shape)


def place_of(column, row, me, half):
    low = (column < TX // 2).astype(I32)
    depth = jnp.where(low == 1, column + 1, TX - column)
    k = ((row >> 3) * 2 + 1 - low) ^ me
    return (k & 1) * half + (k >> 1), depth * 8 + (row & 7)


def scale_of(width):
    return jnp.broadcast_to(BASE / (width * width), (width.shape[0], LANES))


def own_columns_kernel(block, mine, columns, east, north, facts, sem):
    copy = pltpu.make_async_copy(mine, facts, sem)
    copy.start()
    scale = scale_of(mine[:, WIDTH : WIDTH + 1])[None]
    east[...] = columns_of(2.0 * scale * block[EAST])
    north[...] = columns_of(2.0 * scale * block[NORTH])

    def number_of(t):
        return facts[t, COUNT].astype(I32)

    spread_columns(block.shape[2], number_of, east, north, columns, copy.wait)


def records(tiles):
    shape = (2, tiles, LANES)
    number = lax.broadcasted_iota(I32, shape, 2) + LANES * lax.broadcasted_iota(I32, shape, 0)
    return number.astype(F32)


def columns_of(rows):
    pad = jnp.zeros((64 - rows.shape[1], LANES), F32)
    return jnp.concatenate([rows[0], pad, rows[1], pad], axis=0).T


def rows_of(low, high, tiles):
    low, high = low.T, high.T
    return [jnp.stack([low[k : k + tiles], high[k : k + tiles]]) for k in (0, 64)]


def spread_columns(tiles, number_of, east, north, columns, ready=None):
    def lay(t, nb, values):
        i = (nb >> 1) * 64 + t
        for k, value in enumerate(values):
            wide = jnp.broadcast_to(value[:, i : i + 1], (64, LANES))
            columns[t, k, nb * 64 : nb * 64 + 64, :] = wide

    low = (east[0:64, :], north[0:64, :])
    for t in range(tiles):
        lay(t, 0, low)
    if ready is not None:
        ready()
    for t in range(tiles):
        number = number_of(t)

        @pl.when(number > 64)
        def _():
            lay(t, 1, (east[64:128, :], north[64:128, :]))

        @pl.when(number > 128)
        def _():
            lay(t, 2, (east[0:64, :], north[0:64, :]))
            lay(t, 3, (east[64:128, :], north[64:128, :]))


def collect_sums(tiles, number_of, sums, low_ref, high_ref):
    split_at = lax.broadcasted_iota(I32, (2 * LANES, LANES), 0) // LANES
    sides = lax.broadcasted_iota(I32, (2 * LANES, LANES), 1) // 64
    ones = (split_at == sides).astype(F32).astype(jnp.bfloat16)
    lane = lax.broadcasted_iota(I32, (64, LANES), 1) & 63

    def total(values):
        high = values.astype(jnp.bfloat16)
        low = (values - high.astype(F32)).astype(jnp.bfloat16)
        return jnp.dot(high, ones, preferred_element_type=F32) + jnp.dot(
            low, ones, preferred_element_type=F32
        )

    for nb in range(2):
        result = jnp.zeros((64, LANES), F32)
        for t in range(tiles):
            x = total(sums[t, nb * 64 : nb * 64 + 64, :])
            result = jnp.where(lane == t, x, result)
        low_ref[nb * 64 : nb * 64 + 64, :] = result
    high_ref[...] = jnp.zeros_like(high_ref)

    def rest(t, carry):
        @pl.when(number_of(t) > 128)
        def _():
            x = total(sums[t, 128:256, :])
            mine = lax.broadcasted_iota(I32, (128, LANES), 1) & 63
            high_ref[...] = jnp.where(mine == t, x, high_ref[...])

        return carry

    lax.fori_loop(0, tiles, rest, 0)


def sweep_tile(t, at_column, scale, columns, sums, words, steps, rows_for):
    scale = jnp.broadcast_to(scale, (8, LANES))
    left = lax.broadcasted_iota(I32, (8, LANES), 1) < LANES // 2

    def chunk(i):
        sides = []
        for k in range(2):
            u, v, c, d = [jnp.broadcast_to(row, (8, LANES)) for row in rows_for(t, i + k)]
            sides.append((u + steps[0, t, i + k], v + steps[1, t, i + k], c, d))
        u, v, c, d = [jnp.where(left, *pair) for pair in zip(*sides)]
        fade = jnp.exp2(-scale * (u * u + v * v))
        return u, v, c * c * fade, d * fade

    def block(nb, size, step):
        at = pl.ds(pl.multiple_of(nb * 64, 64), size)
        x = columns[at_column, 0, at, :].reshape(size // 8, 8, LANES)
        y = columns[at_column, 1, at, :].reshape(size // 8, 8, LANES)

        def some(p, sums_now):
            den, num = sums_now
            for k in range(step):
                u, v, c, d = chunk(2 * (step * p + k))
                w = jnp.exp2(x * u + y * v)
                den = den + w * c
                num = num + w * d
            return den, num

        zero = jnp.zeros((size // 8, 8, LANES), F32)
        trips = (words[0, t, USED] + 2 * step - 1) // (2 * step)
        den, num = lax.fori_loop(0, trips, some, (zero, zero))
        sums[t, at, 0:LANES] = den.reshape(size, LANES)
        sums[t, at, LANES : 2 * LANES] = num.reshape(size, LANES)

    number = words[0, t, LIVE]
    whole = (number + 31) >> 6

    def full(nb, carry):
        block(nb, 64, 2)
        return carry

    lax.fori_loop(0, whole, full, 0)

    @pl.when(number > whole * 64)
    def _():
        block(whole, 32, 4)


def first_lists(near_info, edge_info, rows):
    me = lax.axis_index("tile")
    odd = me & 1
    first = (me >> 1) * 8
    near_live, edge_live = column_of(near_info, COUNT), column_of(edge_info, COUNT)
    step = lax.broadcasted_iota(I32, (8, LANES), 0)
    on_map = [(first > 0).astype(F32), (first + 8 < rows).astype(F32)]
    lines = []
    for u in range(5):
        if u < 2:
            away = 1 - u
            parts = [edge_live[i : i + n] for i, n in ((16 + 2 * away, 1), (8 * away, 8), (17 + 2 * away, 1))]
        else:
            parts = [near_live[10 * (u - 2) + i : 10 * (u - 2) + i + n] for i, n in ((0, 1), (1, 8), (9, 1))]
        lines.append(jnp.concatenate([parts[0] * on_map[0], parts[1], parts[2] * on_map[1]], axis=0))

    def source(u, b):
        if u >= 2:
            return (u - 2) * 10 + 1 + b + step
        start = NEAR_ROWS + 8 * (1 - u)
        at = start + b + step
        if b == 0:
            return at
        corner = NEAR_ROWS + 16 + 2 * (1 - u) + (b + 1) // 2
        return jnp.where(step == (0 if b < 0 else 7), corner, at)

    result = []
    for j, info in enumerate((edge_info[0:8], near_info[1:9], near_info[11:19])):
        entries = []
        for du in (-1, 0, 1):
            for b in (-1, 0, 1):
                here, there = 3 * (du + 1) + b + 1, 3 * (1 - du) + b + 1
                a = jnp.where(odd == 1, -du, du).astype(F32)
                chunks = halves_in(lines[j + 1 + du][1 + b : 9 + b])
                if here != 4:
                    taken = jnp.where(odd == 1, column_of(info, REACH + there), column_of(info, REACH + here))
                    chunks = jnp.where(taken > 0.5, chunks, 0)
                entries.append((source(j + 1 + du, b), 0, a, jnp.float32(b), chunks))
        plane = NEAR_ROWS + EDGE_ROWS
        result.append(list_halves(entries, column_of(info, COUNT), SPARE, 10 * plane, plane))
    return [jnp.concatenate(parts, axis=0) for parts in zip(*result)]


def first_kernel(
    near, near_columns, border, out,
    table, own, east, north, low, high, columns, sums, listed, stepped,
    words, steps, sem, word_sem,
):
    rows = lax.axis_size("tile") * SLOTS // TX
    near_at, edge_at = pl.ds(0, NEAR_ROWS), pl.ds(NEAR_ROWS, EDGE_ROWS)
    copies = [
        pltpu.make_async_copy(near.at[pl.ds(0, 6)], table.at[pl.ds(0, 6), :, near_at], sem)
    ]
    for f, field in enumerate((EAST, NORTH, ONE, PART)):
        held = border.at[:, pl.ds(f * 24, 24)]
        copies.append(pltpu.make_async_copy(held, table.at[field, :, edge_at], sem))
    for f, field in enumerate((TWO, PRICE)):
        held = border.at[:, pl.ds(120 + 8 * f, 8)]
        copies.append(pltpu.make_async_copy(held, table.at[field, :, pl.ds(NEAR_ROWS, 8)], sem))
    for copy in copies:
        copy.start()
    near_info, edge_info = near[INFO, 0], border[0, 4 * 24 : 5 * 24, :]
    listed[0], _, stepped[0], stepped[1] = first_lists(near_info, edge_info, rows)
    word_copies = [
        pltpu.make_async_copy(listed, words, word_sem),
        pltpu.make_async_copy(stepped, steps, word_sem),
    ]
    for copy in word_copies:
        copy.start()
    tiles = 24
    info = jnp.concatenate([edge_info[0:8], near_info[1:9], near_info[11:19]], axis=0)
    scales = scale_of(info[:, WIDTH : WIDTH + 1])
    counts = column_of(info, COUNT)
    for copy in copies:
        copy.wait()

    def of_targets(field):
        parts = [table[field, :, 32:40, :], table[field, :, 1:9, :], table[field, :, 11:19, :]]
        return jnp.concatenate(parts, axis=1)

    present = records(tiles) < counts[None]
    scale_rows = scales[None]
    own[...] = scales
    x, y = of_targets(EAST), of_targets(NORTH)
    east[...] = columns_of(2.0 * scale_rows[:, 0:8] * x[:, 0:8])
    north[...] = columns_of(2.0 * scale_rows[:, 0:8] * y[:, 0:8])

    def number_of(t):
        return words[0, t, LIVE]

    def ready():
        for copy in word_copies:
            copy.wait()

    spread_columns(8, number_of, east, north, columns, ready)

    table[6:10] = turned(table[EAST : PART + 1])

    plane = 2 * (NEAR_ROWS + EDGE_ROWS)
    flat = table.reshape(10 * plane, LANES)

    def rows_for(t, i):
        row = words[0, t, i]
        return [flat[pl.ds(row + field * plane, 1), :] for field in (EAST, NORTH, ONE, PART)]

    def each(t, carry, held, skip):
        sweep_tile(t, t - skip, own[pl.ds(t, 1), :], held, sums, words, steps, rows_for)
        return carry

    lax.fori_loop(0, 8, lambda t, c: each(t, c, columns, 0), 0)
    lax.fori_loop(8, tiles, lambda t, c: each(t, c, near_columns, 8), 0)
    collect_sums(tiles, number_of, sums, low, high)
    shrink = jnp.exp2(-scale_rows * (x * x + y * y))
    den, num = rows_of(low[...], high[...], tiles)
    inv = 1.0 / (1.0 + shrink * den)
    beta = jnp.where(present, shrink * num * inv, 0.0)
    one, two = of_targets(ONE), of_targets(TWO)
    out[:, 0:24, :] = two * (of_targets(PRICE) - one * beta)
    out[:, 24:40, :] = beta[:, 8:24]
    out[:, 40:56, :] = jnp.where(present, one * one * inv, 0.0)[:, 8:24]
    out[:, 56:64, :] = two[:, 0:8]
    out[:, 64:72, :] = x[:, 0:8]
    out[:, 72:80, :] = y[:, 0:8]
    out[:, 80:88, :] = jnp.broadcast_to(counts[0:8][None], (2, 8, LANES))


def second_lists(mine, same, other, same_b, other_b):
    half = same.shape[0]
    cells = 2 * half * SLOTS
    rows = cells // TX
    edge = 2 * half * 8
    padded = -(-edge // LANES) * LANES
    me = lax.axis_index("tile")
    info = jnp.concatenate([x[:, INFO, 0].reshape(half * SLOTS, LANES) for x in (same, other)], axis=0)
    keys = [info[k : k + LANES].T[LABEL : LABEL + 1] + rows for k in range(0, cells, LANES)]
    at = lax.broadcasted_iota(I32, (1, padded), 1)
    n = at >> 3
    device = (((n & (half - 1)) << 1) | (n >= half).astype(I32)) ^ me
    row = (device >> 1) * 8 + (at & 7)
    key = jnp.where((device & 1) == 1, (TX + 1) * rows + row, row)
    keys.append(jnp.where(at < edge, key, -1).astype(F32))
    keys = jnp.concatenate(keys, axis=1)
    total = cells + padded
    edge_live = [x[k, 0, 80:88, :] for x in (same_b, other_b) for k in range(half)]
    if padded > edge:
        edge_live.append(jnp.zeros((padded - edge, LANES), F32))
    live = jnp.concatenate([column_of(info, COUNT), *edge_live], axis=0)
    index = lax.broadcasted_iota(I32, (total, LANES), 0)
    cell = column_of(mine, LABEL).astype(I32)
    column, across = split(cell, rows)
    hot = []
    for a, b in NEAR:
        row = across + b
        wanted = jnp.where((row >= 0) & (row < rows), (column + a + 1) * rows + row, -2).astype(F32)
        parts = [keys[:, k : k + LANES] == wanted for k in range(0, total, LANES)]
        hot.append(jnp.concatenate([p.astype(F32) for p in parts], axis=1))
    hot = jnp.concatenate(hot, axis=0).astype(jnp.bfloat16)

    def look_up(values):
        return jnp.dot(hot, values.astype(F32).astype(jnp.bfloat16), preferred_element_type=F32)

    blocks, slots = look_up(index >> 4), look_up(index & 15)
    lives = look_up(live)
    tiles = mine.shape[0]
    entries = []
    for e, (a, b) in enumerate(NEAR):
        at = slice(e * tiles, (e + 1) * tiles)
        chunks = halves_in(lives[at])
        if e != 4:
            chunks = jnp.where(column_of(mine, REACH + e) > 0.5, chunks, 0)
        row = blocks[at].astype(I32) * (12 * SLOTS) + slots[at].astype(I32)
        n, spot = place_of(column + a, across + b, me, half)
        entries.append((row, n * 64 + spot, jnp.float32(a), jnp.float32(b), chunks))
    count = 2 * half
    spare = (cells + edge) // SLOTS * (12 * SLOTS)
    rows, givens, east, north = list_halves(
        entries, column_of(mine, COUNT), spare, 6 * SLOTS, SLOTS, 24, (count * 64, 32)
    )
    lane = lax.broadcasted_iota(I32, rows.shape, 1)
    n, spot = place_of(column, across, me, half)
    givens = jnp.where(lane == HOLDER, n, givens)
    return rows, jnp.where(lane == HELD_AT, spot, givens), east, north


def second_kernel(
    own_block, mine, columns, same, other, same_b, other_b,
    betas, hats, residual,
    table, given, own, scales, low, high, sums, listed, stepped,
    words, steps, sem, word_sem,
):
    copies = fetch(same, other, table, 3, sem)
    half, _, _, tiles, _ = same.shape
    blocks = 2 * half
    for side, held in enumerate((same_b, other_b)):
        at = pl.ds(side * half, half)
        to = given.at[0, at, :, pl.ds(0, 24)]
        copies.append(pltpu.make_async_copy(held.at[:, :, pl.ds(0, 24)], to, sem))
    for copy in copies:
        copy.start()
    listed[0], listed[1], stepped[0], stepped[1] = second_lists(mine, same, other, same_b, other_b)
    word_copies = [
        pltpu.make_async_copy(listed, words, word_sem),
        pltpu.make_async_copy(stepped, steps, word_sem),
    ]
    for copy in word_copies:
        copy.start()
    scales[...] = scale_of(mine[:, WIDTH : WIDTH + 1])
    present = records(tiles) < column_of(mine, COUNT)[None]
    scale_rows = scales[...][None]
    x, y = own_block[EAST], own_block[NORTH]

    def number_of(t):
        return words[0, t, LIVE]

    for n in range(2 * half):
        held = (same_b if n < half else other_b).at[n % half]
        for field in range(3):
            table[blocks + n // 2, field, :, n % 2 * 8 : n % 2 * 8 + 8, :] = held[
                :, 56 + 8 * field : 64 + 8 * field, :
            ]
    for field in range(3):
        table[blocks + half, field, :, 0:8, :] = jnp.zeros((2, 8, LANES), F32)
    given[0, :, :, 24:32, :] = jnp.zeros((2 * half, 2, 8, LANES), F32)
    for copy in copies:
        copy.wait()

    def turn(n, carry):
        table[n, 3:6] = turned(table[n, 0:3])
        return carry

    def turn_given(n, carry):
        given[1, n] = turned(given[0, n])
        return carry

    lax.fori_loop(0, table.shape[0], turn, 0)
    lax.fori_loop(0, 2 * half, turn_given, 0)
    for copy in word_copies:
        copy.wait()

    flat = table.reshape(table.shape[0] * 12 * SLOTS, LANES)
    flat_given = given.reshape(2 * 2 * half * 64, LANES)

    def rows_for(t, i):
        row = words[0, t, i]
        held = [flat[pl.ds(row + field * 2 * SLOTS, 1), :] for field in (EAST, NORTH, TWO)]
        return [*held, flat_given[pl.ds(words[1, t, i], 1), :]]

    def each(t, carry):
        n, at = words[1, t, HOLDER], words[1, t, HELD_AT]
        for k in range(2):
            here = (n & (half - 1), slice(None), pl.ds(16 * (k + 1) + at, 1), slice(None))
            own[k, :, pl.ds(t, 1), :] = jnp.where(n >= half, other_b[here], same_b[here])
        sweep_tile(t, t, scales[pl.ds(t, 1), :], columns, sums, words, steps, rows_for)
        return carry

    lax.fori_loop(0, tiles, each, 0)
    collect_sums(tiles, number_of, sums, low, high)
    shrink = jnp.exp2(-scale_rows * (x * x + y * y))
    den, num = rows_of(low[...], high[...], tiles)
    inv = 1.0 / (1.0 + shrink * den)
    beta_two = jnp.where(present, shrink * num * inv, 0.0)
    beta_one = own[0]
    one, two = own_block[ONE], own_block[TWO]
    left = jnp.where(present, own_block[PRICE] - one * beta_one - two * beta_two, 0.0)
    hat_two = jnp.where(present, two * two * inv, 0.0)
    for t in range(tiles):
        for h in range(2):
            at = slice(t * TILE + h * LANES, t * TILE + (h + 1) * LANES)
            betas[0:1, at] = beta_one[h, t : t + 1]
            betas[1:2, at] = beta_two[h, t : t + 1]
            hats[0:1, at] = own[1, h, t : t + 1, :]
            hats[1:2, at] = hat_two[h, t : t + 1]
            residual[0:1, at] = left[h, t : t + 1]


def swap(x, k):
    count = lax.axis_size("tile")
    return lax.ppermute(x, "tile", [(i, i ^ k) for i in range(count)])


def spread(block):
    count = lax.axis_size("tile")
    same = jnp.stack([block] + [swap(block, k) for k in range(2, count, 2)])
    return same, swap(same, 1)


def body(offsets, design, target, beta_second, counts, kernel_width, reach, assignment):
    tiles = counts.shape[0]
    count = lax.axis_size("tile")
    regions = lax.axis_size("region")
    cells = tiles * count
    limit = pltpu.CompilerParams(vmem_limit_bytes=24 * 1024 * 1024)
    price = target.reshape(1, -1)
    wide = tiles * TILE
    given = (
        offsets, design, price, beta_second.reshape(1, -1),
        counts, kernel_width, reach.transpose(2, 0, 1), assignment,
    )
    block, mine = pl.pallas_call(
        prepare_kernel,
        out_shape=(
            pltpu.VMEM((7, 2, tiles, LANES), F32),
            pltpu.VMEM((tiles, LANES), F32),
        ),
        in_specs=[pl.BlockSpec(memory_space=pltpu.HBM)] * 8,
        out_specs=(VMEM, VMEM),
        scratch_shapes=[pltpu.VMEM((2, wide), F32)] * 2
        + [pltpu.VMEM((1, wide), F32)] * 2
        + [
            pltpu.SMEM((tiles,), I32),
            pltpu.SMEM((2, tiles), I32),
            pltpu.SMEM((9, 2, tiles), I32),
            pltpu.SMEM((1, tiles), I32),
            pltpu.SemaphoreType.DMA,
        ],
        compiler_params=limit,
    )(*[pltpu.with_memory_space_constraint(x, pltpu.HBM) for x in given])
    square = pltpu.VMEM((LANES, LANES), F32)
    dma = pltpu.SemaphoreType.DMA
    own_columns = pl.pallas_call(
        own_columns_kernel,
        out_shape=pltpu.VMEM((tiles, 2, TILE, LANES), F32),
        in_specs=[VMEM, VMEM],
        out_specs=VMEM,
        scratch_shapes=[square, square, pltpu.SMEM((tiles, LANES), F32), dma],
        compiler_params=limit,
        cost_estimate=pl.CostEstimate(flops=4000000, bytes_accessed=4000000, transcendentals=0),
    )(block, mine)
    same, other = spread(block)
    edge, near = pl.pallas_call(
        border_kernel,
        out_shape=(
            jax.ShapeDtypeStruct((2, 136, LANES), F32),
            pltpu.VMEM((7, 2, NEAR_ROWS, LANES), F32),
        ),
        in_specs=[VMEM, VMEM],
        out_specs=(VMEM, VMEM),
        compiler_params=limit,
    )(same, other)
    near_columns = pl.pallas_call(
        near_kernel,
        out_shape=pltpu.VMEM((16, 2, TILE, LANES), F32),
        in_specs=[VMEM],
        out_specs=VMEM,
        scratch_shapes=[square, square, pltpu.SMEM((NEAR_ROWS, LANES), F32), dma],
        compiler_params=limit,
        cost_estimate=pl.CostEstimate(flops=4000000, bytes_accessed=4000000, transcendentals=0),
    )(near)
    moves = []
    for r in range(regions):
        for t in range(count):
            to = r + 1 - 2 * (t % 2)
            if 0 <= to < regions:
                moves.append((r * count + t, to * count + t))
    border = lax.ppermute(edge, ("region", "tile"), moves)
    first = pl.pallas_call(
        first_kernel,
        out_shape=jax.ShapeDtypeStruct((2, 88, LANES), F32),
        in_specs=[VMEM, VMEM, VMEM],
        out_specs=VMEM,
        scratch_shapes=[
            pltpu.VMEM((10, 2, NEAR_ROWS + EDGE_ROWS, LANES), F32),
            pltpu.VMEM((24, LANES), F32),
            square,
            square,
            square,
            square,
            pltpu.VMEM((8, 2, TILE, LANES), F32),
            pltpu.VMEM((24, TILE, 2 * LANES), F32),
            pltpu.VMEM((1, 24, LANES), I32),
            pltpu.VMEM((2, 24, LANES), F32),
            pltpu.SMEM((1, 24, LANES), I32),
            pltpu.SMEM((2, 24, LANES), F32),
            dma,
            dma,
        ],
        compiler_params=limit,
    )(near, near_columns, border)
    same_b, other_b = spread(first)
    betas, hats, residual = pl.pallas_call(
        second_kernel,
        out_shape=(
            jax.ShapeDtypeStruct((2, wide), F32),
            jax.ShapeDtypeStruct((2, wide), F32),
            jax.ShapeDtypeStruct((1, wide), F32),
        ),
        in_specs=[VMEM] * 7,
        out_specs=(VMEM, VMEM, VMEM),
        scratch_shapes=[
            pltpu.VMEM((count + count // 2 + 1, 6, 2, tiles, LANES), F32),
            pltpu.VMEM((2, count, 2, 32, LANES), F32),
            pltpu.VMEM((2, 2, tiles, LANES), F32),
            pltpu.VMEM((tiles, LANES), F32),
            square,
            square,
            pltpu.VMEM((tiles, TILE, 2 * LANES), F32),
            pltpu.VMEM((2, tiles, LANES), I32),
            pltpu.VMEM((2, tiles, LANES), F32),
            pltpu.SMEM((2, tiles, LANES), I32),
            pltpu.SMEM((2, tiles, LANES), F32),
            dma,
            dma,
        ],
        compiler_params=limit,
    )(block, mine, own_columns, same, other, same_b, other_b)
    return (betas, hats, residual.reshape(-1))


def solution(mesh):
    in_specs = (
        P(None, ("region", "tile")),
        P(None, ("region", "tile")),
        P(("region", "tile")),
        P(("region", "tile")),
        P(("region", "tile")),
        P(None, ("region", "tile")),
        P(None, ("region", "tile"), None),
        P("region", "tile"),
    )
    out_specs = (P(None, ("region", "tile")), P(None, ("region", "tile")), P(("region", "tile")))
    return jax.shard_map(body, mesh=mesh, in_specs=in_specs, out_specs=out_specs, check_vma=False)
```

```python
import functools

import jax
import jax.numpy as jnp
from jax import lax
from jax.experimental import pallas as pl
from jax.experimental.pallas import tpu as pltpu
from jax.sharding import PartitionSpec as P

TILE = 256
TX = 4
LANES = 128
TWO, EAST, NORTH, ONE, PART, PRICE, INFO = range(7)
SLOTS = 16
BASE = 32.0 * 1.4426950408889634
LABEL, COUNT, WIDTH, REACH = 0, 1, 2, 3
NEAR = [(a, b) for a in (-1, 0, 1) for b in (-1, 0, 1)]
F32, I32 = jnp.float32, jnp.int32
ANY = pl.BlockSpec(memory_space=pl.ANY)
SMEM = pl.BlockSpec(memory_space=pltpu.SMEM)
VMEM = pl.BlockSpec(memory_space=pltpu.VMEM)


def prepare_kernel(*refs):
    given, (out, mine), held, sem = refs[:8], refs[8:10], refs[10:18], refs[18]
    copies = [pltpu.make_async_copy(a, b, sem) for a, b in zip(given, held)]
    for copy in copies:
        copy.start()
    for copy in copies:
        copy.wait()
    off, des, tgt, sec, counts, widths, reach, cells = held
    lane = lax.broadcasted_iota(I32, (1, LANES), 1)
    for t in range(counts.shape[0]):
        row = jnp.zeros((1, LANES), F32)
        facts = [cells[0, t], counts[t], widths[0, t]] + [reach[e, 0, t] for e in range(9)]
        for k, fact in enumerate(facts):
            row = jnp.where(lane == k, fact.astype(F32), row)
        out[INFO, 0, t : t + 1, :] = row
        for k, value in enumerate([widths[1, t]] + [reach[e, 1, t] for e in range(9)]):
            row = jnp.where(lane == WIDTH + k, value.astype(F32), row)
        mine[t : t + 1, :] = row
        for h in range(2):
            at = slice(t * TILE + h * LANES, t * TILE + (h + 1) * LANES)
            live = lane + h * LANES < counts[t]
            one = jnp.where(live, des[0:1, at], 0.0)
            two = jnp.where(live, des[1:2, at], 0.0)
            price = tgt[0:1, at]
            out[EAST, h, t : t + 1, :] = off[0:1, at] - 0.5
            out[NORTH, h, t : t + 1, :] = off[1:2, at] - 0.5
            out[ONE, h, t : t + 1, :] = one
            out[PART, h, t : t + 1, :] = one * (price - two * sec[0:1, at])
            out[TWO, h, t : t + 1, :] = two
            out[PRICE, h, t : t + 1, :] = price
    out[INFO, 1] = jnp.zeros_like(out[INFO, 1])


def split(number, size):
    return number >> (size.bit_length() - 1), number & (size - 1)


def fetch(same, other, table, fields, sem):
    half = same.shape[0]
    return [
        pltpu.make_async_copy(
            held.at[:, pl.ds(0, fields)], table.at[pl.ds(side * half, half), pl.ds(0, fields)], sem
        )
        for side, held in enumerate((same, other))
    ]


ORDER = [(0, r) for r in range(1, 9)] + [(1, r) for r in range(1, 9)]
ORDER += [(0, 0), (0, 9), (1, 0), (1, 9)]
NEAR_ROWS, EDGE_ROWS, SPARE = 32, 24, 30


def wanted_cells(rows):
    me = lax.axis_index("tile")
    odd = me & 1
    first = (me >> 1) * 8
    i = lax.broadcasted_iota(I32, (64, LANES), 0)
    u = (i >= 10).astype(I32) + (i >= 20).astype(I32)
    j = i - NEAR_ROWS
    away = jnp.where(j < 16, j >> 3, (j >> 1) & 1)
    own = i < NEAR_ROWS
    r = jnp.where(own, i - 10 * u, jnp.where(j < 16, (j & 7) + 1, (j & 1) * 9))
    low = jnp.where(own, u, TX - 1 - away)
    column = jnp.where(odd == 1, TX - 1 - low, low)
    cell = column * rows + jnp.clip(first + r - 1, 0, rows - 1)
    none = (i == SPARE) | (i == SPARE + 1) | (j >= len(ORDER))
    return jnp.where(none, -1, cell).astype(F32)


def border_kernel(same, other, out, near):
    half = same.shape[0]
    cells = 2 * half * SLOTS

    def plane(field, h):
        parts = [x[:, field, h].reshape(half * SLOTS, LANES) for x in (same, other)]
        return jnp.concatenate(parts, axis=0)

    info = plane(INFO, 0)
    wanted = wanted_cells(cells // TX)
    hot = []
    for k in range(0, cells, LANES):
        labels = info[k : k + LANES].T[LABEL : LABEL + 1]
        hot.append((jnp.broadcast_to(labels, wanted.shape) == wanted).astype(F32))
    hot = jnp.concatenate(hot, axis=1).astype(jnp.bfloat16)

    def pick(values, pieces):
        total = jnp.zeros((64, LANES), F32)
        for _ in range(pieces):
            piece = values.astype(jnp.bfloat16)
            values = values - piece.astype(F32)
            total = total + jnp.dot(hot, piece, preferred_element_type=F32)
        return total

    for field in (EAST, NORTH, ONE, PART, INFO, TWO, PRICE):
        for h in range(2):
            if field != INFO:
                got = pick(plane(field, h), 3)
            elif h == 0:
                got = pick(info, 1)
            near[field, h] = got[0:NEAR_ROWS]
            edge = got[NEAR_ROWS : NEAR_ROWS + EDGE_ROWS]
            if field in (TWO, PRICE):
                f = (TWO, PRICE).index(field)
                out[h, 120 + 8 * f : 128 + 8 * f, :] = edge[0:8]
            else:
                f = (EAST, NORTH, ONE, PART, INFO).index(field)
                out[h, f * 24 : f * 24 + 24, :] = edge


def targets_of(near, field):
    return jnp.concatenate([near[field, :, 1:9, :], near[field, :, 11:19, :]], axis=1)


def near_kernel(
    near, columns, sums,
    table, own, east, north, listed, stepped, facts, words, steps, sem, word_sem,
):
    copy = pltpu.make_async_copy(near.at[INFO, 0], facts, sem)
    copy.start()
    rows = lax.axis_size("tile") * SLOTS // TX
    near_info = near[INFO, 0]
    listed[0], _, stepped[0], stepped[1] = first_lists(near_info, None, rows, (2,), 4, NEAR_ROWS)
    word_copies = [
        pltpu.make_async_copy(listed, words, word_sem),
        pltpu.make_async_copy(stepped, steps, word_sem),
    ]
    for word_copy in word_copies:
        word_copy.start()
    info = targets_of(near, INFO)[0]
    own[...] = scale_of(info[:, WIDTH : WIDTH + 1])
    scale = own[...][None]
    east[...] = columns_of(2.0 * scale * targets_of(near, EAST))
    north[...] = columns_of(2.0 * scale * targets_of(near, NORTH))
    table[0:4] = near[EAST : PART + 1]
    table[4:8] = turned(near[EAST : PART + 1])

    def number_of(t):
        return facts[(t >> 3) * 10 + (t & 7) + 1, COUNT].astype(I32)

    spread_columns(16, number_of, east, north, columns, copy.wait)
    for word_copy in word_copies:
        word_copy.wait()
    flat = table.reshape(16 * NEAR_ROWS, LANES)

    def rows_for(t, i):
        row = words[0, t, i]
        return [flat[pl.ds(row + k * 2 * NEAR_ROWS, 1), :] for k in range(4)]

    def each(t, carry):
        sweep_tile(t, t + 8, own[pl.ds(t + 8, 1), :], columns, sums, words, steps, rows_for)
        return carry

    lax.fori_loop(0, 8, each, 0)


USED, LIVE, HOLDER, HELD_AT = 100, 101, 102, 103


def column_of(info, k):
    return jnp.broadcast_to(info[:, k : k + 1], (info.shape[0], LANES))


def halves_in(number):
    return sum((number > 64.0 * q).astype(I32) for q in range(4))


def list_halves(entries, number, spare, other, half_at, spare_given=0, given_at=(0, 0)):
    lane = lax.broadcasted_iota(I32, number.shape, 1)
    rows = jnp.full(number.shape, spare, I32)
    givens = jnp.full(number.shape, spare_given, I32)
    east, north = jnp.zeros(number.shape, F32), jnp.zeros(number.shape, F32)
    used = jnp.zeros(number.shape, I32)
    for row, given, a, b, halves in entries:
        moved = used & 1
        row = row + moved * other
        given = given + moved * given_at[0]
        for q in range(4):
            here = (lane == used + q) & (halves > q)
            rows = jnp.where(here, row + (q >> 1) * half_at, rows)
            givens = jnp.where(here, given + (q >> 1) * given_at[1], givens)
        here = (lane >= used) & (lane < used + halves)
        east = jnp.where(here, a, east)
        north = jnp.where(here, b, north)
        used = used + halves
    rows = jnp.where(lane == USED, used, rows)
    rows = jnp.where(lane == LIVE, number.astype(I32), rows)
    return rows, givens, east, north


def turned(values):
    flat = pltpu.roll(values.reshape(-1, LANES), LANES // 2, 1)
    return flat.reshape(values.shape)


def place_of(column, row, me, half):
    low = (column < TX // 2).astype(I32)
    depth = jnp.where(low == 1, column + 1, TX - column)
    k = ((row >> 3) * 2 + 1 - low) ^ me
    return (k & 1) * half + (k >> 1), depth * 8 + (row & 7)


def scale_of(width):
    return jnp.broadcast_to(BASE / (width * width), (width.shape[0], LANES))


def own_columns_kernel(block, mine, columns, east, north, facts, sem):
    copy = pltpu.make_async_copy(mine, facts, sem)
    copy.start()
    scale = scale_of(mine[:, WIDTH : WIDTH + 1])[None]
    east[...] = columns_of(2.0 * scale * block[EAST])
    north[...] = columns_of(2.0 * scale * block[NORTH])

    def number_of(t):
        return facts[t, COUNT].astype(I32)

    spread_columns(block.shape[2], number_of, east, north, columns, copy.wait)


def records(tiles):
    shape = (2, tiles, LANES)
    number = lax.broadcasted_iota(I32, shape, 2) + LANES * lax.broadcasted_iota(I32, shape, 0)
    return number.astype(F32)


def columns_of(rows):
    pad = jnp.zeros((64 - rows.shape[1], LANES), F32)
    return jnp.concatenate([rows[0], pad, rows[1], pad], axis=0).T


def rows_of(low, high, tiles):
    low, high = low.T, high.T
    return [jnp.stack([low[k : k + tiles], high[k : k + tiles]]) for k in (0, 64)]


def spread_columns(tiles, number_of, east, north, columns, ready=None):
    def lay(t, nb, values):
        i = (nb >> 1) * 64 + t
        for k, value in enumerate(values):
            wide = jnp.broadcast_to(value[:, i : i + 1], (64, LANES))
            columns[t, k, nb * 64 : nb * 64 + 64, :] = wide

    low = (east[0:64, :], north[0:64, :])
    for t in range(tiles):
        lay(t, 0, low)
    if ready is not None:
        ready()
    for t in range(tiles):
        number = number_of(t)

        @pl.when(number > 64)
        def _():
            lay(t, 1, (east[64:128, :], north[64:128, :]))

        @pl.when(number > 128)
        def _():
            lay(t, 2, (east[0:64, :], north[0:64, :]))
            lay(t, 3, (east[64:128, :], north[64:128, :]))


SHARE = 3
GROUP = 4


def collect_sums(parts, number_of, low_ref, high_ref, large):
    split_at = (lax.broadcasted_iota(I32, (4 * LANES, LANES), 0) // LANES) & 1
    sides = lax.broadcasted_iota(I32, (4 * LANES, LANES), 1) // 64
    ones = (split_at == sides).astype(F32).astype(jnp.bfloat16)
    place = lax.broadcasted_iota(I32, (64, LANES), 1)
    lane = place & 63

    def total(values):
        high = values.astype(jnp.bfloat16)
        low = (values - high.astype(F32)).astype(jnp.bfloat16)
        return jnp.dot(jnp.concatenate([high, low], axis=1), ones, preferred_element_type=F32)

    for nb in range(2):
        result = jnp.zeros((64, LANES), F32)
        held = [(sums, t) for sums, tiles in parts for t in range(tiles)]
        for i, (sums, t) in enumerate(held):
            values = sums[t, nb * 64 : nb * 64 + 64, :]
            if i % SHARE == SHARE - 1:
                for k in range(2):
                    x = jnp.sum(values[:, k * LANES : (k + 1) * LANES], axis=1, keepdims=True)
                    result = jnp.where(place == k * 64 + i, x, result)
            else:
                result = jnp.where(lane == i, total(values), result)
        low_ref[nb * 64 : nb * 64 + 64, :] = result
    high_ref[...] = jnp.zeros_like(high_ref)

    start = 0
    for sums, tiles in parts:
        many = jnp.int32(0)
        for t in range(tiles):
            large[many] = jnp.int32(t)
            many = many + (number_of(start + t) > 128).astype(I32)
        last = large[jnp.maximum(many - 1, 0)]
        for k in range(GROUP - 1):
            large[many + k] = last

        def some(g, carry, sums=sums, start=start):
            result = high_ref[...]
            for i in range(GROUP):
                t = large[g * GROUP + i]
                mine = (lax.broadcasted_iota(I32, (LANES, LANES), 1) & 63) == start + t
                result = jnp.where(mine, total(sums[t, 128:256, :]), result)
            high_ref[...] = result
            return carry

        lax.fori_loop(0, (many + GROUP - 1) // GROUP, some, 0)
        start += tiles


def sweep_tile(t, at_column, scale, columns, sums, words, steps, rows_for):
    scale = jnp.broadcast_to(scale, (8, LANES))
    left = lax.broadcasted_iota(I32, (8, LANES), 1) < LANES // 2

    def chunk(i):
        sides = []
        for k in range(2):
            u, v, c, d = [jnp.broadcast_to(row, (8, LANES)) for row in rows_for(t, i + k)]
            sides.append((u + steps[0, t, i + k], v + steps[1, t, i + k], c, d))
        u, v, c, d = [jnp.where(left, *pair) for pair in zip(*sides)]
        fade = jnp.exp2(-scale * (u * u + v * v))
        return u, v, c * c * fade, d * fade

    def block(nb, size, step):
        at = pl.ds(pl.multiple_of(nb * 64, 64), size)
        x = columns[at_column, 0, at, :].reshape(size // 8, 8, LANES)
        y = columns[at_column, 1, at, :].reshape(size // 8, 8, LANES)

        def some(p, sums_now):
            den, num = sums_now
            for k in range(step):
                u, v, c, d = chunk(2 * (step * p + k))
                w = jnp.exp2(x * u + y * v)
                den = den + w * c
                num = num + w * d
            return den, num

        zero = jnp.zeros((size // 8, 8, LANES), F32)
        trips = (words[0, t, USED] + 2 * step - 1) // (2 * step)
        den, num = lax.fori_loop(0, trips, some, (zero, zero))
        sums[t, at, 0:LANES] = den.reshape(size, LANES)
        sums[t, at, LANES : 2 * LANES] = num.reshape(size, LANES)

    number = words[0, t, LIVE]
    whole = (number + 31) >> 6

    def full(nb, carry):
        block(nb, 64, 2)
        return carry

    lax.fori_loop(0, whole, full, 0)

    @pl.when(number > whole * 64)
    def _():
        block(whole, 32, 4)


def first_lists(near_info, edge_info, rows, groups, fields, plane):
    me = lax.axis_index("tile")
    odd = me & 1
    first = (me >> 1) * 8
    near_live = column_of(near_info, COUNT)
    if edge_info is not None:
        edge_live = column_of(edge_info, COUNT)
    step = lax.broadcasted_iota(I32, (8, LANES), 0)
    on_map = [(first > 0).astype(F32), (first + 8 < rows).astype(F32)]
    lines = []
    for u in range(5):
        if u < 2 and edge_info is None:
            lines.append(None)
            continue
        if u < 2:
            away = 1 - u
            parts = [edge_live[i : i + n] for i, n in ((16 + 2 * away, 1), (8 * away, 8), (17 + 2 * away, 1))]
        else:
            parts = [near_live[10 * (u - 2) + i : 10 * (u - 2) + i + n] for i, n in ((0, 1), (1, 8), (9, 1))]
        lines.append(jnp.concatenate([parts[0] * on_map[0], parts[1], parts[2] * on_map[1]], axis=0))

    def source(u, b):
        if u >= 2:
            return (u - 2) * 10 + 1 + b + step
        start = NEAR_ROWS + 8 * (1 - u)
        at = start + b + step
        if b == 0:
            return at
        corner = NEAR_ROWS + 16 + 2 * (1 - u) + (b + 1) // 2
        return jnp.where(step == (0 if b < 0 else 7), corner, at)

    result = []
    infos = (None if edge_info is None else edge_info[0:8], near_info[1:9], near_info[11:19])
    for j, info in enumerate(infos):
        if info is None or (edge_info is None and j not in groups):
            continue
        entries = []
        for du in (-1, 0, 1) if j in groups else ():
            for b in (-1, 0, 1):
                here, there = 3 * (du + 1) + b + 1, 3 * (1 - du) + b + 1
                a = jnp.where(odd == 1, -du, du).astype(F32)
                chunks = halves_in(lines[j + 1 + du][1 + b : 9 + b])
                if here != 4:
                    taken = jnp.where(odd == 1, column_of(info, REACH + there), column_of(info, REACH + here))
                    chunks = jnp.where(taken > 0.5, chunks, 0)
                entries.append((source(j + 1 + du, b), 0, a, jnp.float32(b), chunks))
        moved = 2 * fields * plane
        result.append(list_halves(entries, column_of(info, COUNT), SPARE, moved, plane))
    return [jnp.concatenate(parts, axis=0) for parts in zip(*result)]


def first_kernel(
    near, near_columns, near_sums, border, out,
    table, own, east, north, low, high, columns, sums, listed, stepped,
    words, steps, large, sem, word_sem,
):
    rows = lax.axis_size("tile") * SLOTS // TX
    near_at, edge_at = pl.ds(0, NEAR_ROWS), pl.ds(NEAR_ROWS, EDGE_ROWS)
    copies = [
        pltpu.make_async_copy(near.at[pl.ds(0, 6)], table.at[pl.ds(0, 6), :, near_at], sem)
    ]
    for f, field in enumerate((EAST, NORTH, ONE, PART)):
        held = border.at[:, pl.ds(f * 24, 24)]
        copies.append(pltpu.make_async_copy(held, table.at[field, :, edge_at], sem))
    for f, field in enumerate((TWO, PRICE)):
        held = border.at[:, pl.ds(120 + 8 * f, 8)]
        copies.append(pltpu.make_async_copy(held, table.at[field, :, pl.ds(NEAR_ROWS, 8)], sem))
    for copy in copies:
        copy.start()
    near_info, edge_info = near[INFO, 0], border[0, 4 * 24 : 5 * 24, :]
    listed[0], _, stepped[0], stepped[1] = first_lists(
        near_info, edge_info, rows, (0, 1), 5, NEAR_ROWS + EDGE_ROWS
    )
    word_copies = [
        pltpu.make_async_copy(listed, words, word_sem),
        pltpu.make_async_copy(stepped, steps, word_sem),
    ]
    for copy in word_copies:
        copy.start()
    tiles = 24
    info = jnp.concatenate([edge_info[0:8], near_info[1:9], near_info[11:19]], axis=0)
    scales = scale_of(info[:, WIDTH : WIDTH + 1])
    counts = column_of(info, COUNT)
    for copy in copies:
        copy.wait()

    def of_targets(field):
        parts = [table[field, :, 32:40, :], table[field, :, 1:9, :], table[field, :, 11:19, :]]
        return jnp.concatenate(parts, axis=1)

    present = records(tiles) < counts[None]
    scale_rows = scales[None]
    own[...] = scales
    x, y = of_targets(EAST), of_targets(NORTH)
    east[...] = columns_of(2.0 * scale_rows[:, 0:8] * x[:, 0:8])
    north[...] = columns_of(2.0 * scale_rows[:, 0:8] * y[:, 0:8])

    def number_of(t):
        return words[0, t, LIVE]

    def ready():
        for copy in word_copies:
            copy.wait()

    spread_columns(8, number_of, east, north, columns, ready)

    table[6:10] = turned(table[EAST : PART + 1])

    plane = 2 * (NEAR_ROWS + EDGE_ROWS)
    flat = table.reshape(10 * plane, LANES)

    def rows_for(t, i):
        row = words[0, t, i]
        return [flat[pl.ds(row + field * plane, 1), :] for field in (EAST, NORTH, ONE, PART)]

    def each(t, carry, held, skip):
        sweep_tile(t, t - skip, own[pl.ds(t, 1), :], held, sums, words, steps, rows_for)
        return carry

    lax.fori_loop(0, 8, lambda t, c: each(t, c, columns, 0), 0)
    lax.fori_loop(8, 16, lambda t, c: each(t, c, near_columns, 8), 0)
    collect_sums([(sums, 16), (near_sums, 8)], number_of, low, high, large)
    shrink = jnp.exp2(-scale_rows * (x * x + y * y))
    den, num = rows_of(low[...], high[...], tiles)
    inv = 1.0 / (1.0 + shrink * den)
    beta = jnp.where(present, shrink * num * inv, 0.0)
    one, two = of_targets(ONE), of_targets(TWO)
    out[:, 0:24, :] = two * (of_targets(PRICE) - one * beta)
    out[:, 24:40, :] = beta[:, 8:24]
    out[:, 40:56, :] = jnp.where(present, one * one * inv, 0.0)[:, 8:24]
    out[:, 56:64, :] = two[:, 0:8]
    out[:, 64:72, :] = x[:, 0:8]
    out[:, 72:80, :] = y[:, 0:8]
    out[:, 80:88, :] = jnp.broadcast_to(counts[0:8][None], (2, 8, LANES))


def second_lists(mine, same, other, same_b, other_b):
    half = same.shape[0]
    cells = 2 * half * SLOTS
    rows = cells // TX
    edge = 2 * half * 8
    padded = -(-edge // LANES) * LANES
    me = lax.axis_index("tile")
    info = jnp.concatenate([x[:, INFO, 0].reshape(half * SLOTS, LANES) for x in (same, other)], axis=0)
    keys = [info[k : k + LANES].T[LABEL : LABEL + 1] + rows for k in range(0, cells, LANES)]
    at = lax.broadcasted_iota(I32, (1, padded), 1)
    n = at >> 3
    device = (((n & (half - 1)) << 1) | (n >= half).astype(I32)) ^ me
    row = (device >> 1) * 8 + (at & 7)
    key = jnp.where((device & 1) == 1, (TX + 1) * rows + row, row)
    keys.append(jnp.where(at < edge, key, -1).astype(F32))
    keys = jnp.concatenate(keys, axis=1)
    total = cells + padded
    edge_live = [x[k, 0, 80:88, :] for x in (same_b, other_b) for k in range(half)]
    if padded > edge:
        edge_live.append(jnp.zeros((padded - edge, LANES), F32))
    live = jnp.concatenate([column_of(info, COUNT), *edge_live], axis=0)
    index = lax.broadcasted_iota(I32, (total, LANES), 0)
    cell = column_of(mine, LABEL).astype(I32)
    column, across = split(cell, rows)
    hot = []
    for a, b in NEAR:
        row = across + b
        wanted = jnp.where((row >= 0) & (row < rows), (column + a + 1) * rows + row, -2).astype(F32)
        parts = [keys[:, k : k + LANES] == wanted for k in range(0, total, LANES)]
        hot.append(jnp.concatenate([p.astype(F32) for p in parts], axis=1))
    hot = jnp.concatenate(hot, axis=0).astype(jnp.bfloat16)

    def look_up(values):
        return jnp.dot(hot, values.astype(F32).astype(jnp.bfloat16), preferred_element_type=F32)

    blocks, slots = look_up(index >> 4), look_up(index & 15)
    lives = look_up(live)
    tiles = mine.shape[0]
    entries = []
    for e, (a, b) in enumerate(NEAR):
        at = slice(e * tiles, (e + 1) * tiles)
        chunks = halves_in(lives[at])
        if e != 4:
            chunks = jnp.where(column_of(mine, REACH + e) > 0.5, chunks, 0)
        row = blocks[at].astype(I32) * (12 * SLOTS) + slots[at].astype(I32)
        n, spot = place_of(column + a, across + b, me, half)
        entries.append((row, n * 64 + spot, jnp.float32(a), jnp.float32(b), chunks))
    count = 2 * half
    spare = (cells + edge) // SLOTS * (12 * SLOTS)
    rows, givens, east, north = list_halves(
        entries, column_of(mine, COUNT), spare, 6 * SLOTS, SLOTS, 24, (count * 64, 32)
    )
    lane = lax.broadcasted_iota(I32, rows.shape, 1)
    n, spot = place_of(column, across, me, half)
    givens = jnp.where(lane == HOLDER, n, givens)
    return rows, jnp.where(lane == HELD_AT, spot, givens), east, north


def second_kernel(
    own_block, mine, columns, same, other, same_b, other_b,
    betas, hats, residual,
    table, given, own, scales, low, high, sums, listed, stepped,
    words, steps, large, sem, word_sem,
):
    copies = fetch(same, other, table, 3, sem)
    half, _, _, tiles, _ = same.shape
    blocks = 2 * half
    for side, held in enumerate((same_b, other_b)):
        at = pl.ds(side * half, half)
        to = given.at[0, at, :, pl.ds(0, 24)]
        copies.append(pltpu.make_async_copy(held.at[:, :, pl.ds(0, 24)], to, sem))
    for copy in copies:
        copy.start()
    listed[0], listed[1], stepped[0], stepped[1] = second_lists(mine, same, other, same_b, other_b)
    word_copies = [
        pltpu.make_async_copy(listed, words, word_sem),
        pltpu.make_async_copy(stepped, steps, word_sem),
    ]
    for copy in word_copies:
        copy.start()
    scales[...] = scale_of(mine[:, WIDTH : WIDTH + 1])
    present = records(tiles) < column_of(mine, COUNT)[None]
    scale_rows = scales[...][None]
    x, y = own_block[EAST], own_block[NORTH]

    def number_of(t):
        return words[0, t, LIVE]

    for n in range(2 * half):
        held = (same_b if n < half else other_b).at[n % half]
        for field in range(3):
            table[blocks + n // 2, field, :, n % 2 * 8 : n % 2 * 8 + 8, :] = held[
                :, 56 + 8 * field : 64 + 8 * field, :
            ]
    for field in range(3):
        table[blocks + half, field, :, 0:8, :] = jnp.zeros((2, 8, LANES), F32)
    given[0, :, :, 24:32, :] = jnp.zeros((2 * half, 2, 8, LANES), F32)
    for copy in copies:
        copy.wait()

    def turn(n, carry):
        table[n, 3:6] = turned(table[n, 0:3])
        return carry

    def turn_given(n, carry):
        given[1, n] = turned(given[0, n])
        return carry

    lax.fori_loop(0, table.shape[0], turn, 0)
    lax.fori_loop(0, 2 * half, turn_given, 0)
    for copy in word_copies:
        copy.wait()

    flat = table.reshape(table.shape[0] * 12 * SLOTS, LANES)
    flat_given = given.reshape(2 * 2 * half * 64, LANES)

    def rows_for(t, i):
        row = words[0, t, i]
        held = [flat[pl.ds(row + field * 2 * SLOTS, 1), :] for field in (EAST, NORTH, TWO)]
        return [*held, flat_given[pl.ds(words[1, t, i], 1), :]]

    def each(t, carry):
        n, at = words[1, t, HOLDER], words[1, t, HELD_AT]
        for k in range(2):
            here = (n & (half - 1), slice(None), pl.ds(16 * (k + 1) + at, 1), slice(None))
            own[k, :, pl.ds(t, 1), :] = jnp.where(n >= half, other_b[here], same_b[here])
        sweep_tile(t, t, scales[pl.ds(t, 1), :], columns, sums, words, steps, rows_for)
        return carry

    lax.fori_loop(0, tiles, each, 0)
    collect_sums([(sums, tiles)], number_of, low, high, large)
    shrink = jnp.exp2(-scale_rows * (x * x + y * y))
    den, num = rows_of(low[...], high[...], tiles)
    inv = 1.0 / (1.0 + shrink * den)
    beta_two = jnp.where(present, shrink * num * inv, 0.0)
    beta_one = own[0]
    one, two = own_block[ONE], own_block[TWO]
    left = jnp.where(present, own_block[PRICE] - one * beta_one - two * beta_two, 0.0)
    hat_two = jnp.where(present, two * two * inv, 0.0)
    for t in range(tiles):
        for h in range(2):
            at = slice(t * TILE + h * LANES, t * TILE + (h + 1) * LANES)
            betas[0:1, at] = beta_one[h, t : t + 1]
            betas[1:2, at] = beta_two[h, t : t + 1]
            hats[0:1, at] = own[1, h, t : t + 1, :]
            hats[1:2, at] = hat_two[h, t : t + 1]
            residual[0:1, at] = left[h, t : t + 1]


def swap(x, k):
    count = lax.axis_size("tile")
    return lax.ppermute(x, "tile", [(i, i ^ k) for i in range(count)])


def spread(block):
    count = lax.axis_size("tile")
    same = jnp.stack([block] + [swap(block, k) for k in range(2, count, 2)])
    return same, swap(same, 1)


def body(offsets, design, target, beta_second, counts, kernel_width, reach, assignment):
    tiles = counts.shape[0]
    count = lax.axis_size("tile")
    regions = lax.axis_size("region")
    cells = tiles * count
    limit = pltpu.CompilerParams(vmem_limit_bytes=24 * 1024 * 1024)
    price = target.reshape(1, -1)
    wide = tiles * TILE
    given = (
        offsets, design, price, beta_second.reshape(1, -1),
        counts, kernel_width, reach.transpose(2, 0, 1), assignment,
    )
    block, mine = pl.pallas_call(
        prepare_kernel,
        out_shape=(
            pltpu.VMEM((7, 2, tiles, LANES), F32),
            pltpu.VMEM((tiles, LANES), F32),
        ),
        in_specs=[pl.BlockSpec(memory_space=pltpu.HBM)] * 8,
        out_specs=(VMEM, VMEM),
        scratch_shapes=[pltpu.VMEM((2, wide), F32)] * 2
        + [pltpu.VMEM((1, wide), F32)] * 2
        + [
            pltpu.SMEM((tiles,), I32),
            pltpu.SMEM((2, tiles), I32),
            pltpu.SMEM((9, 2, tiles), I32),
            pltpu.SMEM((1, tiles), I32),
            pltpu.SemaphoreType.DMA,
        ],
        compiler_params=limit,
    )(*[pltpu.with_memory_space_constraint(x, pltpu.HBM) for x in given])
    square = pltpu.VMEM((LANES, LANES), F32)
    dma = pltpu.SemaphoreType.DMA
    own_columns = pl.pallas_call(
        own_columns_kernel,
        out_shape=pltpu.VMEM((tiles, 2, TILE, LANES), F32),
        in_specs=[VMEM, VMEM],
        out_specs=VMEM,
        scratch_shapes=[square, square, pltpu.SMEM((tiles, LANES), F32), dma],
        compiler_params=limit,
        cost_estimate=pl.CostEstimate(flops=4000000, bytes_accessed=4000000, transcendentals=0),
    )(block, mine)
    same, other = spread(block)
    edge, near = pl.pallas_call(
        border_kernel,
        out_shape=(
            jax.ShapeDtypeStruct((2, 136, LANES), F32),
            pltpu.VMEM((7, 2, NEAR_ROWS, LANES), F32),
        ),
        in_specs=[VMEM, VMEM],
        out_specs=(VMEM, VMEM),
        compiler_params=limit,
    )(same, other)
    near_columns, near_sums = pl.pallas_call(
        near_kernel,
        out_shape=(
            pltpu.VMEM((16, 2, TILE, LANES), F32),
            pltpu.VMEM((8, TILE, 2 * LANES), F32),
        ),
        in_specs=[VMEM],
        out_specs=(VMEM, VMEM),
        scratch_shapes=[
            pltpu.VMEM((8, 2, NEAR_ROWS, LANES), F32),
            pltpu.VMEM((16, LANES), F32),
            square,
            square,
            pltpu.VMEM((1, 8, LANES), I32),
            pltpu.VMEM((2, 8, LANES), F32),
            pltpu.SMEM((NEAR_ROWS, LANES), F32),
            pltpu.SMEM((1, 8, LANES), I32),
            pltpu.SMEM((2, 8, LANES), F32),
            dma,
            dma,
        ],
        compiler_params=limit,
        cost_estimate=pl.CostEstimate(flops=4000000, bytes_accessed=4000000, transcendentals=0),
    )(near)
    moves = []
    for r in range(regions):
        for t in range(count):
            to = r + 1 - 2 * (t % 2)
            if 0 <= to < regions:
                moves.append((r * count + t, to * count + t))
    border = lax.ppermute(edge, ("region", "tile"), moves)
    first = pl.pallas_call(
        first_kernel,
        out_shape=jax.ShapeDtypeStruct((2, 88, LANES), F32),
        in_specs=[VMEM] * 4,
        out_specs=VMEM,
        scratch_shapes=[
            pltpu.VMEM((10, 2, NEAR_ROWS + EDGE_ROWS, LANES), F32),
            pltpu.VMEM((24, LANES), F32),
            square,
            square,
            square,
            square,
            pltpu.VMEM((8, 2, TILE, LANES), F32),
            pltpu.VMEM((16, TILE, 2 * LANES), F32),
            pltpu.VMEM((1, 24, LANES), I32),
            pltpu.VMEM((2, 24, LANES), F32),
            pltpu.SMEM((1, 24, LANES), I32),
            pltpu.SMEM((2, 24, LANES), F32),
            pltpu.SMEM((24,), I32),
            dma,
            dma,
        ],
        compiler_params=limit,
    )(near, near_columns, near_sums, border)
    same_b, other_b = spread(first)
    betas, hats, residual = pl.pallas_call(
        second_kernel,
        out_shape=(
            jax.ShapeDtypeStruct((2, wide), F32),
            jax.ShapeDtypeStruct((2, wide), F32),
            jax.ShapeDtypeStruct((1, wide), F32),
        ),
        in_specs=[VMEM] * 7,
        out_specs=(VMEM, VMEM, VMEM),
        scratch_shapes=[
            pltpu.VMEM((count + count // 2 + 1, 6, 2, tiles, LANES), F32),
            pltpu.VMEM((2, count, 2, 32, LANES), F32),
            pltpu.VMEM((2, 2, tiles, LANES), F32),
            pltpu.VMEM((tiles, LANES), F32),
            square,
            square,
            pltpu.VMEM((tiles, TILE, 2 * LANES), F32),
            pltpu.VMEM((2, tiles, LANES), I32),
            pltpu.VMEM((2, tiles, LANES), F32),
            pltpu.SMEM((2, tiles, LANES), I32),
            pltpu.SMEM((2, tiles, LANES), F32),
            pltpu.SMEM((24,), I32),
            dma,
            dma,
        ],
        compiler_params=limit,
    )(block, mine, own_columns, same, other, same_b, other_b)
    return (betas, hats, residual.reshape(-1))


def solution(mesh):
    in_specs = (
        P(None, ("region", "tile")),
        P(None, ("region", "tile")),
        P(("region", "tile")),
        P(("region", "tile")),
        P(("region", "tile")),
        P(None, ("region", "tile")),
        P(None, ("region", "tile"), None),
        P("region", "tile"),
    )
    out_specs = (P(None, ("region", "tile")), P(None, ("region", "tile")), P(("region", "tile")))
    return jax.shard_map(body, mesh=mesh, in_specs=in_specs, out_specs=out_specs, check_vma=False)
```

```python
import functools

import jax
import jax.numpy as jnp
from jax import lax
from jax.experimental import pallas as pl
from jax.experimental.pallas import tpu as pltpu
from jax.sharding import PartitionSpec as P

TILE = 256
TX = 4
LANES = 128
TWO, EAST, NORTH, ONE, PART, PRICE, INFO = range(7)
SLOTS = 16
BASE = 32.0 * 1.4426950408889634
LABEL, COUNT, WIDTH, REACH = 0, 1, 2, 3
NEAR = [(a, b) for a in (-1, 0, 1) for b in (-1, 0, 1)]
F32, I32 = jnp.float32, jnp.int32
ANY = pl.BlockSpec(memory_space=pl.ANY)
SMEM = pl.BlockSpec(memory_space=pltpu.SMEM)
VMEM = pl.BlockSpec(memory_space=pltpu.VMEM)


def prepare_kernel(*refs):
    given, (out, mine), held, sem = refs[:8], refs[8:10], refs[10:18], refs[18]
    copies = [pltpu.make_async_copy(a, b, sem) for a, b in zip(given, held)]
    for copy in copies:
        copy.start()
    for copy in copies:
        copy.wait()
    off, des, tgt, sec, counts, widths, reach, cells = held
    lane = lax.broadcasted_iota(I32, (1, LANES), 1)
    for t in range(counts.shape[0]):
        row = jnp.zeros((1, LANES), F32)
        facts = [cells[0, t], counts[t], widths[0, t]] + [reach[e, 0, t] for e in range(9)]
        for k, fact in enumerate(facts):
            row = jnp.where(lane == k, fact.astype(F32), row)
        out[INFO, 0, t : t + 1, :] = row
        for k, value in enumerate([widths[1, t]] + [reach[e, 1, t] for e in range(9)]):
            row = jnp.where(lane == WIDTH + k, value.astype(F32), row)
        mine[t : t + 1, :] = row
        for h in range(2):
            at = slice(t * TILE + h * LANES, t * TILE + (h + 1) * LANES)
            live = lane + h * LANES < counts[t]
            one = jnp.where(live, des[0:1, at], 0.0)
            two = jnp.where(live, des[1:2, at], 0.0)
            price = tgt[0:1, at]
            out[EAST, h, t : t + 1, :] = off[0:1, at] - 0.5
            out[NORTH, h, t : t + 1, :] = off[1:2, at] - 0.5
            out[ONE, h, t : t + 1, :] = one
            out[PART, h, t : t + 1, :] = one * (price - two * sec[0:1, at])
            out[TWO, h, t : t + 1, :] = two
            out[PRICE, h, t : t + 1, :] = price
    out[INFO, 1] = jnp.zeros_like(out[INFO, 1])


def split(number, size):
    return number >> (size.bit_length() - 1), number & (size - 1)


def fetch(same, other, table, fields, sem):
    half = same.shape[0]
    return [
        pltpu.make_async_copy(
            held.at[:, pl.ds(0, fields)], table.at[pl.ds(side * half, half), pl.ds(0, fields)], sem
        )
        for side, held in enumerate((same, other))
    ]


ORDER = [(0, r) for r in range(1, 9)] + [(1, r) for r in range(1, 9)]
ORDER += [(0, 0), (0, 9), (1, 0), (1, 9)]
NEAR_ROWS, EDGE_ROWS, SPARE = 32, 24, 30


def wanted_cells(rows):
    me = lax.axis_index("tile")
    odd = me & 1
    first = (me >> 1) * 8
    i = lax.broadcasted_iota(I32, (64, LANES), 0)
    u = (i >= 10).astype(I32) + (i >= 20).astype(I32)
    j = i - NEAR_ROWS
    away = jnp.where(j < 16, j >> 3, (j >> 1) & 1)
    own = i < NEAR_ROWS
    r = jnp.where(own, i - 10 * u, jnp.where(j < 16, (j & 7) + 1, (j & 1) * 9))
    low = jnp.where(own, u, TX - 1 - away)
    column = jnp.where(odd == 1, TX - 1 - low, low)
    cell = column * rows + jnp.clip(first + r - 1, 0, rows - 1)
    none = (i == SPARE) | (i == SPARE + 1) | (j >= len(ORDER))
    return jnp.where(none, -1, cell).astype(F32)


def border_kernel(same, other, out, near):
    half = same.shape[0]
    cells = 2 * half * SLOTS

    def plane(field, h):
        parts = [x[:, field, h].reshape(half * SLOTS, LANES) for x in (same, other)]
        return jnp.concatenate(parts, axis=0)

    info = plane(INFO, 0)
    wanted = wanted_cells(cells // TX)
    hot = []
    for k in range(0, cells, LANES):
        labels = info[k : k + LANES].T[LABEL : LABEL + 1]
        hot.append((jnp.broadcast_to(labels, wanted.shape) == wanted).astype(F32))
    hot = jnp.concatenate(hot, axis=1).astype(jnp.bfloat16)

    def pick(values, pieces):
        total = jnp.zeros((64, LANES), F32)
        for _ in range(pieces):
            piece = values.astype(jnp.bfloat16)
            values = values - piece.astype(F32)
            total = total + jnp.dot(hot, piece, preferred_element_type=F32)
        return total

    for field in (EAST, NORTH, ONE, PART, INFO, TWO, PRICE):
        for h in range(2):
            if field != INFO:
                got = pick(plane(field, h), 3)
            elif h == 0:
                got = pick(info, 1)
            near[field, h] = got[0:NEAR_ROWS]
            edge = got[NEAR_ROWS : NEAR_ROWS + EDGE_ROWS]
            if field in (TWO, PRICE):
                f = (TWO, PRICE).index(field)
                out[h, 120 + 8 * f : 128 + 8 * f, :] = edge[0:8]
            else:
                f = (EAST, NORTH, ONE, PART, INFO).index(field)
                out[h, f * 24 : f * 24 + 24, :] = edge


def targets_of(near, field):
    return jnp.concatenate([near[field, :, 1:9, :], near[field, :, 11:19, :]], axis=1)


def near_kernel(
    near, columns, sums,
    table, own, east, north, listed, stepped, facts, words, steps, sem, word_sem,
):
    copy = pltpu.make_async_copy(near.at[INFO, 0], facts, sem)
    copy.start()
    rows = lax.axis_size("tile") * SLOTS // TX
    near_info = near[INFO, 0]
    listed[0], _, stepped[0], stepped[1] = first_lists(near_info, None, rows, (2,), 4, NEAR_ROWS)
    word_copies = [
        pltpu.make_async_copy(listed, words, word_sem),
        pltpu.make_async_copy(stepped, steps, word_sem),
    ]
    for word_copy in word_copies:
        word_copy.start()
    info = targets_of(near, INFO)[0]
    own[...] = scale_of(info[:, WIDTH : WIDTH + 1])
    scale = own[...][None]
    east[...] = columns_of(2.0 * scale * targets_of(near, EAST))
    north[...] = columns_of(2.0 * scale * targets_of(near, NORTH))
    table[0:4] = near[EAST : PART + 1]
    table[4:8] = turned(near[EAST : PART + 1])

    def number_of(t):
        return facts[(t >> 3) * 10 + (t & 7) + 1, COUNT].astype(I32)

    spread_columns(16, number_of, east, north, columns, copy.wait)
    for word_copy in word_copies:
        word_copy.wait()
    flat = table.reshape(16 * NEAR_ROWS, LANES)

    def rows_for(t, i):
        row = words[0, t, i]
        return [flat[pl.ds(row + k * 2 * NEAR_ROWS, 1), :] for k in range(4)]

    def each(t, carry):
        sweep_tile(t, t + 8, own[pl.ds(t + 8, 1), :], columns, sums, words, steps, rows_for)
        return carry

    lax.fori_loop(0, 8, each, 0)


USED, LIVE, HOLDER, HELD_AT = 100, 101, 102, 103


def column_of(info, k):
    return jnp.broadcast_to(info[:, k : k + 1], (info.shape[0], LANES))


def halves_in(number):
    return sum((number > 64.0 * q).astype(I32) for q in range(4))


def list_halves(entries, number, spare, other, half_at, spare_given=0, given_at=(0, 0)):
    lane = lax.broadcasted_iota(I32, number.shape, 1)
    rows = jnp.full(number.shape, spare, I32)
    givens = jnp.full(number.shape, spare_given, I32)
    east, north = jnp.zeros(number.shape, F32), jnp.zeros(number.shape, F32)
    used = jnp.zeros(number.shape, I32)
    for row, given, a, b, halves in entries:
        moved = used & 1
        row = row + moved * other
        given = given + moved * given_at[0]
        for q in range(4):
            here = (lane == used + q) & (halves > q)
            rows = jnp.where(here, row + (q >> 1) * half_at, rows)
            givens = jnp.where(here, given + (q >> 1) * given_at[1], givens)
        here = (lane >= used) & (lane < used + halves)
        east = jnp.where(here, a, east)
        north = jnp.where(here, b, north)
        used = used + halves
    rows = jnp.where(lane == USED, used, rows)
    rows = jnp.where(lane == LIVE, number.astype(I32), rows)
    return rows, givens, east, north


def turned(values):
    flat = pltpu.roll(values.reshape(-1, LANES), LANES // 2, 1)
    return flat.reshape(values.shape)


def place_of(column, row, me, half):
    low = (column < TX // 2).astype(I32)
    depth = jnp.where(low == 1, column + 1, TX - column)
    k = ((row >> 3) * 2 + 1 - low) ^ me
    return (k & 1) * half + (k >> 1), depth * 8 + (row & 7)


def scale_of(width):
    return jnp.broadcast_to(BASE / (width * width), (width.shape[0], LANES))


def own_columns_kernel(block, mine, columns, east, north, facts, sem):
    copy = pltpu.make_async_copy(mine, facts, sem)
    copy.start()
    scale = scale_of(mine[:, WIDTH : WIDTH + 1])[None]
    east[...] = columns_of(2.0 * scale * block[EAST])
    north[...] = columns_of(2.0 * scale * block[NORTH])

    def number_of(t):
        return facts[t, COUNT].astype(I32)

    spread_columns(block.shape[2], number_of, east, north, columns, copy.wait)


def records(tiles):
    shape = (2, tiles, LANES)
    number = lax.broadcasted_iota(I32, shape, 2) + LANES * lax.broadcasted_iota(I32, shape, 0)
    return number.astype(F32)


def columns_of(rows):
    pad = jnp.zeros((64 - rows.shape[1], LANES), F32)
    return jnp.concatenate([rows[0], pad, rows[1], pad], axis=0).T


def rows_of(low, high, tiles):
    low, high = low.T, high.T
    return [jnp.stack([low[k : k + tiles], high[k : k + tiles]]) for k in (0, 64)]


def spread_columns(tiles, number_of, east, north, columns, ready=None):
    def lay(t, nb, values):
        i = (nb >> 1) * 64 + t
        for k, value in enumerate(values):
            wide = jnp.broadcast_to(value[:, i : i + 1], (64, LANES))
            columns[t, k, nb * 64 : nb * 64 + 64, :] = wide

    low = (east[0:64, :], north[0:64, :])
    for t in range(tiles):
        lay(t, 0, low)
    if ready is not None:
        ready()
    for t in range(tiles):
        number = number_of(t)

        @pl.when(number > 64)
        def _():
            lay(t, 1, (east[64:128, :], north[64:128, :]))

        @pl.when(number > 128)
        def _():
            lay(t, 2, (east[0:64, :], north[0:64, :]))
            lay(t, 3, (east[64:128, :], north[64:128, :]))


SHARE = 3
GROUP = 4


def collect_sums(parts, number_of, low_ref, high_ref, large):
    split_at = (lax.broadcasted_iota(I32, (4 * LANES, LANES), 0) // LANES) & 1
    sides = lax.broadcasted_iota(I32, (4 * LANES, LANES), 1) // 64
    ones = (split_at == sides).astype(F32).astype(jnp.bfloat16)
    place = lax.broadcasted_iota(I32, (64, LANES), 1)
    lane = place & 63

    def total(values):
        high = values.astype(jnp.bfloat16)
        low = (values - high.astype(F32)).astype(jnp.bfloat16)
        return jnp.dot(jnp.concatenate([high, low], axis=1), ones, preferred_element_type=F32)

    for nb in range(2):
        result = jnp.zeros((64, LANES), F32)
        held = [(sums, t) for sums, tiles in parts for t in range(tiles)]
        for i, (sums, t) in enumerate(held):
            values = sums[t, nb * 64 : nb * 64 + 64, :]
            if i % SHARE == SHARE - 1:
                for k in range(2):
                    x = jnp.sum(values[:, k * LANES : (k + 1) * LANES], axis=1, keepdims=True)
                    result = jnp.where(place == k * 64 + i, x, result)
            else:
                result = jnp.where(lane == i, total(values), result)
        low_ref[nb * 64 : nb * 64 + 64, :] = result
    high_ref[...] = jnp.zeros_like(high_ref)

    start = 0
    for sums, tiles in parts:
        many = jnp.int32(0)
        for t in range(tiles):
            large[many] = jnp.int32(t)
            many = many + (number_of(start + t) > 128).astype(I32)
        last = large[jnp.maximum(many - 1, 0)]
        for k in range(GROUP - 1):
            large[many + k] = last

        def some(g, carry, sums=sums, start=start):
            result = high_ref[...]
            for i in range(GROUP):
                t = large[g * GROUP + i]
                mine = (lax.broadcasted_iota(I32, (LANES, LANES), 1) & 63) == start + t
                result = jnp.where(mine, total(sums[t, 128:256, :]), result)
            high_ref[...] = result
            return carry

        lax.fori_loop(0, (many + GROUP - 1) // GROUP, some, 0)
        start += tiles


def sweep_tile(t, at_column, scale, columns, sums, words, steps, rows_for):
    scale = jnp.broadcast_to(scale, (8, LANES))
    left = lax.broadcasted_iota(I32, (8, LANES), 1) < LANES // 2

    def chunk(i):
        sides = []
        for k in range(2):
            u, v, c, d = [jnp.broadcast_to(row, (8, LANES)) for row in rows_for(t, i + k)]
            sides.append((u + steps[0, t, i + k], v + steps[1, t, i + k], c, d))
        u, v, c, d = [jnp.where(left, *pair) for pair in zip(*sides)]
        fade = jnp.exp2(-scale * (u * u + v * v))
        return u, v, c * c * fade, d * fade

    def block(nb, size, step):
        at = pl.ds(pl.multiple_of(nb * 64, 64), size)
        x = columns[at_column, 0, at, :].reshape(size // 8, 8, LANES)
        y = columns[at_column, 1, at, :].reshape(size // 8, 8, LANES)

        def some(p, sums_now):
            den, num = sums_now
            for k in range(step):
                u, v, c, d = chunk(2 * (step * p + k))
                w = jnp.exp2(x * u + y * v)
                den = den + w * c
                num = num + w * d
            return den, num

        zero = jnp.zeros((size // 8, 8, LANES), F32)
        trips = (words[0, t, USED] + 2 * step - 1) // (2 * step)
        den, num = lax.fori_loop(0, trips, some, (zero, zero))
        sums[t, at, 0:LANES] = den.reshape(size, LANES)
        sums[t, at, LANES : 2 * LANES] = num.reshape(size, LANES)

    number = words[0, t, LIVE]
    whole = (number + 31) >> 6

    def full(nb, carry):
        block(nb, 64, 2)
        return carry

    lax.fori_loop(0, whole, full, 0)

    @pl.when(number > whole * 64)
    def _():
        block(whole, 32, 4)


def first_lists(near_info, edge_info, rows, groups, fields, plane):
    me = lax.axis_index("tile")
    odd = me & 1
    first = (me >> 1) * 8
    near_live = column_of(near_info, COUNT)
    if edge_info is not None:
        edge_live = column_of(edge_info, COUNT)
    step = lax.broadcasted_iota(I32, (8, LANES), 0)
    on_map = [(first > 0).astype(F32), (first + 8 < rows).astype(F32)]
    lines = []
    for u in range(5):
        if u < 2 and edge_info is None:
            lines.append(None)
            continue
        if u < 2:
            away = 1 - u
            parts = [edge_live[i : i + n] for i, n in ((16 + 2 * away, 1), (8 * away, 8), (17 + 2 * away, 1))]
        else:
            parts = [near_live[10 * (u - 2) + i : 10 * (u - 2) + i + n] for i, n in ((0, 1), (1, 8), (9, 1))]
        lines.append(jnp.concatenate([parts[0] * on_map[0], parts[1], parts[2] * on_map[1]], axis=0))

    def source(u, b):
        if u >= 2:
            return (u - 2) * 10 + 1 + b + step
        start = NEAR_ROWS + 8 * (1 - u)
        at = start + b + step
        if b == 0:
            return at
        corner = NEAR_ROWS + 16 + 2 * (1 - u) + (b + 1) // 2
        return jnp.where(step == (0 if b < 0 else 7), corner, at)

    result = []
    infos = (None if edge_info is None else edge_info[0:8], near_info[1:9], near_info[11:19])
    for j, info in enumerate(infos):
        if info is None or (edge_info is None and j not in groups):
            continue
        entries = []
        for du in (-1, 0, 1) if j in groups else ():
            for b in (-1, 0, 1):
                here, there = 3 * (du + 1) + b + 1, 3 * (1 - du) + b + 1
                a = jnp.where(odd == 1, -du, du).astype(F32)
                chunks = halves_in(lines[j + 1 + du][1 + b : 9 + b])
                if here != 4:
                    taken = jnp.where(odd == 1, column_of(info, REACH + there), column_of(info, REACH + here))
                    chunks = jnp.where(taken > 0.5, chunks, 0)
                entries.append((source(j + 1 + du, b), 0, a, jnp.float32(b), chunks))
        moved = 2 * fields * plane
        result.append(list_halves(entries, column_of(info, COUNT), SPARE, moved, plane))
    return [jnp.concatenate(parts, axis=0) for parts in zip(*result)]


def first_kernel(
    near, near_columns, near_sums, border, out,
    table, own, east, north, low, high, columns, sums, listed, stepped,
    words, steps, large, sem, word_sem,
):
    rows = lax.axis_size("tile") * SLOTS // TX
    near_at, edge_at = pl.ds(0, NEAR_ROWS), pl.ds(NEAR_ROWS, EDGE_ROWS)
    copies = [
        pltpu.make_async_copy(near.at[pl.ds(0, 6)], table.at[pl.ds(0, 6), :, near_at], sem)
    ]
    for f, field in enumerate((EAST, NORTH, ONE, PART)):
        held = border.at[:, pl.ds(f * 24, 24)]
        copies.append(pltpu.make_async_copy(held, table.at[field, :, edge_at], sem))
    for f, field in enumerate((TWO, PRICE)):
        held = border.at[:, pl.ds(120 + 8 * f, 8)]
        copies.append(pltpu.make_async_copy(held, table.at[field, :, pl.ds(NEAR_ROWS, 8)], sem))
    for copy in copies:
        copy.start()
    near_info, edge_info = near[INFO, 0], border[0, 4 * 24 : 5 * 24, :]
    listed[0], _, stepped[0], stepped[1] = first_lists(
        near_info, edge_info, rows, (0, 1), 5, NEAR_ROWS + EDGE_ROWS
    )
    word_copies = [
        pltpu.make_async_copy(listed, words, word_sem),
        pltpu.make_async_copy(stepped, steps, word_sem),
    ]
    for copy in word_copies:
        copy.start()
    tiles = 24
    info = jnp.concatenate([edge_info[0:8], near_info[1:9], near_info[11:19]], axis=0)
    scales = scale_of(info[:, WIDTH : WIDTH + 1])
    counts = column_of(info, COUNT)
    for copy in copies:
        copy.wait()

    def of_targets(field):
        parts = [table[field, :, 32:40, :], table[field, :, 1:9, :], table[field, :, 11:19, :]]
        return jnp.concatenate(parts, axis=1)

    present = records(tiles) < counts[None]
    scale_rows = scales[None]
    own[...] = scales
    x, y = of_targets(EAST), of_targets(NORTH)
    east[...] = columns_of(2.0 * scale_rows[:, 0:8] * x[:, 0:8])
    north[...] = columns_of(2.0 * scale_rows[:, 0:8] * y[:, 0:8])

    def number_of(t):
        return words[0, t, LIVE]

    def ready():
        for copy in word_copies:
            copy.wait()

    spread_columns(8, number_of, east, north, columns, ready)

    table[6:10] = turned(table[EAST : PART + 1])

    plane = 2 * (NEAR_ROWS + EDGE_ROWS)
    flat = table.reshape(10 * plane, LANES)

    def rows_for(t, i):
        row = words[0, t, i]
        return [flat[pl.ds(row + field * plane, 1), :] for field in (EAST, NORTH, ONE, PART)]

    def each(t, carry, held, skip):
        sweep_tile(t, t - skip, own[pl.ds(t, 1), :], held, sums, words, steps, rows_for)
        return carry

    lax.fori_loop(0, 8, lambda t, c: each(t, c, columns, 0), 0)
    lax.fori_loop(8, 16, lambda t, c: each(t, c, near_columns, 8), 0)
    collect_sums([(sums, 16), (near_sums, 8)], number_of, low, high, large)
    shrink = jnp.exp2(-scale_rows * (x * x + y * y))
    den, num = rows_of(low[...], high[...], tiles)
    inv = 1.0 / (1.0 + shrink * den)
    beta = jnp.where(present, shrink * num * inv, 0.0)
    one, two = of_targets(ONE), of_targets(TWO)
    out[:, 0:24, :] = two * (of_targets(PRICE) - one * beta)
    out[:, 24:40, :] = beta[:, 8:24]
    out[:, 40:56, :] = jnp.where(present, one * one * inv, 0.0)[:, 8:24]
    out[:, 56:64, :] = two[:, 0:8]
    out[:, 64:72, :] = x[:, 0:8]
    out[:, 72:80, :] = y[:, 0:8]
    out[:, 80:88, :] = jnp.broadcast_to(counts[0:8][None], (2, 8, LANES))


def second_lists(mine, same, other, same_b, other_b):
    half = same.shape[0]
    cells = 2 * half * SLOTS
    rows = cells // TX
    edge = 2 * half * 8
    padded = -(-edge // LANES) * LANES
    me = lax.axis_index("tile")
    info = jnp.concatenate([x[:, INFO, 0].reshape(half * SLOTS, LANES) for x in (same, other)], axis=0)
    keys = [info[k : k + LANES].T[LABEL : LABEL + 1] + rows for k in range(0, cells, LANES)]
    at = lax.broadcasted_iota(I32, (1, padded), 1)
    n = at >> 3
    device = (((n & (half - 1)) << 1) | (n >= half).astype(I32)) ^ me
    row = (device >> 1) * 8 + (at & 7)
    key = jnp.where((device & 1) == 1, (TX + 1) * rows + row, row)
    keys.append(jnp.where(at < edge, key, -1).astype(F32))
    keys = jnp.concatenate(keys, axis=1)
    total = cells + padded
    edge_live = [x[k, 0, 80:88, :] for x in (same_b, other_b) for k in range(half)]
    if padded > edge:
        edge_live.append(jnp.zeros((padded - edge, LANES), F32))
    live = jnp.concatenate([column_of(info, COUNT), *edge_live], axis=0)
    index = lax.broadcasted_iota(I32, (total, LANES), 0)
    cell = column_of(mine, LABEL).astype(I32)
    column, across = split(cell, rows)
    hot = []
    for a, b in NEAR:
        row = across + b
        wanted = jnp.where((row >= 0) & (row < rows), (column + a + 1) * rows + row, -2).astype(F32)
        parts = [keys[:, k : k + LANES] == wanted for k in range(0, total, LANES)]
        hot.append(jnp.concatenate([p.astype(F32) for p in parts], axis=1))
    hot = jnp.concatenate(hot, axis=0).astype(jnp.bfloat16)

    def look_up(values):
        return jnp.dot(hot, values.astype(F32).astype(jnp.bfloat16), preferred_element_type=F32)

    blocks, slots = look_up(index >> 4), look_up(index & 15)
    lives = look_up(live)
    tiles = mine.shape[0]
    entries = []
    for e, (a, b) in enumerate(NEAR):
        at = slice(e * tiles, (e + 1) * tiles)
        chunks = halves_in(lives[at])
        if e != 4:
            chunks = jnp.where(column_of(mine, REACH + e) > 0.5, chunks, 0)
        row = blocks[at].astype(I32) * (12 * SLOTS) + slots[at].astype(I32)
        n, spot = place_of(column + a, across + b, me, half)
        entries.append((row, n * 64 + spot, jnp.float32(a), jnp.float32(b), chunks))
    count = 2 * half
    spare = (cells + edge) // SLOTS * (12 * SLOTS)
    rows, givens, east, north = list_halves(
        entries, column_of(mine, COUNT), spare, 6 * SLOTS, SLOTS, 24, (count * 64, 32)
    )
    lane = lax.broadcasted_iota(I32, rows.shape, 1)
    n, spot = place_of(column, across, me, half)
    givens = jnp.where(lane == HOLDER, n, givens)
    return rows, jnp.where(lane == HELD_AT, spot, givens), east, north


def second_kernel(
    own_block, mine, columns, same, other, same_b, other_b,
    betas, hats, residual,
    table, given, own, scales, low, high, sums, listed, stepped,
    words, steps, large, sem, word_sem,
):
    copies = fetch(same, other, table, 3, sem)
    half, _, _, tiles, _ = same.shape
    blocks = 2 * half
    for side, held in enumerate((same_b, other_b)):
        at = pl.ds(side * half, half)
        to = given.at[0, at, :, pl.ds(0, 24)]
        copies.append(pltpu.make_async_copy(held.at[:, :, pl.ds(0, 24)], to, sem))
    for copy in copies:
        copy.start()
    listed[0], listed[1], stepped[0], stepped[1] = second_lists(mine, same, other, same_b, other_b)
    word_copies = [
        pltpu.make_async_copy(listed, words, word_sem),
        pltpu.make_async_copy(stepped, steps, word_sem),
    ]
    for copy in word_copies:
        copy.start()
    scales[...] = scale_of(mine[:, WIDTH : WIDTH + 1])
    present = records(tiles) < column_of(mine, COUNT)[None]
    scale_rows = scales[...][None]
    x, y = own_block[EAST], own_block[NORTH]

    def number_of(t):
        return words[0, t, LIVE]

    for n in range(2 * half):
        held = (same_b if n < half else other_b).at[n % half]
        for field in range(3):
            table[blocks + n // 2, field, :, n % 2 * 8 : n % 2 * 8 + 8, :] = held[
                :, 56 + 8 * field : 64 + 8 * field, :
            ]
    for field in range(3):
        table[blocks + half, field, :, 0:8, :] = jnp.zeros((2, 8, LANES), F32)
    given[0, :, :, 24:32, :] = jnp.zeros((2 * half, 2, 8, LANES), F32)
    for copy in copies:
        copy.wait()

    def turn(n, carry):
        table[n, 3:6] = turned(table[n, 0:3])
        return carry

    def turn_given(n, carry):
        given[1, n] = turned(given[0, n])
        return carry

    lax.fori_loop(0, table.shape[0], turn, 0, unroll=True)
    lax.fori_loop(0, 2 * half, turn_given, 0, unroll=True)
    for copy in word_copies:
        copy.wait()

    flat = table.reshape(table.shape[0] * 12 * SLOTS, LANES)
    flat_given = given.reshape(2 * 2 * half * 64, LANES)

    def rows_for(t, i):
        row = words[0, t, i]
        held = [flat[pl.ds(row + field * 2 * SLOTS, 1), :] for field in (EAST, NORTH, TWO)]
        return [*held, flat_given[pl.ds(words[1, t, i], 1), :]]

    def each(t, carry):
        n, at = words[1, t, HOLDER], words[1, t, HELD_AT]
        for k in range(2):
            here = (n & (half - 1), slice(None), pl.ds(16 * (k + 1) + at, 1), slice(None))
            own[k, :, pl.ds(t, 1), :] = jnp.where(n >= half, other_b[here], same_b[here])
        sweep_tile(t, t, scales[pl.ds(t, 1), :], columns, sums, words, steps, rows_for)
        return carry

    lax.fori_loop(0, tiles, each, 0)
    collect_sums([(sums, tiles)], number_of, low, high, large)
    shrink = jnp.exp2(-scale_rows * (x * x + y * y))
    den, num = rows_of(low[...], high[...], tiles)
    inv = 1.0 / (1.0 + shrink * den)
    beta_two = jnp.where(present, shrink * num * inv, 0.0)
    beta_one = own[0]
    one, two = own_block[ONE], own_block[TWO]
    left = jnp.where(present, own_block[PRICE] - one * beta_one - two * beta_two, 0.0)
    hat_two = jnp.where(present, two * two * inv, 0.0)
    for t in range(tiles):
        for h in range(2):
            at = slice(t * TILE + h * LANES, t * TILE + (h + 1) * LANES)
            betas[0:1, at] = beta_one[h, t : t + 1]
            betas[1:2, at] = beta_two[h, t : t + 1]
            hats[0:1, at] = own[1, h, t : t + 1, :]
            hats[1:2, at] = hat_two[h, t : t + 1]
            residual[0:1, at] = left[h, t : t + 1]


def swap(x, k):
    count = lax.axis_size("tile")
    return lax.ppermute(x, "tile", [(i, i ^ k) for i in range(count)])


def spread(block, beside=None):
    count = lax.axis_size("tile")
    same = jnp.stack([block] + [swap(block, k) for k in range(2, count, 2)])
    if beside is None:
        return same, swap(same, 1)
    same, beside = lax.optimization_barrier((same, beside))
    return same, swap(same, 1), beside


def body(offsets, design, target, beta_second, counts, kernel_width, reach, assignment):
    tiles = counts.shape[0]
    count = lax.axis_size("tile")
    regions = lax.axis_size("region")
    cells = tiles * count
    limit = pltpu.CompilerParams(vmem_limit_bytes=24 * 1024 * 1024)
    price = target.reshape(1, -1)
    wide = tiles * TILE
    given = (
        offsets, design, price, beta_second.reshape(1, -1),
        counts, kernel_width, reach.transpose(2, 0, 1), assignment,
    )
    block, mine = pl.pallas_call(
        prepare_kernel,
        out_shape=(
            pltpu.VMEM((7, 2, tiles, LANES), F32),
            pltpu.VMEM((tiles, LANES), F32),
        ),
        in_specs=[pl.BlockSpec(memory_space=pltpu.HBM)] * 8,
        out_specs=(VMEM, VMEM),
        scratch_shapes=[pltpu.VMEM((2, wide), F32)] * 2
        + [pltpu.VMEM((1, wide), F32)] * 2
        + [
            pltpu.SMEM((tiles,), I32),
            pltpu.SMEM((2, tiles), I32),
            pltpu.SMEM((9, 2, tiles), I32),
            pltpu.SMEM((1, tiles), I32),
            pltpu.SemaphoreType.DMA,
        ],
        compiler_params=limit,
    )(*[pltpu.with_memory_space_constraint(x, pltpu.HBM) for x in given])
    square = pltpu.VMEM((LANES, LANES), F32)
    dma = pltpu.SemaphoreType.DMA
    own_columns = pl.pallas_call(
        own_columns_kernel,
        out_shape=pltpu.VMEM((tiles, 2, TILE, LANES), F32),
        in_specs=[VMEM, VMEM],
        out_specs=VMEM,
        scratch_shapes=[square, square, pltpu.SMEM((tiles, LANES), F32), dma],
        compiler_params=limit,
        cost_estimate=pl.CostEstimate(flops=4000000, bytes_accessed=4000000, transcendentals=0),
    )(block, mine)
    same, other, own_columns = spread(block, own_columns)
    edge, near = pl.pallas_call(
        border_kernel,
        out_shape=(
            jax.ShapeDtypeStruct((2, 136, LANES), F32),
            pltpu.VMEM((7, 2, NEAR_ROWS, LANES), F32),
        ),
        in_specs=[VMEM, VMEM],
        out_specs=(VMEM, VMEM),
        compiler_params=limit,
    )(same, other)
    near_columns, near_sums = pl.pallas_call(
        near_kernel,
        out_shape=(
            pltpu.VMEM((16, 2, TILE, LANES), F32),
            pltpu.VMEM((8, TILE, 2 * LANES), F32),
        ),
        in_specs=[VMEM],
        out_specs=(VMEM, VMEM),
        scratch_shapes=[
            pltpu.VMEM((8, 2, NEAR_ROWS, LANES), F32),
            pltpu.VMEM((16, LANES), F32),
            square,
            square,
            pltpu.VMEM((1, 8, LANES), I32),
            pltpu.VMEM((2, 8, LANES), F32),
            pltpu.SMEM((NEAR_ROWS, LANES), F32),
            pltpu.SMEM((1, 8, LANES), I32),
            pltpu.SMEM((2, 8, LANES), F32),
            dma,
            dma,
        ],
        compiler_params=limit,
        cost_estimate=pl.CostEstimate(flops=4000000, bytes_accessed=4000000, transcendentals=0),
    )(near)
    moves = []
    for r in range(regions):
        for t in range(count):
            to = r + 1 - 2 * (t % 2)
            if 0 <= to < regions:
                moves.append((r * count + t, to * count + t))
    border = lax.ppermute(edge, ("region", "tile"), moves)
    first = pl.pallas_call(
        first_kernel,
        out_shape=jax.ShapeDtypeStruct((2, 88, LANES), F32),
        in_specs=[VMEM] * 4,
        out_specs=VMEM,
        scratch_shapes=[
            pltpu.VMEM((10, 2, NEAR_ROWS + EDGE_ROWS, LANES), F32),
            pltpu.VMEM((24, LANES), F32),
            square,
            square,
            square,
            square,
            pltpu.VMEM((8, 2, TILE, LANES), F32),
            pltpu.VMEM((16, TILE, 2 * LANES), F32),
            pltpu.VMEM((1, 24, LANES), I32),
            pltpu.VMEM((2, 24, LANES), F32),
            pltpu.SMEM((1, 24, LANES), I32),
            pltpu.SMEM((2, 24, LANES), F32),
            pltpu.SMEM((24,), I32),
            dma,
            dma,
        ],
        compiler_params=limit,
    )(near, near_columns, near_sums, border)
    same_b, other_b = spread(first)
    betas, hats, residual = pl.pallas_call(
        second_kernel,
        out_shape=(
            jax.ShapeDtypeStruct((2, wide), F32),
            jax.ShapeDtypeStruct((2, wide), F32),
            jax.ShapeDtypeStruct((1, wide), F32),
        ),
        in_specs=[VMEM] * 7,
        out_specs=(VMEM, VMEM, VMEM),
        scratch_shapes=[
            pltpu.VMEM((count + count // 2 + 1, 6, 2, tiles, LANES), F32),
            pltpu.VMEM((2, count, 2, 32, LANES), F32),
            pltpu.VMEM((2, 2, tiles, LANES), F32),
            pltpu.VMEM((tiles, LANES), F32),
            square,
            square,
            pltpu.VMEM((tiles, TILE, 2 * LANES), F32),
            pltpu.VMEM((2, tiles, LANES), I32),
            pltpu.VMEM((2, tiles, LANES), F32),
            pltpu.SMEM((2, tiles, LANES), I32),
            pltpu.SMEM((2, tiles, LANES), F32),
            pltpu.SMEM((24,), I32),
            dma,
            dma,
        ],
        compiler_params=limit,
    )(block, mine, own_columns, same, other, same_b, other_b)
    return (betas, hats, residual.reshape(-1))


def solution(mesh):
    in_specs = (
        P(None, ("region", "tile")),
        P(None, ("region", "tile")),
        P(("region", "tile")),
        P(("region", "tile")),
        P(("region", "tile")),
        P(None, ("region", "tile")),
        P(None, ("region", "tile"), None),
        P("region", "tile"),
    )
    out_specs = (P(None, ("region", "tile")), P(None, ("region", "tile")), P(("region", "tile")))
    return jax.shard_map(body, mesh=mesh, in_specs=in_specs, out_specs=out_specs, check_vma=False)
```

```python
import functools

import jax
import jax.numpy as jnp
from jax import lax
from jax.experimental import pallas as pl
from jax.experimental.pallas import tpu as pltpu
from jax.sharding import PartitionSpec as P

TILE = 256
TX = 4
LANES = 128
TWO, EAST, NORTH, ONE, PART, PRICE, INFO = range(7)
SLOTS = 16
BASE = 32.0 * 1.4426950408889634
LABEL, COUNT, WIDTH, REACH = 0, 1, 2, 3
NEAR = [(a, b) for a in (-1, 0, 1) for b in (-1, 0, 1)]
F32, I32 = jnp.float32, jnp.int32
ANY = pl.BlockSpec(memory_space=pl.ANY)
SMEM = pl.BlockSpec(memory_space=pltpu.SMEM)
VMEM = pl.BlockSpec(memory_space=pltpu.VMEM)


def prepare_kernel(*refs):
    given, (out, mine), held, sem = refs[:8], refs[8:10], refs[10:18], refs[18]
    copies = [pltpu.make_async_copy(a, b, sem) for a, b in zip(given, held)]
    for copy in copies:
        copy.start()
    for copy in copies:
        copy.wait()
    off, des, tgt, sec, counts, widths, reach, cells = held
    lane = lax.broadcasted_iota(I32, (1, LANES), 1)
    for t in range(counts.shape[0]):
        row = jnp.zeros((1, LANES), F32)
        facts = [cells[0, t], counts[t], widths[0, t]] + [reach[e, 0, t] for e in range(9)]
        for k, fact in enumerate(facts):
            row = jnp.where(lane == k, fact.astype(F32), row)
        out[INFO, 0, t : t + 1, :] = row
        for k, value in enumerate([widths[1, t]] + [reach[e, 1, t] for e in range(9)]):
            row = jnp.where(lane == WIDTH + k, value.astype(F32), row)
        mine[t : t + 1, :] = row
        for h in range(2):
            at = slice(t * TILE + h * LANES, t * TILE + (h + 1) * LANES)
            live = lane + h * LANES < counts[t]
            one = jnp.where(live, des[0:1, at], 0.0)
            two = jnp.where(live, des[1:2, at], 0.0)
            price = tgt[0:1, at]
            out[EAST, h, t : t + 1, :] = off[0:1, at] - 0.5
            out[NORTH, h, t : t + 1, :] = off[1:2, at] - 0.5
            out[ONE, h, t : t + 1, :] = one
            out[PART, h, t : t + 1, :] = one * (price - two * sec[0:1, at])
            out[TWO, h, t : t + 1, :] = two
            out[PRICE, h, t : t + 1, :] = price
    out[INFO, 1] = jnp.zeros_like(out[INFO, 1])


def split(number, size):
    return number >> (size.bit_length() - 1), number & (size - 1)


def fetch(same, other, table, fields, sem):
    half = same.shape[0]
    return [
        pltpu.make_async_copy(
            held.at[:, pl.ds(0, fields)], table.at[pl.ds(side * half, half), pl.ds(0, fields)], sem
        )
        for side, held in enumerate((same, other))
    ]


ORDER = [(0, r) for r in range(1, 9)] + [(1, r) for r in range(1, 9)]
ORDER += [(0, 0), (0, 9), (1, 0), (1, 9)]
NEAR_ROWS, EDGE_ROWS, SPARE = 32, 24, 30


def wanted_cells(rows):
    me = lax.axis_index("tile")
    odd = me & 1
    first = (me >> 1) * 8
    i = lax.broadcasted_iota(I32, (64, LANES), 0)
    u = (i >= 10).astype(I32) + (i >= 20).astype(I32)
    j = i - NEAR_ROWS
    away = jnp.where(j < 16, j >> 3, (j >> 1) & 1)
    own = i < NEAR_ROWS
    r = jnp.where(own, i - 10 * u, jnp.where(j < 16, (j & 7) + 1, (j & 1) * 9))
    low = jnp.where(own, u, TX - 1 - away)
    column = jnp.where(odd == 1, TX - 1 - low, low)
    cell = column * rows + jnp.clip(first + r - 1, 0, rows - 1)
    none = (i == SPARE) | (i == SPARE + 1) | (j >= len(ORDER))
    return jnp.where(none, -1, cell).astype(F32)


def border_kernel(same, other, out, near):
    half = same.shape[0]
    cells = 2 * half * SLOTS

    def plane(field, h):
        parts = [x[:, field, h].reshape(half * SLOTS, LANES) for x in (same, other)]
        return jnp.concatenate(parts, axis=0)

    info = plane(INFO, 0)
    wanted = wanted_cells(cells // TX)
    hot = []
    for k in range(0, cells, LANES):
        labels = info[k : k + LANES].T[LABEL : LABEL + 1]
        hot.append((jnp.broadcast_to(labels, wanted.shape) == wanted).astype(F32))
    hot = jnp.concatenate(hot, axis=1).astype(jnp.bfloat16)

    def pick(values, pieces):
        total = jnp.zeros((64, LANES), F32)
        for _ in range(pieces):
            piece = values.astype(jnp.bfloat16)
            values = values - piece.astype(F32)
            total = total + jnp.dot(hot, piece, preferred_element_type=F32)
        return total

    for field in (EAST, NORTH, ONE, PART, INFO, TWO, PRICE):
        for h in range(2):
            if field != INFO:
                got = pick(plane(field, h), 3)
            elif h == 0:
                got = pick(info, 1)
            near[field, h] = got[0:NEAR_ROWS]
            edge = got[NEAR_ROWS : NEAR_ROWS + EDGE_ROWS]
            if field in (TWO, PRICE):
                f = (TWO, PRICE).index(field)
                out[h, 120 + 8 * f : 128 + 8 * f, :] = edge[0:8]
            else:
                f = (EAST, NORTH, ONE, PART, INFO).index(field)
                out[h, f * 24 : f * 24 + 24, :] = edge


def targets_of(near, field):
    return jnp.concatenate([near[field, :, 1:9, :], near[field, :, 11:19, :]], axis=1)


def near_kernel(
    near, columns, sums,
    table, own, east, north, listed, stepped, facts, words, steps, sem, word_sem,
):
    copy = pltpu.make_async_copy(near.at[INFO, 0], facts, sem)
    copy.start()
    rows = lax.axis_size("tile") * SLOTS // TX
    near_info = near[INFO, 0]
    listed[0], _, stepped[0], stepped[1] = first_lists(near_info, None, rows, (2,), 4, NEAR_ROWS)
    word_copies = [
        pltpu.make_async_copy(listed, words, word_sem),
        pltpu.make_async_copy(stepped, steps, word_sem),
    ]
    for word_copy in word_copies:
        word_copy.start()
    info = targets_of(near, INFO)[0]
    own[...] = scale_of(info[:, WIDTH : WIDTH + 1])
    scale = own[...][None]
    east[...] = columns_of(2.0 * scale * targets_of(near, EAST))
    north[...] = columns_of(2.0 * scale * targets_of(near, NORTH))
    table[0:4] = near[EAST : PART + 1]
    table[4:8] = turned(near[EAST : PART + 1])

    def number_of(t):
        return facts[(t >> 3) * 10 + (t & 7) + 1, COUNT].astype(I32)

    spread_columns(16, number_of, east, north, columns, copy.wait)
    for word_copy in word_copies:
        word_copy.wait()
    flat = table.reshape(16 * NEAR_ROWS, LANES)

    def rows_for(t, i):
        row = words[0, t, i]
        return [flat[pl.ds(row + k * 2 * NEAR_ROWS, 1), :] for k in range(4)]

    def each(t, carry):
        sweep_tile(t, t + 8, own[pl.ds(t + 8, 1), :], columns, sums, words, steps, rows_for)
        return carry

    lax.fori_loop(0, 8, each, 0)


USED, LIVE, HOLDER, HELD_AT = 100, 101, 102, 103


def column_of(info, k):
    return jnp.broadcast_to(info[:, k : k + 1], (info.shape[0], LANES))


def halves_in(number):
    return sum((number > 64.0 * q).astype(I32) for q in range(4))


def list_halves(entries, number, spare, other, half_at, spare_given=0, given_at=(0, 0)):
    lane = lax.broadcasted_iota(I32, number.shape, 1)
    rows = jnp.full(number.shape, spare, I32)
    givens = jnp.full(number.shape, spare_given, I32)
    east, north = jnp.zeros(number.shape, F32), jnp.zeros(number.shape, F32)
    used = jnp.zeros(number.shape, I32)
    for row, given, a, b, halves in entries:
        moved = used & 1
        row = row + moved * other
        given = given + moved * given_at[0]
        for q in range(4):
            here = (lane == used + q) & (halves > q)
            rows = jnp.where(here, row + (q >> 1) * half_at, rows)
            givens = jnp.where(here, given + (q >> 1) * given_at[1], givens)
        here = (lane >= used) & (lane < used + halves)
        east = jnp.where(here, a, east)
        north = jnp.where(here, b, north)
        used = used + halves
    rows = jnp.where(lane == USED, used, rows)
    rows = jnp.where(lane == LIVE, number.astype(I32), rows)
    return rows, givens, east, north


def turned(values):
    flat = pltpu.roll(values.reshape(-1, LANES), LANES // 2, 1)
    return flat.reshape(values.shape)


def place_of(column, row, me, half):
    low = (column < TX // 2).astype(I32)
    depth = jnp.where(low == 1, column + 1, TX - column)
    k = ((row >> 3) * 2 + 1 - low) ^ me
    return (k & 1) * half + (k >> 1), depth * 8 + (row & 7)


def scale_of(width):
    return jnp.broadcast_to(BASE / (width * width), (width.shape[0], LANES))


def own_columns_kernel(block, mine, columns, east, north, facts, sem):
    copy = pltpu.make_async_copy(mine, facts, sem)
    copy.start()
    scale = scale_of(mine[:, WIDTH : WIDTH + 1])[None]
    east[...] = columns_of(2.0 * scale * block[EAST])
    north[...] = columns_of(2.0 * scale * block[NORTH])

    def number_of(t):
        return facts[t, COUNT].astype(I32)

    spread_columns(block.shape[2], number_of, east, north, columns, copy.wait)


def records(tiles):
    shape = (2, tiles, LANES)
    number = lax.broadcasted_iota(I32, shape, 2) + LANES * lax.broadcasted_iota(I32, shape, 0)
    return number.astype(F32)


def columns_of(rows):
    pad = jnp.zeros((64 - rows.shape[1], LANES), F32)
    return jnp.concatenate([rows[0], pad, rows[1], pad], axis=0).T


def rows_of(low, high, tiles):
    low, high = low.T, high.T
    return [jnp.stack([low[k : k + tiles], high[k : k + tiles]]) for k in (0, 64)]


def spread_columns(tiles, number_of, east, north, columns, ready=None):
    def lay(t, nb, values):
        i = (nb >> 1) * 64 + t
        for k, value in enumerate(values):
            wide = jnp.broadcast_to(value[:, i : i + 1], (64, LANES))
            columns[t, k, nb * 64 : nb * 64 + 64, :] = wide

    low = (east[0:64, :], north[0:64, :])
    for t in range(tiles):
        lay(t, 0, low)
    if ready is not None:
        ready()
    for t in range(tiles):
        number = number_of(t)

        @pl.when(number > 64)
        def _():
            lay(t, 1, (east[64:128, :], north[64:128, :]))

        @pl.when(number > 128)
        def _():
            lay(t, 2, (east[0:64, :], north[0:64, :]))
            lay(t, 3, (east[64:128, :], north[64:128, :]))


SHARE = 2
GROUP = 4


def collect_sums(parts, number_of, low_ref, high_ref, large):
    split_at = (lax.broadcasted_iota(I32, (4 * LANES, LANES), 0) // LANES) & 1
    sides = lax.broadcasted_iota(I32, (4 * LANES, LANES), 1) // 64
    ones = (split_at == sides).astype(F32).astype(jnp.bfloat16)
    place = lax.broadcasted_iota(I32, (64, LANES), 1)
    lane = place & 63

    def total(values):
        high = values.astype(jnp.bfloat16)
        low = (values - high.astype(F32)).astype(jnp.bfloat16)
        return jnp.dot(jnp.concatenate([high, low], axis=1), ones, preferred_element_type=F32)

    for nb in range(2):
        result = jnp.zeros((64, LANES), F32)
        held = [(sums, t) for sums, tiles in parts for t in range(tiles)]
        for i, (sums, t) in enumerate(held):
            values = sums[t, nb * 64 : nb * 64 + 64, :]
            if i % SHARE == SHARE - 1:
                for k in range(2):
                    x = jnp.sum(values[:, k * LANES : (k + 1) * LANES], axis=1, keepdims=True)
                    result = jnp.where(place == k * 64 + i, x, result)
            else:
                result = jnp.where(lane == i, total(values), result)
        low_ref[nb * 64 : nb * 64 + 64, :] = result
    high_ref[...] = jnp.zeros_like(high_ref)

    start = 0
    for sums, tiles in parts:
        many = jnp.int32(0)
        for t in range(tiles):
            large[many] = jnp.int32(t)
            many = many + (number_of(start + t) > 128).astype(I32)
        last = large[jnp.maximum(many - 1, 0)]
        for k in range(GROUP - 1):
            large[many + k] = last

        def some(g, carry, sums=sums, start=start):
            result = high_ref[...]
            for i in range(GROUP):
                t = large[g * GROUP + i]
                mine = (lax.broadcasted_iota(I32, (LANES, LANES), 1) & 63) == start + t
                result = jnp.where(mine, total(sums[t, 128:256, :]), result)
            high_ref[...] = result
            return carry

        lax.fori_loop(0, (many + GROUP - 1) // GROUP, some, 0)
        start += tiles


def sweep_tile(t, at_column, scale, columns, sums, words, steps, rows_for):
    scale = jnp.broadcast_to(scale, (8, LANES))
    left = lax.broadcasted_iota(I32, (8, LANES), 1) < LANES // 2

    def chunk(i):
        sides = []
        for k in range(2):
            u, v, c, d = [jnp.broadcast_to(row, (8, LANES)) for row in rows_for(t, i + k)]
            sides.append((u + steps[0, t, i + k], v + steps[1, t, i + k], c, d))
        u, v, c, d = [jnp.where(left, *pair) for pair in zip(*sides)]
        fade = jnp.exp2(-scale * (u * u + v * v))
        return u, v, c * c * fade, d * fade

    def block(nb, size, step):
        at = pl.ds(pl.multiple_of(nb * 64, 64), size)
        x = columns[at_column, 0, at, :].reshape(size // 8, 8, LANES)
        y = columns[at_column, 1, at, :].reshape(size // 8, 8, LANES)

        def some(p, sums_now):
            den, num = sums_now
            for k in range(step):
                u, v, c, d = chunk(2 * (step * p + k))
                w = jnp.exp2(x * u + y * v)
                den = den + w * c
                num = num + w * d
            return den, num

        zero = jnp.zeros((size // 8, 8, LANES), F32)
        trips = (words[0, t, USED] + 2 * step - 1) // (2 * step)
        den, num = lax.fori_loop(0, trips, some, (zero, zero))
        sums[t, at, 0:LANES] = den.reshape(size, LANES)
        sums[t, at, LANES : 2 * LANES] = num.reshape(size, LANES)

    number = words[0, t, LIVE]
    whole = (number + 31) >> 6

    def full(nb, carry):
        block(nb, 64, 2)
        return carry

    lax.fori_loop(0, whole, full, 0)

    @pl.when(number > whole * 64)
    def _():
        block(whole, 32, 4)


def first_lists(near_info, edge_info, rows, groups, fields, plane):
    me = lax.axis_index("tile")
    odd = me & 1
    first = (me >> 1) * 8
    near_live = column_of(near_info, COUNT)
    if edge_info is not None:
        edge_live = column_of(edge_info, COUNT)
    step = lax.broadcasted_iota(I32, (8, LANES), 0)
    on_map = [(first > 0).astype(F32), (first + 8 < rows).astype(F32)]
    lines = []
    for u in range(5):
        if u < 2 and edge_info is None:
            lines.append(None)
            continue
        if u < 2:
            away = 1 - u
            parts = [edge_live[i : i + n] for i, n in ((16 + 2 * away, 1), (8 * away, 8), (17 + 2 * away, 1))]
        else:
            parts = [near_live[10 * (u - 2) + i : 10 * (u - 2) + i + n] for i, n in ((0, 1), (1, 8), (9, 1))]
        lines.append(jnp.concatenate([parts[0] * on_map[0], parts[1], parts[2] * on_map[1]], axis=0))

    def source(u, b):
        if u >= 2:
            return (u - 2) * 10 + 1 + b + step
        start = NEAR_ROWS + 8 * (1 - u)
        at = start + b + step
        if b == 0:
            return at
        corner = NEAR_ROWS + 16 + 2 * (1 - u) + (b + 1) // 2
        return jnp.where(step == (0 if b < 0 else 7), corner, at)

    result = []
    infos = (None if edge_info is None else edge_info[0:8], near_info[1:9], near_info[11:19])
    for j, info in enumerate(infos):
        if info is None or (edge_info is None and j not in groups):
            continue
        entries = []
        for du in (-1, 0, 1) if j in groups else ():
            for b in (-1, 0, 1):
                here, there = 3 * (du + 1) + b + 1, 3 * (1 - du) + b + 1
                a = jnp.where(odd == 1, -du, du).astype(F32)
                chunks = halves_in(lines[j + 1 + du][1 + b : 9 + b])
                if here != 4:
                    taken = jnp.where(odd == 1, column_of(info, REACH + there), column_of(info, REACH + here))
                    chunks = jnp.where(taken > 0.5, chunks, 0)
                entries.append((source(j + 1 + du, b), 0, a, jnp.float32(b), chunks))
        moved = 2 * fields * plane
        result.append(list_halves(entries, column_of(info, COUNT), SPARE, moved, plane))
    return [jnp.concatenate(parts, axis=0) for parts in zip(*result)]


def first_kernel(
    near, near_columns, near_sums, border, out,
    table, own, east, north, low, high, columns, sums, listed, stepped,
    words, steps, large, sem, word_sem,
):
    rows = lax.axis_size("tile") * SLOTS // TX
    near_at, edge_at = pl.ds(0, NEAR_ROWS), pl.ds(NEAR_ROWS, EDGE_ROWS)
    copies = [
        pltpu.make_async_copy(near.at[pl.ds(0, 6)], table.at[pl.ds(0, 6), :, near_at], sem)
    ]
    for f, field in enumerate((EAST, NORTH, ONE, PART)):
        held = border.at[:, pl.ds(f * 24, 24)]
        copies.append(pltpu.make_async_copy(held, table.at[field, :, edge_at], sem))
    for f, field in enumerate((TWO, PRICE)):
        held = border.at[:, pl.ds(120 + 8 * f, 8)]
        copies.append(pltpu.make_async_copy(held, table.at[field, :, pl.ds(NEAR_ROWS, 8)], sem))
    for copy in copies:
        copy.start()
    near_info, edge_info = near[INFO, 0], border[0, 4 * 24 : 5 * 24, :]
    listed[0], _, stepped[0], stepped[1] = first_lists(
        near_info, edge_info, rows, (0, 1), 5, NEAR_ROWS + EDGE_ROWS
    )
    word_copies = [
        pltpu.make_async_copy(listed, words, word_sem),
        pltpu.make_async_copy(stepped, steps, word_sem),
    ]
    for copy in word_copies:
        copy.start()
    tiles = 24
    info = jnp.concatenate([edge_info[0:8], near_info[1:9], near_info[11:19]], axis=0)
    scales = scale_of(info[:, WIDTH : WIDTH + 1])
    counts = column_of(info, COUNT)
    for copy in copies:
        copy.wait()

    def of_targets(field):
        parts = [table[field, :, 32:40, :], table[field, :, 1:9, :], table[field, :, 11:19, :]]
        return jnp.concatenate(parts, axis=1)

    present = records(tiles) < counts[None]
    scale_rows = scales[None]
    own[...] = scales
    x, y = of_targets(EAST), of_targets(NORTH)
    east[...] = columns_of(2.0 * scale_rows[:, 0:8] * x[:, 0:8])
    north[...] = columns_of(2.0 * scale_rows[:, 0:8] * y[:, 0:8])

    def number_of(t):
        return words[0, t, LIVE]

    def ready():
        for copy in word_copies:
            copy.wait()

    spread_columns(8, number_of, east, north, columns, ready)

    table[6:10] = turned(table[EAST : PART + 1])

    plane = 2 * (NEAR_ROWS + EDGE_ROWS)
    flat = table.reshape(10 * plane, LANES)

    def rows_for(t, i):
        row = words[0, t, i]
        return [flat[pl.ds(row + field * plane, 1), :] for field in (EAST, NORTH, ONE, PART)]

    def each(t, carry, held, skip):
        sweep_tile(t, t - skip, own[pl.ds(t, 1), :], held, sums, words, steps, rows_for)
        return carry

    lax.fori_loop(0, 8, lambda t, c: each(t, c, columns, 0), 0)
    lax.fori_loop(8, 16, lambda t, c: each(t, c, near_columns, 8), 0)
    collect_sums([(sums, 16), (near_sums, 8)], number_of, low, high, large)
    shrink = jnp.exp2(-scale_rows * (x * x + y * y))
    den, num = rows_of(low[...], high[...], tiles)
    inv = 1.0 / (1.0 + shrink * den)
    beta = jnp.where(present, shrink * num * inv, 0.0)
    one, two = of_targets(ONE), of_targets(TWO)
    out[:, 0:24, :] = two * (of_targets(PRICE) - one * beta)
    out[:, 24:40, :] = beta[:, 8:24]
    out[:, 40:56, :] = jnp.where(present, one * one * inv, 0.0)[:, 8:24]
    out[:, 56:64, :] = two[:, 0:8]
    out[:, 64:72, :] = x[:, 0:8]
    out[:, 72:80, :] = y[:, 0:8]
    out[:, 80:88, :] = jnp.broadcast_to(counts[0:8][None], (2, 8, LANES))


def second_lists(mine, same, other, same_b, other_b):
    half = same.shape[0]
    cells = 2 * half * SLOTS
    rows = cells // TX
    edge = 2 * half * 8
    padded = -(-edge // LANES) * LANES
    me = lax.axis_index("tile")
    info = jnp.concatenate([x[:, INFO, 0].reshape(half * SLOTS, LANES) for x in (same, other)], axis=0)
    keys = [info[k : k + LANES].T[LABEL : LABEL + 1] + rows for k in range(0, cells, LANES)]
    at = lax.broadcasted_iota(I32, (1, padded), 1)
    n = at >> 3
    device = (((n & (half - 1)) << 1) | (n >= half).astype(I32)) ^ me
    row = (device >> 1) * 8 + (at & 7)
    key = jnp.where((device & 1) == 1, (TX + 1) * rows + row, row)
    keys.append(jnp.where(at < edge, key, -1).astype(F32))
    keys = jnp.concatenate(keys, axis=1)
    total = cells + padded
    edge_live = [x[k, 0, 80:88, :] for x in (same_b, other_b) for k in range(half)]
    if padded > edge:
        edge_live.append(jnp.zeros((padded - edge, LANES), F32))
    live = jnp.concatenate([column_of(info, COUNT), *edge_live], axis=0)
    index = lax.broadcasted_iota(I32, (total, LANES), 0)
    cell = column_of(mine, LABEL).astype(I32)
    column, across = split(cell, rows)
    hot = []
    for a, b in NEAR:
        row = across + b
        wanted = jnp.where((row >= 0) & (row < rows), (column + a + 1) * rows + row, -2).astype(F32)
        parts = [keys[:, k : k + LANES] == wanted for k in range(0, total, LANES)]
        hot.append(jnp.concatenate([p.astype(F32) for p in parts], axis=1))
    hot = jnp.concatenate(hot, axis=0).astype(jnp.bfloat16)

    def look_up(values):
        return jnp.dot(hot, values.astype(F32).astype(jnp.bfloat16), preferred_element_type=F32)

    blocks, slots = look_up(index >> 4), look_up(index & 15)
    lives = look_up(live)
    tiles = mine.shape[0]
    entries = []
    for e, (a, b) in enumerate(NEAR):
        at = slice(e * tiles, (e + 1) * tiles)
        chunks = halves_in(lives[at])
        if e != 4:
            chunks = jnp.where(column_of(mine, REACH + e) > 0.5, chunks, 0)
        row = blocks[at].astype(I32) * (12 * SLOTS) + slots[at].astype(I32)
        n, spot = place_of(column + a, across + b, me, half)
        entries.append((row, n * 64 + spot, jnp.float32(a), jnp.float32(b), chunks))
    count = 2 * half
    spare = (cells + edge) // SLOTS * (12 * SLOTS)
    rows, givens, east, north = list_halves(
        entries, column_of(mine, COUNT), spare, 6 * SLOTS, SLOTS, 24, (count * 64, 32)
    )
    lane = lax.broadcasted_iota(I32, rows.shape, 1)
    n, spot = place_of(column, across, me, half)
    givens = jnp.where(lane == HOLDER, n, givens)
    return rows, jnp.where(lane == HELD_AT, spot, givens), east, north


def second_kernel(
    own_block, mine, columns, same, other, same_b, other_b,
    betas, hats, residual,
    table, given, own, scales, low, high, sums, listed, stepped,
    words, steps, large, sem, word_sem,
):
    copies = fetch(same, other, table, 3, sem)
    half, _, _, tiles, _ = same.shape
    blocks = 2 * half
    for side, held in enumerate((same_b, other_b)):
        at = pl.ds(side * half, half)
        to = given.at[0, at, :, pl.ds(0, 24)]
        copies.append(pltpu.make_async_copy(held.at[:, :, pl.ds(0, 24)], to, sem))
    for copy in copies:
        copy.start()
    listed[0], listed[1], stepped[0], stepped[1] = second_lists(mine, same, other, same_b, other_b)
    word_copies = [
        pltpu.make_async_copy(listed, words, word_sem),
        pltpu.make_async_copy(stepped, steps, word_sem),
    ]
    for copy in word_copies:
        copy.start()
    scales[...] = scale_of(mine[:, WIDTH : WIDTH + 1])
    present = records(tiles) < column_of(mine, COUNT)[None]
    scale_rows = scales[...][None]
    x, y = own_block[EAST], own_block[NORTH]

    def number_of(t):
        return words[0, t, LIVE]

    for n in range(2 * half):
        held = (same_b if n < half else other_b).at[n % half]
        for field in range(3):
            table[blocks + n // 2, field, :, n % 2 * 8 : n % 2 * 8 + 8, :] = held[
                :, 56 + 8 * field : 64 + 8 * field, :
            ]
    for field in range(3):
        table[blocks + half, field, :, 0:8, :] = jnp.zeros((2, 8, LANES), F32)
    given[0, :, :, 24:32, :] = jnp.zeros((2 * half, 2, 8, LANES), F32)
    for copy in copies:
        copy.wait()

    def turn(n, carry):
        table[n, 3:6] = turned(table[n, 0:3])
        return carry

    def turn_given(n, carry):
        given[1, n] = turned(given[0, n])
        return carry

    lax.fori_loop(0, table.shape[0], turn, 0, unroll=True)
    lax.fori_loop(0, 2 * half, turn_given, 0, unroll=True)
    for copy in word_copies:
        copy.wait()

    flat = table.reshape(table.shape[0] * 12 * SLOTS, LANES)
    flat_given = given.reshape(2 * 2 * half * 64, LANES)

    def rows_for(t, i):
        row = words[0, t, i]
        held = [flat[pl.ds(row + field * 2 * SLOTS, 1), :] for field in (EAST, NORTH, TWO)]
        return [*held, flat_given[pl.ds(words[1, t, i], 1), :]]

    def each(t, carry):
        n, at = words[1, t, HOLDER], words[1, t, HELD_AT]
        for k in range(2):
            here = (n & (half - 1), slice(None), pl.ds(16 * (k + 1) + at, 1), slice(None))
            own[k, :, pl.ds(t, 1), :] = jnp.where(n >= half, other_b[here], same_b[here])
        sweep_tile(t, t, scales[pl.ds(t, 1), :], columns, sums, words, steps, rows_for)
        return carry

    lax.fori_loop(0, tiles, each, 0)
    collect_sums([(sums, tiles)], number_of, low, high, large)
    shrink = jnp.exp2(-scale_rows * (x * x + y * y))
    den, num = rows_of(low[...], high[...], tiles)
    inv = 1.0 / (1.0 + shrink * den)
    beta_two = jnp.where(present, shrink * num * inv, 0.0)
    beta_one = own[0]
    one, two = own_block[ONE], own_block[TWO]
    left = jnp.where(present, own_block[PRICE] - one * beta_one - two * beta_two, 0.0)
    hat_two = jnp.where(present, two * two * inv, 0.0)
    for t in range(tiles):
        for h in range(2):
            at = slice(t * TILE + h * LANES, t * TILE + (h + 1) * LANES)
            betas[0:1, at] = beta_one[h, t : t + 1]
            betas[1:2, at] = beta_two[h, t : t + 1]
            hats[0:1, at] = own[1, h, t : t + 1, :]
            hats[1:2, at] = hat_two[h, t : t + 1]
            residual[0:1, at] = left[h, t : t + 1]


def swap(x, k):
    count = lax.axis_size("tile")
    return lax.ppermute(x, "tile", [(i, i ^ k) for i in range(count)])


def spread(block, beside=None):
    count = lax.axis_size("tile")
    same = jnp.stack([block] + [swap(block, k) for k in range(2, count, 2)])
    if beside is None:
        return same, swap(same, 1)
    same, beside = lax.optimization_barrier((same, beside))
    return same, swap(same, 1), beside


def body(offsets, design, target, beta_second, counts, kernel_width, reach, assignment):
    tiles = counts.shape[0]
    count = lax.axis_size("tile")
    regions = lax.axis_size("region")
    cells = tiles * count
    limit = pltpu.CompilerParams(vmem_limit_bytes=24 * 1024 * 1024)
    price = target.reshape(1, -1)
    wide = tiles * TILE
    given = (
        offsets, design, price, beta_second.reshape(1, -1),
        counts, kernel_width, reach.transpose(2, 0, 1), assignment,
    )
    block, mine = pl.pallas_call(
        prepare_kernel,
        out_shape=(
            pltpu.VMEM((7, 2, tiles, LANES), F32),
            pltpu.VMEM((tiles, LANES), F32),
        ),
        in_specs=[pl.BlockSpec(memory_space=pltpu.HBM)] * 8,
        out_specs=(VMEM, VMEM),
        scratch_shapes=[pltpu.VMEM((2, wide), F32)] * 2
        + [pltpu.VMEM((1, wide), F32)] * 2
        + [
            pltpu.SMEM((tiles,), I32),
            pltpu.SMEM((2, tiles), I32),
            pltpu.SMEM((9, 2, tiles), I32),
            pltpu.SMEM((1, tiles), I32),
            pltpu.SemaphoreType.DMA,
        ],
        compiler_params=limit,
    )(*[pltpu.with_memory_space_constraint(x, pltpu.HBM) for x in given])
    square = pltpu.VMEM((LANES, LANES), F32)
    dma = pltpu.SemaphoreType.DMA
    own_columns = pl.pallas_call(
        own_columns_kernel,
        out_shape=pltpu.VMEM((tiles, 2, TILE, LANES), F32),
        in_specs=[VMEM, VMEM],
        out_specs=VMEM,
        scratch_shapes=[square, square, pltpu.SMEM((tiles, LANES), F32), dma],
        compiler_params=limit,
        cost_estimate=pl.CostEstimate(flops=4000000, bytes_accessed=4000000, transcendentals=0),
    )(block, mine)
    same, other, own_columns = spread(block, own_columns)
    edge, near = pl.pallas_call(
        border_kernel,
        out_shape=(
            jax.ShapeDtypeStruct((2, 136, LANES), F32),
            pltpu.VMEM((7, 2, NEAR_ROWS, LANES), F32),
        ),
        in_specs=[VMEM, VMEM],
        out_specs=(VMEM, VMEM),
        compiler_params=limit,
    )(same, other)
    near_columns, near_sums = pl.pallas_call(
        near_kernel,
        out_shape=(
            pltpu.VMEM((16, 2, TILE, LANES), F32),
            pltpu.VMEM((8, TILE, 2 * LANES), F32),
        ),
        in_specs=[VMEM],
        out_specs=(VMEM, VMEM),
        scratch_shapes=[
            pltpu.VMEM((8, 2, NEAR_ROWS, LANES), F32),
            pltpu.VMEM((16, LANES), F32),
            square,
            square,
            pltpu.VMEM((1, 8, LANES), I32),
            pltpu.VMEM((2, 8, LANES), F32),
            pltpu.SMEM((NEAR_ROWS, LANES), F32),
            pltpu.SMEM((1, 8, LANES), I32),
            pltpu.SMEM((2, 8, LANES), F32),
            dma,
            dma,
        ],
        compiler_params=limit,
        cost_estimate=pl.CostEstimate(flops=4000000, bytes_accessed=4000000, transcendentals=0),
    )(near)
    moves = []
    for r in range(regions):
        for t in range(count):
            to = r + 1 - 2 * (t % 2)
            if 0 <= to < regions:
                moves.append((r * count + t, to * count + t))
    border = lax.ppermute(edge, ("region", "tile"), moves)
    first = pl.pallas_call(
        first_kernel,
        out_shape=jax.ShapeDtypeStruct((2, 88, LANES), F32),
        in_specs=[VMEM] * 4,
        out_specs=VMEM,
        scratch_shapes=[
            pltpu.VMEM((10, 2, NEAR_ROWS + EDGE_ROWS, LANES), F32),
            pltpu.VMEM((24, LANES), F32),
            square,
            square,
            square,
            square,
            pltpu.VMEM((8, 2, TILE, LANES), F32),
            pltpu.VMEM((16, TILE, 2 * LANES), F32),
            pltpu.VMEM((1, 24, LANES), I32),
            pltpu.VMEM((2, 24, LANES), F32),
            pltpu.SMEM((1, 24, LANES), I32),
            pltpu.SMEM((2, 24, LANES), F32),
            pltpu.SMEM((24,), I32),
            dma,
            dma,
        ],
        compiler_params=limit,
    )(near, near_columns, near_sums, border)
    same_b, other_b = spread(first)
    betas, hats, residual = pl.pallas_call(
        second_kernel,
        out_shape=(
            jax.ShapeDtypeStruct((2, wide), F32),
            jax.ShapeDtypeStruct((2, wide), F32),
            jax.ShapeDtypeStruct((1, wide), F32),
        ),
        in_specs=[VMEM] * 7,
        out_specs=(VMEM, VMEM, VMEM),
        scratch_shapes=[
            pltpu.VMEM((count + count // 2 + 1, 6, 2, tiles, LANES), F32),
            pltpu.VMEM((2, count, 2, 32, LANES), F32),
            pltpu.VMEM((2, 2, tiles, LANES), F32),
            pltpu.VMEM((tiles, LANES), F32),
            square,
            square,
            pltpu.VMEM((tiles, TILE, 2 * LANES), F32),
            pltpu.VMEM((2, tiles, LANES), I32),
            pltpu.VMEM((2, tiles, LANES), F32),
            pltpu.SMEM((2, tiles, LANES), I32),
            pltpu.SMEM((2, tiles, LANES), F32),
            pltpu.SMEM((24,), I32),
            dma,
            dma,
        ],
        compiler_params=limit,
    )(block, mine, own_columns, same, other, same_b, other_b)
    return (betas, hats, residual.reshape(-1))


def solution(mesh):
    in_specs = (
        P(None, ("region", "tile")),
        P(None, ("region", "tile")),
        P(("region", "tile")),
        P(("region", "tile")),
        P(("region", "tile")),
        P(None, ("region", "tile")),
        P(None, ("region", "tile"), None),
        P("region", "tile"),
    )
    out_specs = (P(None, ("region", "tile")), P(None, ("region", "tile")), P(("region", "tile")))
    return jax.shard_map(body, mesh=mesh, in_specs=in_specs, out_specs=out_specs, check_vma=False)
```

```python
import functools

import jax
import jax.numpy as jnp
from jax import lax
from jax.experimental import pallas as pl
from jax.experimental.pallas import tpu as pltpu
from jax.sharding import PartitionSpec as P

TILE = 256
TX = 4
LANES = 128
TWO, EAST, NORTH, ONE, PART, PRICE, INFO = range(7)
SLOTS = 16
BASE = 32.0 * 1.4426950408889634
LABEL, COUNT, WIDTH, REACH = 0, 1, 2, 3
NEAR = [(a, b) for a in (-1, 0, 1) for b in (-1, 0, 1)]
F32, I32 = jnp.float32, jnp.int32
ANY = pl.BlockSpec(memory_space=pl.ANY)
SMEM = pl.BlockSpec(memory_space=pltpu.SMEM)
VMEM = pl.BlockSpec(memory_space=pltpu.VMEM)


def prepare_kernel(*refs):
    given, (out, mine), held, sem = refs[:8], refs[8:10], refs[10:18], refs[18]
    copies = [pltpu.make_async_copy(a, b, sem) for a, b in zip(given, held)]
    for copy in copies:
        copy.start()
    for copy in copies:
        copy.wait()
    off, des, tgt, sec, counts, widths, reach, cells = held
    lane = lax.broadcasted_iota(I32, (1, LANES), 1)
    for t in range(counts.shape[0]):
        row = jnp.zeros((1, LANES), F32)
        facts = [cells[0, t], counts[t], widths[0, t]] + [reach[e, 0, t] for e in range(9)]
        for k, fact in enumerate(facts):
            row = jnp.where(lane == k, fact.astype(F32), row)
        out[INFO, 0, t : t + 1, :] = row
        for k, value in enumerate([widths[1, t]] + [reach[e, 1, t] for e in range(9)]):
            row = jnp.where(lane == WIDTH + k, value.astype(F32), row)
        mine[t : t + 1, :] = row
        for h in range(2):
            at = slice(t * TILE + h * LANES, t * TILE + (h + 1) * LANES)
            live = lane + h * LANES < counts[t]
            one = jnp.where(live, des[0:1, at], 0.0)
            two = jnp.where(live, des[1:2, at], 0.0)
            price = tgt[0:1, at]
            out[EAST, h, t : t + 1, :] = off[0:1, at] - 0.5
            out[NORTH, h, t : t + 1, :] = off[1:2, at] - 0.5
            out[ONE, h, t : t + 1, :] = one
            out[PART, h, t : t + 1, :] = one * (price - two * sec[0:1, at])
            out[TWO, h, t : t + 1, :] = two
            out[PRICE, h, t : t + 1, :] = price
    out[INFO, 1] = jnp.zeros_like(out[INFO, 1])


def split(number, size):
    return number >> (size.bit_length() - 1), number & (size - 1)


def fetch(same, other, table, fields, sem):
    half = same.shape[0]
    return [
        pltpu.make_async_copy(
            held.at[:, pl.ds(0, fields)], table.at[pl.ds(side * half, half), pl.ds(0, fields)], sem
        )
        for side, held in enumerate((same, other))
    ]


ORDER = [(0, r) for r in range(1, 9)] + [(1, r) for r in range(1, 9)]
ORDER += [(0, 0), (0, 9), (1, 0), (1, 9)]
NEAR_ROWS, EDGE_ROWS, SPARE = 32, 24, 30


def wanted_cells(rows):
    me = lax.axis_index("tile")
    odd = me & 1
    first = (me >> 1) * 8
    i = lax.broadcasted_iota(I32, (64, LANES), 0)
    u = (i >= 10).astype(I32) + (i >= 20).astype(I32)
    j = i - NEAR_ROWS
    away = jnp.where(j < 16, j >> 3, (j >> 1) & 1)
    own = i < NEAR_ROWS
    r = jnp.where(own, i - 10 * u, jnp.where(j < 16, (j & 7) + 1, (j & 1) * 9))
    low = jnp.where(own, u, TX - 1 - away)
    column = jnp.where(odd == 1, TX - 1 - low, low)
    cell = column * rows + jnp.clip(first + r - 1, 0, rows - 1)
    none = (i == SPARE) | (i == SPARE + 1) | (j >= len(ORDER))
    return jnp.where(none, -1, cell).astype(F32)


def border_kernel(same, other, out, near):
    half = same.shape[0]
    cells = 2 * half * SLOTS

    def plane(field, h):
        parts = [x[:, field, h].reshape(half * SLOTS, LANES) for x in (same, other)]
        return jnp.concatenate(parts, axis=0)

    info = plane(INFO, 0)
    wanted = wanted_cells(cells // TX)
    hot = []
    for k in range(0, cells, LANES):
        labels = info[k : k + LANES].T[LABEL : LABEL + 1]
        hot.append((jnp.broadcast_to(labels, wanted.shape) == wanted).astype(F32))
    hot = jnp.concatenate(hot, axis=1).astype(jnp.bfloat16)

    def pick(values, pieces):
        total = jnp.zeros((64, LANES), F32)
        for _ in range(pieces):
            piece = values.astype(jnp.bfloat16)
            values = values - piece.astype(F32)
            total = total + jnp.dot(hot, piece, preferred_element_type=F32)
        return total

    for field in (EAST, NORTH, ONE, PART, INFO, TWO, PRICE):
        for h in range(2):
            if field != INFO:
                got = pick(plane(field, h), 3)
            elif h == 0:
                got = pick(info, 1)
            near[field, h] = got[0:NEAR_ROWS]
            edge = got[NEAR_ROWS : NEAR_ROWS + EDGE_ROWS]
            if field in (TWO, PRICE):
                f = (TWO, PRICE).index(field)
                out[h, 120 + 8 * f : 128 + 8 * f, :] = edge[0:8]
            else:
                f = (EAST, NORTH, ONE, PART, INFO).index(field)
                out[h, f * 24 : f * 24 + 24, :] = edge


def targets_of(near, field):
    return jnp.concatenate([near[field, :, 1:9, :], near[field, :, 11:19, :]], axis=1)


def near_kernel(
    near, columns, sums,
    table, own, east, north, listed, stepped, facts, words, steps, sem, word_sem,
):
    copy = pltpu.make_async_copy(near.at[INFO, 0], facts, sem)
    copy.start()
    rows = lax.axis_size("tile") * SLOTS // TX
    near_info = near[INFO, 0]
    listed[0], _, stepped[0], stepped[1] = first_lists(near_info, None, rows, (2,), 4, NEAR_ROWS)
    word_copies = [
        pltpu.make_async_copy(listed, words, word_sem),
        pltpu.make_async_copy(stepped, steps, word_sem),
    ]
    for word_copy in word_copies:
        word_copy.start()
    info = targets_of(near, INFO)[0]
    own[...] = scale_of(info[:, WIDTH : WIDTH + 1])
    scale = own[...][None]
    east[...] = columns_of(2.0 * scale * targets_of(near, EAST))
    north[...] = columns_of(2.0 * scale * targets_of(near, NORTH))
    table[0:4] = near[EAST : PART + 1]
    table[4:8] = turned(near[EAST : PART + 1])

    def number_of(t):
        return facts[(t >> 3) * 10 + (t & 7) + 1, COUNT].astype(I32)

    spread_columns(16, number_of, east, north, columns, copy.wait)
    for word_copy in word_copies:
        word_copy.wait()
    flat = table.reshape(16 * NEAR_ROWS, LANES)

    def rows_for(t, i):
        row = words[0, t, i]
        return [flat[pl.ds(row + k * 2 * NEAR_ROWS, 1), :] for k in range(4)]

    def each(t, carry):
        sweep_tile(t, t + 8, own[pl.ds(t + 8, 1), :], columns, sums, words, steps, rows_for)
        return carry

    lax.fori_loop(0, 8, each, 0)


USED, LIVE, HOLDER, HELD_AT = 100, 101, 102, 103


def column_of(info, k):
    return jnp.broadcast_to(info[:, k : k + 1], (info.shape[0], LANES))


def halves_in(number):
    return sum((number > 64.0 * q).astype(I32) for q in range(4))


def list_halves(entries, number, spare, other, half_at, spare_given=0, given_at=(0, 0)):
    lane = lax.broadcasted_iota(I32, number.shape, 1)
    rows = jnp.full(number.shape, spare, I32)
    givens = jnp.full(number.shape, spare_given, I32)
    east, north = jnp.zeros(number.shape, F32), jnp.zeros(number.shape, F32)
    used = jnp.zeros(number.shape, I32)
    for row, given, a, b, halves in entries:
        moved = used & 1
        row = row + moved * other
        given = given + moved * given_at[0]
        for q in range(4):
            here = (lane == used + q) & (halves > q)
            rows = jnp.where(here, row + (q >> 1) * half_at, rows)
            givens = jnp.where(here, given + (q >> 1) * given_at[1], givens)
        here = (lane >= used) & (lane < used + halves)
        east = jnp.where(here, a, east)
        north = jnp.where(here, b, north)
        used = used + halves
    rows = jnp.where(lane == USED, used, rows)
    rows = jnp.where(lane == LIVE, number.astype(I32), rows)
    return rows, givens, east, north


def turned(values):
    flat = pltpu.roll(values.reshape(-1, LANES), LANES // 2, 1)
    return flat.reshape(values.shape)


def place_of(column, row, me, half):
    low = (column < TX // 2).astype(I32)
    depth = jnp.where(low == 1, column + 1, TX - column)
    k = ((row >> 3) * 2 + 1 - low) ^ me
    return (k & 1) * half + (k >> 1), depth * 8 + (row & 7)


def scale_of(width):
    return jnp.broadcast_to(BASE / (width * width), (width.shape[0], LANES))


def own_columns_kernel(block, mine, columns, east, north, facts, sem):
    copy = pltpu.make_async_copy(mine, facts, sem)
    copy.start()
    scale = scale_of(mine[:, WIDTH : WIDTH + 1])[None]
    east[...] = columns_of(2.0 * scale * block[EAST])
    north[...] = columns_of(2.0 * scale * block[NORTH])

    def number_of(t):
        return facts[t, COUNT].astype(I32)

    spread_columns(block.shape[2], number_of, east, north, columns, copy.wait)


def records(tiles):
    shape = (2, tiles, LANES)
    number = lax.broadcasted_iota(I32, shape, 2) + LANES * lax.broadcasted_iota(I32, shape, 0)
    return number.astype(F32)


def columns_of(rows):
    pad = jnp.zeros((64 - rows.shape[1], LANES), F32)
    return jnp.concatenate([rows[0], pad, rows[1], pad], axis=0).T


def rows_of(low, high, tiles):
    low, high = low.T, high.T
    return [jnp.stack([low[k : k + tiles], high[k : k + tiles]]) for k in (0, 64)]


def spread_columns(tiles, number_of, east, north, columns, ready=None):
    def lay(t, nb, values):
        i = (nb >> 1) * 64 + t
        for k, value in enumerate(values):
            wide = jnp.broadcast_to(value[:, i : i + 1], (64, LANES))
            columns[t, k, nb * 64 : nb * 64 + 64, :] = wide

    low = (east[0:64, :], north[0:64, :])
    for t in range(tiles):
        lay(t, 0, low)
    if ready is not None:
        ready()
    for t in range(tiles):
        number = number_of(t)

        @pl.when(number > 64)
        def _():
            lay(t, 1, (east[64:128, :], north[64:128, :]))

        @pl.when(number > 128)
        def _():
            lay(t, 2, (east[0:64, :], north[0:64, :]))
            lay(t, 3, (east[64:128, :], north[64:128, :]))


SHARE = 3
GROUP = 4


def collect_sums(parts, number_of, low_ref, high_ref, large):
    split_at = (lax.broadcasted_iota(I32, (4 * LANES, LANES), 0) // LANES) & 1
    sides = lax.broadcasted_iota(I32, (4 * LANES, LANES), 1) // 64
    ones = (split_at == sides).astype(F32).astype(jnp.bfloat16)
    place = lax.broadcasted_iota(I32, (64, LANES), 1)
    lane = place & 63

    def total(values):
        high = values.astype(jnp.bfloat16)
        low = (values - high.astype(F32)).astype(jnp.bfloat16)
        return jnp.dot(jnp.concatenate([high, low], axis=1), ones, preferred_element_type=F32)

    for nb in range(2):
        result = jnp.zeros((64, LANES), F32)
        held = [(sums, t) for sums, tiles in parts for t in range(tiles)]
        for i, (sums, t) in enumerate(held):
            values = sums[t, nb * 64 : nb * 64 + 64, :]
            if i % SHARE == SHARE - 1:
                for k in range(2):
                    x = jnp.sum(values[:, k * LANES : (k + 1) * LANES], axis=1, keepdims=True)
                    result = jnp.where(place == k * 64 + i, x, result)
            else:
                result = jnp.where(lane == i, total(values), result)
        low_ref[nb * 64 : nb * 64 + 64, :] = result
    high_ref[...] = jnp.zeros_like(high_ref)

    start = 0
    for sums, tiles in parts:
        many = jnp.int32(0)
        for t in range(tiles):
            large[many] = jnp.int32(t)
            many = many + (number_of(start + t) > 128).astype(I32)
        last = large[jnp.maximum(many - 1, 0)]
        for k in range(GROUP - 1):
            large[many + k] = last

        def some(g, carry, sums=sums, start=start):
            result = high_ref[...]
            for i in range(GROUP):
                t = large[g * GROUP + i]
                mine = (lax.broadcasted_iota(I32, (LANES, LANES), 1) & 63) == start + t
                result = jnp.where(mine, total(sums[t, 128:256, :]), result)
            high_ref[...] = result
            return carry

        lax.fori_loop(0, (many + GROUP - 1) // GROUP, some, 0)
        start += tiles


def sweep_tile(t, at_column, scale, columns, sums, words, steps, rows_for):
    scale = jnp.broadcast_to(scale, (8, LANES))
    left = lax.broadcasted_iota(I32, (8, LANES), 1) < LANES // 2

    def chunk(i):
        sides = []
        for k in range(2):
            u, v, c, d = [jnp.broadcast_to(row, (8, LANES)) for row in rows_for(t, i + k)]
            sides.append((u + steps[0, t, i + k], v + steps[1, t, i + k], c, d))
        u, v, c, d = [jnp.where(left, *pair) for pair in zip(*sides)]
        fade = jnp.exp2(-scale * (u * u + v * v))
        return u, v, c * c * fade, d * fade

    def block(nb, size, step):
        at = pl.ds(pl.multiple_of(nb * 64, 64), size)
        x = columns[at_column, 0, at, :].reshape(size // 8, 8, LANES)
        y = columns[at_column, 1, at, :].reshape(size // 8, 8, LANES)

        def some(p, sums_now):
            den, num = sums_now
            for k in range(step):
                u, v, c, d = chunk(2 * (step * p + k))
                w = jnp.exp2(x * u + y * v)
                den = den + w * c
                num = num + w * d
            return den, num

        zero = jnp.zeros((size // 8, 8, LANES), F32)
        trips = (words[0, t, USED] + 2 * step - 1) // (2 * step)
        den, num = lax.fori_loop(0, trips, some, (zero, zero))
        sums[t, at, 0:LANES] = den.reshape(size, LANES)
        sums[t, at, LANES : 2 * LANES] = num.reshape(size, LANES)

    number = words[0, t, LIVE]
    whole = (number + 31) >> 6

    def full(nb, carry):
        block(nb, 64, 2)
        return carry

    lax.fori_loop(0, whole, full, 0)

    @pl.when(number > whole * 64)
    def _():
        block(whole, 32, 4)


def first_lists(near_info, edge_info, rows, groups, fields, plane):
    me = lax.axis_index("tile")
    odd = me & 1
    first = (me >> 1) * 8
    near_live = column_of(near_info, COUNT)
    if edge_info is not None:
        edge_live = column_of(edge_info, COUNT)
    step = lax.broadcasted_iota(I32, (8, LANES), 0)
    on_map = [(first > 0).astype(F32), (first + 8 < rows).astype(F32)]
    lines = []
    for u in range(5):
        if u < 2 and edge_info is None:
            lines.append(None)
            continue
        if u < 2:
            away = 1 - u
            parts = [edge_live[i : i + n] for i, n in ((16 + 2 * away, 1), (8 * away, 8), (17 + 2 * away, 1))]
        else:
            parts = [near_live[10 * (u - 2) + i : 10 * (u - 2) + i + n] for i, n in ((0, 1), (1, 8), (9, 1))]
        lines.append(jnp.concatenate([parts[0] * on_map[0], parts[1], parts[2] * on_map[1]], axis=0))

    def source(u, b):
        if u >= 2:
            return (u - 2) * 10 + 1 + b + step
        start = NEAR_ROWS + 8 * (1 - u)
        at = start + b + step
        if b == 0:
            return at
        corner = NEAR_ROWS + 16 + 2 * (1 - u) + (b + 1) // 2
        return jnp.where(step == (0 if b < 0 else 7), corner, at)

    result = []
    infos = (None if edge_info is None else edge_info[0:8], near_info[1:9], near_info[11:19])
    for j, info in enumerate(infos):
        if info is None or (edge_info is None and j not in groups):
            continue
        entries = []
        for du in (-1, 0, 1) if j in groups else ():
            for b in (-1, 0, 1):
                here, there = 3 * (du + 1) + b + 1, 3 * (1 - du) + b + 1
                a = jnp.where(odd == 1, -du, du).astype(F32)
                chunks = halves_in(lines[j + 1 + du][1 + b : 9 + b])
                if here != 4:
                    taken = jnp.where(odd == 1, column_of(info, REACH + there), column_of(info, REACH + here))
                    chunks = jnp.where(taken > 0.5, chunks, 0)
                entries.append((source(j + 1 + du, b), 0, a, jnp.float32(b), chunks))
        moved = 2 * fields * plane
        result.append(list_halves(entries, column_of(info, COUNT), SPARE, moved, plane))
    return [jnp.concatenate(parts, axis=0) for parts in zip(*result)]


def first_kernel(
    near, near_columns, near_sums, border, out,
    table, own, east, north, low, high, columns, sums, listed, stepped,
    words, steps, large, sem, word_sem,
):
    rows = lax.axis_size("tile") * SLOTS // TX
    near_at, edge_at = pl.ds(0, NEAR_ROWS), pl.ds(NEAR_ROWS, EDGE_ROWS)
    copies = [
        pltpu.make_async_copy(near.at[pl.ds(0, 6)], table.at[pl.ds(0, 6), :, near_at], sem)
    ]
    for f, field in enumerate((EAST, NORTH, ONE, PART)):
        held = border.at[:, pl.ds(f * 24, 24)]
        copies.append(pltpu.make_async_copy(held, table.at[field, :, edge_at], sem))
    for f, field in enumerate((TWO, PRICE)):
        held = border.at[:, pl.ds(120 + 8 * f, 8)]
        copies.append(pltpu.make_async_copy(held, table.at[field, :, pl.ds(NEAR_ROWS, 8)], sem))
    for copy in copies:
        copy.start()
    near_info, edge_info = near[INFO, 0], border[0, 4 * 24 : 5 * 24, :]
    listed[0], _, stepped[0], stepped[1] = first_lists(
        near_info, edge_info, rows, (0, 1), 5, NEAR_ROWS + EDGE_ROWS
    )
    word_copies = [
        pltpu.make_async_copy(listed, words, word_sem),
        pltpu.make_async_copy(stepped, steps, word_sem),
    ]
    for copy in word_copies:
        copy.start()
    tiles = 24
    info = jnp.concatenate([edge_info[0:8], near_info[1:9], near_info[11:19]], axis=0)
    scales = scale_of(info[:, WIDTH : WIDTH + 1])
    counts = column_of(info, COUNT)
    for copy in copies:
        copy.wait()

    def of_targets(field):
        parts = [table[field, :, 32:40, :], table[field, :, 1:9, :], table[field, :, 11:19, :]]
        return jnp.concatenate(parts, axis=1)

    present = records(tiles) < counts[None]
    scale_rows = scales[None]
    own[...] = scales
    x, y = of_targets(EAST), of_targets(NORTH)
    east[...] = columns_of(2.0 * scale_rows[:, 0:8] * x[:, 0:8])
    north[...] = columns_of(2.0 * scale_rows[:, 0:8] * y[:, 0:8])

    def number_of(t):
        return words[0, t, LIVE]

    def ready():
        for copy in word_copies:
            copy.wait()

    spread_columns(8, number_of, east, north, columns, ready)

    table[6:10] = turned(table[EAST : PART + 1])

    plane = 2 * (NEAR_ROWS + EDGE_ROWS)
    flat = table.reshape(10 * plane, LANES)

    def rows_for(t, i):
        row = words[0, t, i]
        return [flat[pl.ds(row + field * plane, 1), :] for field in (EAST, NORTH, ONE, PART)]

    def each(t, carry, held, skip):
        sweep_tile(t, t - skip, own[pl.ds(t, 1), :], held, sums, words, steps, rows_for)
        return carry

    lax.fori_loop(0, 8, lambda t, c: each(t, c, columns, 0), 0)
    lax.fori_loop(8, 16, lambda t, c: each(t, c, near_columns, 8), 0)
    collect_sums([(sums, 16), (near_sums, 8)], number_of, low, high, large)
    shrink = jnp.exp2(-scale_rows * (x * x + y * y))
    den, num = rows_of(low[...], high[...], tiles)
    inv = 1.0 / (1.0 + shrink * den)
    beta = jnp.where(present, shrink * num * inv, 0.0)
    one, two = of_targets(ONE), of_targets(TWO)
    out[:, 0:24, :] = two * (of_targets(PRICE) - one * beta)
    out[:, 24:40, :] = beta[:, 8:24]
    out[:, 40:56, :] = jnp.where(present, one * one * inv, 0.0)[:, 8:24]
    out[:, 56:64, :] = two[:, 0:8]
    out[:, 64:72, :] = x[:, 0:8]
    out[:, 72:80, :] = y[:, 0:8]
    out[:, 80:88, :] = jnp.broadcast_to(counts[0:8][None], (2, 8, LANES))


def second_lists(mine, same, other, same_b, other_b):
    half = same.shape[0]
    cells = 2 * half * SLOTS
    rows = cells // TX
    edge = 2 * half * 8
    padded = -(-edge // LANES) * LANES
    me = lax.axis_index("tile")
    info = jnp.concatenate([x[:, INFO, 0].reshape(half * SLOTS, LANES) for x in (same, other)], axis=0)
    keys = [info[k : k + LANES].T[LABEL : LABEL + 1] + rows for k in range(0, cells, LANES)]
    at = lax.broadcasted_iota(I32, (1, padded), 1)
    n = at >> 3
    device = (((n & (half - 1)) << 1) | (n >= half).astype(I32)) ^ me
    row = (device >> 1) * 8 + (at & 7)
    key = jnp.where((device & 1) == 1, (TX + 1) * rows + row, row)
    keys.append(jnp.where(at < edge, key, -1).astype(F32))
    keys = jnp.concatenate(keys, axis=1)
    total = cells + padded
    edge_live = [x[k, 0, 80:88, :] for x in (same_b, other_b) for k in range(half)]
    if padded > edge:
        edge_live.append(jnp.zeros((padded - edge, LANES), F32))
    live = jnp.concatenate([column_of(info, COUNT), *edge_live], axis=0)
    index = lax.broadcasted_iota(I32, (total, LANES), 0)
    cell = column_of(mine, LABEL).astype(I32)
    column, across = split(cell, rows)
    hot = []
    for a, b in NEAR:
        row = across + b
        wanted = jnp.where((row >= 0) & (row < rows), (column + a + 1) * rows + row, -2).astype(F32)
        parts = [keys[:, k : k + LANES] == wanted for k in range(0, total, LANES)]
        hot.append(jnp.concatenate([p.astype(F32) for p in parts], axis=1))
    hot = jnp.concatenate(hot, axis=0).astype(jnp.bfloat16)

    def look_up(values):
        return jnp.dot(hot, values.astype(F32).astype(jnp.bfloat16), preferred_element_type=F32)

    blocks, slots = look_up(index >> 4), look_up(index & 15)
    lives = look_up(live)
    tiles = mine.shape[0]
    entries = []
    for e, (a, b) in enumerate(NEAR):
        at = slice(e * tiles, (e + 1) * tiles)
        chunks = halves_in(lives[at])
        if e != 4:
            chunks = jnp.where(column_of(mine, REACH + e) > 0.5, chunks, 0)
        row = blocks[at].astype(I32) * (12 * SLOTS) + slots[at].astype(I32)
        n, spot = place_of(column + a, across + b, me, half)
        entries.append((row, n * 64 + spot, jnp.float32(a), jnp.float32(b), chunks))
    count = 2 * half
    spare = (cells + edge) // SLOTS * (12 * SLOTS)
    rows, givens, east, north = list_halves(
        entries, column_of(mine, COUNT), spare, 6 * SLOTS, SLOTS, 24, (count * 64, 32)
    )
    lane = lax.broadcasted_iota(I32, rows.shape, 1)
    n, spot = place_of(column, across, me, half)
    givens = jnp.where(lane == HOLDER, n, givens)
    return rows, jnp.where(lane == HELD_AT, spot, givens), east, north


def second_kernel(
    own_block, mine, columns, same, other, same_b, other_b,
    betas, hats, residual,
    table, given, own, scales, low, high, sums, listed, stepped,
    words, steps, large, sem, word_sem,
):
    copies = fetch(same, other, table, 3, sem)
    half, _, _, tiles, _ = same.shape
    blocks = 2 * half
    for side, held in enumerate((same_b, other_b)):
        at = pl.ds(side * half, half)
        to = given.at[0, at, :, pl.ds(0, 24)]
        copies.append(pltpu.make_async_copy(held.at[:, :, pl.ds(0, 24)], to, sem))
    for copy in copies:
        copy.start()
    listed[0], listed[1], stepped[0], stepped[1] = second_lists(mine, same, other, same_b, other_b)
    word_copies = [
        pltpu.make_async_copy(listed, words, word_sem),
        pltpu.make_async_copy(stepped, steps, word_sem),
    ]
    for copy in word_copies:
        copy.start()
    scales[...] = scale_of(mine[:, WIDTH : WIDTH + 1])
    present = records(tiles) < column_of(mine, COUNT)[None]
    scale_rows = scales[...][None]
    x, y = own_block[EAST], own_block[NORTH]

    def number_of(t):
        return words[0, t, LIVE]

    for n in range(2 * half):
        held = (same_b if n < half else other_b).at[n % half]
        for field in range(3):
            table[blocks + n // 2, field, :, n % 2 * 8 : n % 2 * 8 + 8, :] = held[
                :, 56 + 8 * field : 64 + 8 * field, :
            ]
    for field in range(3):
        table[blocks + half, field, :, 0:8, :] = jnp.zeros((2, 8, LANES), F32)
    given[0, :, :, 24:32, :] = jnp.zeros((2 * half, 2, 8, LANES), F32)
    for copy in copies:
        copy.wait()

    def turn(n, carry):
        table[n, 3:6] = turned(table[n, 0:3])
        return carry

    def turn_given(n, carry):
        given[1, n] = turned(given[0, n])
        return carry

    lax.fori_loop(0, table.shape[0], turn, 0, unroll=True)
    lax.fori_loop(0, 2 * half, turn_given, 0, unroll=True)
    for copy in word_copies:
        copy.wait()

    flat = table.reshape(table.shape[0] * 12 * SLOTS, LANES)
    flat_given = given.reshape(2 * 2 * half * 64, LANES)

    def rows_for(t, i):
        row = words[0, t, i]
        held = [flat[pl.ds(row + field * 2 * SLOTS, 1), :] for field in (EAST, NORTH, TWO)]
        return [*held, flat_given[pl.ds(words[1, t, i], 1), :]]

    def fetch_own(t, carry):
        n, at = words[1, t, HOLDER], words[1, t, HELD_AT]
        for k in range(2):
            here = (n & (half - 1), slice(None), pl.ds(16 * (k + 1) + at, 1), slice(None))
            own[k, :, pl.ds(t, 1), :] = jnp.where(n >= half, other_b[here], same_b[here])
        return carry

    lax.fori_loop(0, tiles, fetch_own, 0, unroll=True)

    def each(t, carry):
        sweep_tile(t, t, scales[pl.ds(t, 1), :], columns, sums, words, steps, rows_for)
        return carry

    lax.fori_loop(0, tiles, each, 0)
    collect_sums([(sums, tiles)], number_of, low, high, large)
    shrink = jnp.exp2(-scale_rows * (x * x + y * y))
    den, num = rows_of(low[...], high[...], tiles)
    inv = 1.0 / (1.0 + shrink * den)
    beta_two = jnp.where(present, shrink * num * inv, 0.0)
    beta_one = own[0]
    one, two = own_block[ONE], own_block[TWO]
    left = jnp.where(present, own_block[PRICE] - one * beta_one - two * beta_two, 0.0)
    hat_two = jnp.where(present, two * two * inv, 0.0)
    for t in range(tiles):
        for h in range(2):
            at = slice(t * TILE + h * LANES, t * TILE + (h + 1) * LANES)
            betas[0:1, at] = beta_one[h, t : t + 1]
            betas[1:2, at] = beta_two[h, t : t + 1]
            hats[0:1, at] = own[1, h, t : t + 1, :]
            hats[1:2, at] = hat_two[h, t : t + 1]
            residual[0:1, at] = left[h, t : t + 1]


def swap(x, k):
    count = lax.axis_size("tile")
    return lax.ppermute(x, "tile", [(i, i ^ k) for i in range(count)])


def spread(block, beside=None):
    count = lax.axis_size("tile")
    same = jnp.stack([block] + [swap(block, k) for k in range(2, count, 2)])
    if beside is None:
        return same, swap(same, 1)
    same, beside = lax.optimization_barrier((same, beside))
    return same, swap(same, 1), beside


def body(offsets, design, target, beta_second, counts, kernel_width, reach, assignment):
    tiles = counts.shape[0]
    count = lax.axis_size("tile")
    regions = lax.axis_size("region")
    cells = tiles * count
    limit = pltpu.CompilerParams(vmem_limit_bytes=24 * 1024 * 1024)
    price = target.reshape(1, -1)
    wide = tiles * TILE
    given = (
        offsets, design, price, beta_second.reshape(1, -1),
        counts, kernel_width, reach.transpose(2, 0, 1), assignment,
    )
    block, mine = pl.pallas_call(
        prepare_kernel,
        out_shape=(
            pltpu.VMEM((7, 2, tiles, LANES), F32),
            pltpu.VMEM((tiles, LANES), F32),
        ),
        in_specs=[pl.BlockSpec(memory_space=pltpu.HBM)] * 8,
        out_specs=(VMEM, VMEM),
        scratch_shapes=[pltpu.VMEM((2, wide), F32)] * 2
        + [pltpu.VMEM((1, wide), F32)] * 2
        + [
            pltpu.SMEM((tiles,), I32),
            pltpu.SMEM((2, tiles), I32),
            pltpu.SMEM((9, 2, tiles), I32),
            pltpu.SMEM((1, tiles), I32),
            pltpu.SemaphoreType.DMA,
        ],
        compiler_params=limit,
    )(*[pltpu.with_memory_space_constraint(x, pltpu.HBM) for x in given])
    square = pltpu.VMEM((LANES, LANES), F32)
    dma = pltpu.SemaphoreType.DMA
    own_columns = pl.pallas_call(
        own_columns_kernel,
        out_shape=pltpu.VMEM((tiles, 2, TILE, LANES), F32),
        in_specs=[VMEM, VMEM],
        out_specs=VMEM,
        scratch_shapes=[square, square, pltpu.SMEM((tiles, LANES), F32), dma],
        compiler_params=limit,
        cost_estimate=pl.CostEstimate(flops=4000000, bytes_accessed=4000000, transcendentals=0),
    )(block, mine)
    same, other, own_columns = spread(block, own_columns)
    edge, near = pl.pallas_call(
        border_kernel,
        out_shape=(
            jax.ShapeDtypeStruct((2, 136, LANES), F32),
            pltpu.VMEM((7, 2, NEAR_ROWS, LANES), F32),
        ),
        in_specs=[VMEM, VMEM],
        out_specs=(VMEM, VMEM),
        compiler_params=limit,
    )(same, other)
    near_columns, near_sums = pl.pallas_call(
        near_kernel,
        out_shape=(
            pltpu.VMEM((16, 2, TILE, LANES), F32),
            pltpu.VMEM((8, TILE, 2 * LANES), F32),
        ),
        in_specs=[VMEM],
        out_specs=(VMEM, VMEM),
        scratch_shapes=[
            pltpu.VMEM((8, 2, NEAR_ROWS, LANES), F32),
            pltpu.VMEM((16, LANES), F32),
            square,
            square,
            pltpu.VMEM((1, 8, LANES), I32),
            pltpu.VMEM((2, 8, LANES), F32),
            pltpu.SMEM((NEAR_ROWS, LANES), F32),
            pltpu.SMEM((1, 8, LANES), I32),
            pltpu.SMEM((2, 8, LANES), F32),
            dma,
            dma,
        ],
        compiler_params=limit,
        cost_estimate=pl.CostEstimate(flops=4000000, bytes_accessed=4000000, transcendentals=0),
    )(near)
    moves = []
    for r in range(regions):
        for t in range(count):
            to = r + 1 - 2 * (t % 2)
            if 0 <= to < regions:
                moves.append((r * count + t, to * count + t))
    border = lax.ppermute(edge, ("region", "tile"), moves)
    first = pl.pallas_call(
        first_kernel,
        out_shape=jax.ShapeDtypeStruct((2, 88, LANES), F32),
        in_specs=[VMEM] * 4,
        out_specs=VMEM,
        scratch_shapes=[
            pltpu.VMEM((10, 2, NEAR_ROWS + EDGE_ROWS, LANES), F32),
            pltpu.VMEM((24, LANES), F32),
            square,
            square,
            square,
            square,
            pltpu.VMEM((8, 2, TILE, LANES), F32),
            pltpu.VMEM((16, TILE, 2 * LANES), F32),
            pltpu.VMEM((1, 24, LANES), I32),
            pltpu.VMEM((2, 24, LANES), F32),
            pltpu.SMEM((1, 24, LANES), I32),
            pltpu.SMEM((2, 24, LANES), F32),
            pltpu.SMEM((24,), I32),
            dma,
            dma,
        ],
        compiler_params=limit,
    )(near, near_columns, near_sums, border)
    same_b, other_b = spread(first)
    betas, hats, residual = pl.pallas_call(
        second_kernel,
        out_shape=(
            jax.ShapeDtypeStruct((2, wide), F32),
            jax.ShapeDtypeStruct((2, wide), F32),
            jax.ShapeDtypeStruct((1, wide), F32),
        ),
        in_specs=[VMEM] * 7,
        out_specs=(VMEM, VMEM, VMEM),
        scratch_shapes=[
            pltpu.VMEM((count + count // 2 + 1, 6, 2, tiles, LANES), F32),
            pltpu.VMEM((2, count, 2, 32, LANES), F32),
            pltpu.VMEM((2, 2, tiles, LANES), F32),
            pltpu.VMEM((tiles, LANES), F32),
            square,
            square,
            pltpu.VMEM((tiles, TILE, 2 * LANES), F32),
            pltpu.VMEM((2, tiles, LANES), I32),
            pltpu.VMEM((2, tiles, LANES), F32),
            pltpu.SMEM((2, tiles, LANES), I32),
            pltpu.SMEM((2, tiles, LANES), F32),
            pltpu.SMEM((24,), I32),
            dma,
            dma,
        ],
        compiler_params=limit,
    )(block, mine, own_columns, same, other, same_b, other_b)
    return (betas, hats, residual.reshape(-1))


def solution(mesh):
    in_specs = (
        P(None, ("region", "tile")),
        P(None, ("region", "tile")),
        P(("region", "tile")),
        P(("region", "tile")),
        P(("region", "tile")),
        P(None, ("region", "tile")),
        P(None, ("region", "tile"), None),
        P("region", "tile"),
    )
    out_specs = (P(None, ("region", "tile")), P(None, ("region", "tile")), P(("region", "tile")))
    return jax.shard_map(body, mesh=mesh, in_specs=in_specs, out_specs=out_specs, check_vma=False)
```
